128 devices in a mesh: box: 32 (over y, z, core), node: 4 (over x).
Axes of the slice: x: 4, y: 4, z: 4, core: 2. Of those that a mesh axis runs over, the one named last changes fastest.
Arguments:
- fine_rhs: float32 [1024, 32, 1024], P(('box', 'node')), may hold values from -6 to 6
- fine_diag: float32 [1024, 32, 1024], P(('box', 'node')), may hold values from 0.25 to 4
- fine_count: int32 [32, 4], P('box', 'node'), may hold values from 1 to 8, as said below
- fine_nbr: int32 [1024, 6], P(('box', 'node')), may hold values from -1 to 23, as said below
- fine_cover: int32 [32, 32], P('box', 'node'), may hold values from 0 to 31, each once within a row
- coarse_source: float32 [128, 32, 1024], P(('box', 'node')), may hold values from -6 to 6
- coarse_diag: float32 [128, 32, 1024], P(('box', 'node')), may hold values from 0.25 to 4
- coarse_nbr: int32 [128, 6], P(('box', 'node')), may hold values from -1 to 2, as said below
- coarse_place: int32 [128], P(('box', 'node')), may hold values from 0 to 32767, as said below
- bottom_diag: float32 [256, 256, 256], P('box', 'node'), may hold values from 0.1 to 6
Outputs:
- fine_correction: float32 [1024, 32, 1024], P(('box', 'node'))
- coarse_correction: float32 [128, 32, 1024], P(('box', 'node'))
The draws below stay inside these ranges and needn't reach their ends.
Inputs may be any that keep to these rules, and one draw needn't show every extreme that they name: `fine_count`: the first that many slots of a device hold boxes; some device holds 8. `fine_nbr`: entry w indexes the boxes of the device before, this device and the device after, 8 each in that order; -1 where no fine box lies across the face. Empty slots have -1 throughout; no entry names an empty slot or a device beyond the ends. `fine_cover`: within a group of 4 devices along node, v // 8 counts the group's middle boxes in node order; every pair of box and octant is named once. `coarse_nbr`: as for fine_nbr with 1 boxes a device; every slot holds a box. `coarse_place`: no two middle boxes share a block; some middle box takes the last block.
All inputs are finite; a program needn't handle non-finite values.
Results may differ from the reference program's by a relative error of at most 0.00002.
Values sent between devices are 32-bit elements; how exact they have to be, the bound alone decides.
A program may use at most 128 MiB of HBM per device.

```python
import math
import jax
import jax.numpy as jnp

BOX = 32
COARSE_DEV = 1
FINE_DEV = 8
GRID = 256
BOT_ITERS = 12
FINE_BOXES = 1024
COARSE_BOXES = 128
N_BOX = 32
N_NODE = 4
DEVICES = 128


def live_counts(key):
    counts = jax.random.randint(jax.random.fold_in(key, 101), (DEVICES,), 1, FINE_DEV + 1)
    full_dev = jax.random.randint(jax.random.fold_in(key, 102), (), 0, DEVICES)
    return counts.at[full_dev].set(FINE_DEV).astype(jnp.int32)


def chain_lists(key, counts, per_device):
    slot_total = per_device * DEVICES
    slot_ids = jnp.arange(slot_total, dtype=jnp.int32)
    dev_ids = slot_ids // per_device
    in_dev = slot_ids % per_device
    own_count = counts[dev_ids]
    is_live = in_dev < own_count
    prev_count = counts[jnp.clip(dev_ids - 1, 0, DEVICES - 1)]
    low_link = jnp.where(in_dev > 0, per_device + in_dev - 1, jnp.where(dev_ids > 0, prev_count - 1, -1))
    high_link = jnp.where(in_dev + 1 < own_count, per_device + in_dev + 1, jnp.where(dev_ids < DEVICES - 1, 2 * per_device, -1))
    offset = jax.random.randint(jax.random.fold_in(key, 201), (slot_total, 4), -1, 2)
    raw_dev = dev_ids[:, None] + offset
    other_dev = jnp.clip(raw_dev, 0, DEVICES - 1)
    other_count = counts[other_dev]
    picked = jax.random.randint(jax.random.fold_in(key, 202), (slot_total, 4), 0, per_device) % other_count
    kept_side = (jax.random.randint(jax.random.fold_in(key, 203), (slot_total, 4), 0, 4) > 0) & (raw_dev >= 0) & (raw_dev < DEVICES)
    cross = jnp.where(kept_side, (offset + 1) * per_device + picked, -1)
    linked = jnp.concatenate([low_link[:, None], high_link[:, None], cross], 1)
    return jnp.where(is_live[:, None], linked, -1).astype(jnp.int32)


def draw_fine_count(key, part):
    counts = live_counts(key)
    return counts.reshape(N_BOX, N_NODE)


def draw_fine_nbr(key, part):
    counts = live_counts(key)
    key = jax.random.fold_in(key, 2)
    return chain_lists(key, counts, FINE_DEV)


def draw_coarse_nbr(key, part):
    key = jax.random.fold_in(key, 3)
    return chain_lists(key, jnp.full((DEVICES,), COARSE_DEV, jnp.int32), COARSE_DEV)


def draw_coarse_place(key, part):
    key = jax.random.fold_in(key, 4)
    block_total = (GRID // (BOX // 4)) ** 3
    order = jax.random.permutation(key, block_total).astype(jnp.int32)
    chosen = order[:COARSE_DEV * DEVICES]
    has_last = jnp.any(chosen == block_total - 1)
    return jnp.where(has_last, chosen, chosen.at[0].set(block_total - 1)).astype(jnp.int32)


def steps_of(stream_key, extent, cuts, low, largest):
    gain = 1.0
    for position, parts in cuts:
        draws = jax.random.uniform(jax.random.fold_in(jax.random.fold_in(stream_key, 6), position), (parts,), jnp.float32, low / len(cuts), largest / len(cuts))
        gain = gain * jnp.repeat(jnp.exp(draws), extent[position] // parts).reshape((-1,) + (1,) * (len(extent) - 1 - position))
    return gain


def bell_draw(stream_key, dims, width, limit, split=(), kind=jnp.bfloat16):
    drawn = jax.random.normal(stream_key, dims, jnp.float32) * width
    if len(split) > 0:
        drawn = steps_of(stream_key, dims, split, -0.22, 0.18) * drawn
    return jnp.clip(drawn, min=-limit, max=limit).astype(kind)


def setup_inputs(seed: int = 0) -> dict:
    streams_of = jax.random.split(jax.random.key(seed), 11)
    return {
        "fine_rhs": bell_draw(streams_of[0], (FINE_BOXES, BOX, BOX * BOX), 1.0, 6.0, ((0, 128),), jnp.float32),
        "fine_diag": jnp.clip(jnp.exp(math.log(4.0) - 2.7725887 * jax.random.uniform(streams_of[1], (FINE_BOXES, BOX, BOX * BOX), jnp.float32) ** steps_of(streams_of[1], (FINE_BOXES, BOX, BOX * BOX), ((0, 128),), -0.2, 0.2)), 0.25, 4.0),
        "fine_count": draw_fine_count(jax.random.fold_in(streams_of[10], 71), 0),
        "fine_nbr": draw_fine_nbr(jax.random.fold_in(streams_of[10], 71), 0),
        "fine_cover": jax.vmap(lambda own: jax.random.permutation(own, N_NODE * FINE_DEV))(jax.random.split(streams_of[4], N_BOX)).reshape((N_BOX, N_NODE * FINE_DEV)).astype(jnp.int32),
        "coarse_source": bell_draw(streams_of[5], (COARSE_BOXES, BOX, BOX * BOX), 1.0, 6.0, ((0, 128),), jnp.float32),
        "coarse_diag": jnp.clip(jnp.exp(math.log(4.0) - 2.7725887 * jax.random.uniform(streams_of[6], (COARSE_BOXES, BOX, BOX * BOX), jnp.float32) ** steps_of(streams_of[6], (COARSE_BOXES, BOX, BOX * BOX), ((0, 128),), -0.2, 0.2)), 0.25, 4.0),
        "coarse_nbr": draw_coarse_nbr(jax.random.fold_in(streams_of[10], 71), 0),
        "coarse_place": draw_coarse_place(jax.random.fold_in(streams_of[10], 71), 0),
        "bottom_diag": jnp.clip(jnp.exp(math.log(6.0) - 4.0943445 * jax.random.uniform(streams_of[9], (GRID, GRID, GRID), jnp.float32) ** steps_of(streams_of[9], (GRID, GRID, GRID), ((0, 32), (1, 4)), -0.2, 0.2)), 0.1, 6.0),
    }


relax = 0.8
opposite_faces = (1, 0, 3, 2, 5, 4)


def shift_sum(current, low_x, high_x, low_y, high_y, low_z, high_z):
    edge_len = low_y.shape[2]
    plane_len = current.shape[2]
    along_x = jnp.concatenate([low_x, current[:, :-1]], 1) + jnp.concatenate([current[:, 1:], high_x], 1)
    along_y = jnp.concatenate([low_y, current[:, :, :-edge_len]], 2) + jnp.concatenate([current[:, :, edge_len:], high_y], 2)
    column = jnp.arange(plane_len, dtype=jnp.int32) % edge_len
    below_z = jnp.where(column == 0, jnp.repeat(low_z, edge_len, axis=2), jnp.concatenate([current[:, :, :1], current[:, :, :-1]], 2))
    above_z = jnp.where(column == edge_len - 1, jnp.repeat(high_z, edge_len, axis=2), jnp.concatenate([current[:, :, 1:], current[:, :, -1:]], 2))
    return along_x + along_y + below_z + above_z


def box_sum(current, ghosts):
    box_count, edge_len, plane_len = current.shape

    def face_of(face_no):
        return ghosts[:, face_no].reshape(box_count, edge_len, edge_len)

    return shift_sum(current, ghosts[:, 0:1], ghosts[:, 1:2], face_of(2), face_of(3), face_of(4), face_of(5))


def grid_around(current):
    padded = jnp.pad(current, 1)
    total = padded[2:, 1:-1, 1:-1] + padded[:-2, 1:-1, 1:-1]
    total = total + padded[1:-1, 2:, 1:-1] + padded[1:-1, :-2, 1:-1]
    return total + padded[1:-1, 1:-1, 2:] + padded[1:-1, 1:-1, :-2]


def box_faces(current):
    box_count, edge_len, plane_len = current.shape
    return jnp.stack([current[:, 0], current[:, edge_len - 1],
                      current[:, :, :edge_len].reshape(box_count, plane_len),
                      current[:, :, plane_len - edge_len:].reshape(box_count, plane_len),
                      current[:, :, 0::edge_len].reshape(box_count, plane_len),
                      current[:, :, edge_len - 1::edge_len].reshape(box_count, plane_len)], 1)


def level_ghosts(current, nbr_lists, per_device):
    box_total = current.shape[0]
    faces_all = box_faces(current)
    slot_ids = jnp.arange(box_total, dtype=jnp.int32)
    window_base = slot_ids - slot_ids % per_device - per_device
    targets = window_base[:, None] + nbr_lists
    chosen = faces_all[jnp.clip(targets, 0, box_total - 1), jnp.array(opposite_faces, dtype=jnp.int32)[None, :]]
    return jnp.where((nbr_lists >= 0)[:, :, None], chosen, 0.0)


def relax_first(source, diagonal):
    return relax * (source / (6.0 + diagonal))


def relax_again(current, source, diagonal, around):
    image_sum = (6.0 + diagonal) * current - around
    return current + relax * ((source - image_sum) / (6.0 + diagonal))


def residual_of(current, source, diagonal, around):
    return source - ((6.0 + diagonal) * current - around)


def coarsen(current, factor, weight_scale):
    box_count, edge_len, plane_len = current.shape
    small_len = edge_len // factor
    shaped = current.reshape(box_count, small_len, factor, small_len, factor, small_len, factor)
    return shaped.sum(axis=(2, 4, 6)) * weight_scale


def refine(pieces, factor):
    box_count, small_len = pieces.shape[0], pieces.shape[1]
    grown = jnp.repeat(jnp.repeat(jnp.repeat(pieces, factor, axis=1), factor, axis=2), factor, axis=3)
    return grown.reshape(box_count, small_len * factor, (small_len * factor) ** 2)


def to_octants(current):
    box_count, edge_len, plane_len = current.shape
    half_len = edge_len // 2
    shaped = current.reshape(box_count, 2, half_len, 2, half_len, 2, half_len)
    return shaped.transpose(0, 1, 3, 5, 2, 4, 6).reshape(box_count * 8, half_len, half_len, half_len)


def from_octants(pieces):
    half_len = pieces.shape[1]
    box_count = pieces.shape[0] // 8
    shaped = pieces.reshape(box_count, 2, 2, 2, half_len, half_len, half_len)
    return shaped.transpose(0, 1, 4, 2, 5, 3, 6).reshape(box_count, 2 * half_len, 4 * half_len * half_len)


def blocks_to_grid(blocks, per_side):
    quarter = blocks.shape[1]
    shaped = blocks.reshape(per_side, per_side, per_side, quarter, quarter, quarter)
    grid_len = per_side * quarter
    return shaped.transpose(0, 3, 1, 4, 2, 5).reshape(grid_len, grid_len, grid_len)


def grid_to_blocks(grid, quarter):
    grid_len = grid.shape[0]
    per_side = grid_len // quarter
    shaped = grid.reshape(per_side, quarter, per_side, quarter, per_side, quarter)
    return shaped.transpose(0, 2, 4, 1, 3, 5).reshape(per_side ** 3, quarter, quarter, quarter)


def reference(fine_rhs, fine_diag, fine_count, fine_nbr, fine_cover, coarse_source, coarse_diag, coarse_nbr, coarse_place, bottom_diag):
    fine_total = fine_rhs.shape[0]
    half_len = BOX // 2
    quarter = BOX // 4
    per_side = GRID // quarter
    slot_ids = jnp.arange(fine_total, dtype=jnp.int32)
    is_live = (slot_ids % FINE_DEV) < fine_count.reshape(-1)[slot_ids // FINE_DEV]
    targets = (slot_ids // (N_NODE * FINE_DEV)) * (N_NODE * COARSE_DEV * 8) + fine_cover.reshape(-1)

    def fine_around(current):
        return box_sum(current, level_ghosts(current, fine_nbr, FINE_DEV))

    def coarse_around(current):
        return box_sum(current, level_ghosts(current, coarse_nbr, COARSE_DEV))

    fine = relax_first(fine_rhs, fine_diag)
    fine = relax_again(fine, fine_rhs, fine_diag, fine_around(fine))
    fine_res = jnp.where(is_live[:, None, None], residual_of(fine, fine_rhs, fine_diag, fine_around(fine)), 0.0)
    octants = coarsen(fine_res, 2, 0.5)
    placed = jnp.zeros((COARSE_BOXES * 8, half_len, half_len, half_len), jnp.float32).at[targets].set(octants)
    coarse_rhs = coarse_source + from_octants(placed)

    coarse = relax_first(coarse_rhs, coarse_diag)
    coarse = relax_again(coarse, coarse_rhs, coarse_diag, coarse_around(coarse))
    coarse_res = residual_of(coarse, coarse_rhs, coarse_diag, coarse_around(coarse))
    blocks = coarsen(coarse_res, 4, 0.25)
    grid_rhs = blocks_to_grid(jnp.zeros((per_side ** 3, quarter, quarter, quarter), jnp.float32).at[coarse_place].set(blocks), per_side)
    solved = relax_first(grid_rhs, bottom_diag)
    for sweep_no in range(BOT_ITERS - 1):
        solved = relax_again(solved, grid_rhs, bottom_diag, grid_around(solved))

    coarse = coarse + refine(grid_to_blocks(solved, quarter)[coarse_place], 4)
    for sweep_no in range(2):
        coarse = relax_again(coarse, coarse_rhs, coarse_diag, coarse_around(coarse))

    fine = fine + refine(to_octants(coarse)[targets], 2)
    for sweep_no in range(2):
        fine = relax_again(fine, fine_rhs, fine_diag, fine_around(fine))
    return jnp.where(is_live[:, None, None], fine, 0.0), coarse
```

```python
import functools

import jax
import jax.numpy as jnp
from jax import lax
from jax.experimental import pallas as pl
from jax.experimental.pallas import tpu as pltpu
from jax.sharding import PartitionSpec as P

F32, BF16, I32 = jnp.float32, jnp.bfloat16, jnp.int32
MESH = pl.DeviceIdType.MESH
BOT_ITERS = 12
HALO = BOT_ITERS - 1
Y_HALO = 16
TILES = 8


def grid_of(n_box):
    return {32: (4, 4, 2), 8: (2, 2, 2)}[n_box]


def lanes_of(shape):
    return lax.broadcasted_iota(I32, shape, len(shape) - 1)


def rows_of(shape):
    return lax.broadcasted_iota(I32, shape, len(shape) - 2)


def thirds(a):
    high = a.astype(BF16)
    rest = a - high.astype(F32)
    middle = rest.astype(BF16)
    low = (rest - middle.astype(F32)).astype(BF16)
    return high, middle, low


def pick_right(a, one_hot):
    high, middle, low = [jnp.dot(t, one_hot, preferred_element_type=F32) for t in thirds(a)]
    return high + (middle + low)


def pick_left(one_hot, a):
    high, middle, low = [jnp.dot(one_hot, t, preferred_element_type=F32) for t in thirds(a)]
    return high + (middle + low)


def one_hot_of(shape, test):
    return jnp.where(test(rows_of(shape), lanes_of(shape)), 1.0, 0.0).astype(BF16)


def roll_lanes(a, shift):
    shift = shift % 128
    return a if shift == 0 else pltpu.roll(a, shift, 1)


def tiles_of(ref, box):
    return [ref[box, :, 128 * t : 128 * (t + 1)] for t in range(TILES)]


def pack_faces(tiles):
    lane = lanes_of((32, 128))
    within, quarter = lane % 32, lane // 32
    first, last = tiles[0], tiles[-1]
    packed = jnp.where(
        quarter == 0,
        first,
        jnp.where(
            quarter == 1,
            jnp.where(within < 16, roll_lanes(first, 40), roll_lanes(first, 24)),
            jnp.where(
                quarter == 2,
                jnp.where(within < 16, roll_lanes(last, -24), roll_lanes(last, -40)),
                last,
            ),
        ),
    )
    for t in range(TILES):
        packed = jnp.where(within == t, roll_lanes(tiles[t], t), packed)
        packed = jnp.where(within == 31 - t, roll_lanes(tiles[t], -t), packed)
    return packed


def put_faces(tiles, yz_ref, x_ref, slot):
    yz_ref[slot] = pack_faces(tiles)
    for t in range(TILES):
        x_ref[slot, 0:1, 128 * t : 128 * (t + 1)] = tiles[t][0:1, :]
        x_ref[slot, 1:2, 128 * t : 128 * (t + 1)] = tiles[t][31:32, :]


def ghosts_of(yz_ref, x_ref, nbr_ref, box):
    def chosen(ref, face):
        which = nbr_ref[box, face]
        kept = jnp.where(which >= 0, 1.0, 0.0).astype(F32)
        return ref[jnp.maximum(which, 0)], kept

    def tile(face):
        value, kept = chosen(yz_ref, face)
        return value * kept

    x_low, low_kept = chosen(x_ref, 0)
    x_high, high_kept = chosen(x_ref, 1)
    return (
        x_low[1:2] * low_kept,
        x_high[0:1] * high_kept,
        tile(2),
        tile(3),
        tile(4),
        tile(5),
    )


def beside(tiles, ghosts):
    x_low, x_high, y_low, y_high, z_low, z_high = ghosts
    lane, row = lanes_of((32, 128)), rows_of((32, 128))
    within = lane % 32
    below = jnp.where(
        within < 8,
        roll_lanes(y_low, 56),
        jnp.where(within < 24, roll_lanes(y_low, 32), roll_lanes(y_low, 72)),
    )
    above = jnp.where(
        within < 8,
        roll_lanes(y_high, 56),
        jnp.where(within < 24, roll_lanes(y_high, 96), roll_lanes(y_high, 72)),
    )
    ups = [below] + [roll_lanes(t, 32) for t in tiles]
    downs = [roll_lanes(t, 96) for t in tiles] + [above]
    sums = []
    for t in range(TILES):
        cut = slice(128 * t, 128 * (t + 1))
        along_x = jnp.where(row == 0, x_low[:, cut], pltpu.roll(tiles[t], 1, 0)) + jnp.where(
            row == 31, x_high[:, cut], pltpu.roll(tiles[t], 31, 0)
        )
        along_y = jnp.where(lane < 32, ups[t], ups[t + 1]) + jnp.where(
            lane >= 96, downs[t + 1], downs[t]
        )
        along_z = jnp.where(
            within == 0, roll_lanes(z_low, t - 31), roll_lanes(tiles[t], 1)
        ) + jnp.where(within == 31, roll_lanes(z_high, 31 - t), roll_lanes(tiles[t], 127))
        sums.append(along_x + along_y + along_z)
    return sums


class Copies:
    def __init__(self, send_sems, recv_sems):
        self.send_sems, self.recv_sems, self.made = send_sems, recv_sems, []

    def start(self, source, target, device):
        number = len(self.made)
        copy = pltpu.make_async_remote_copy(
            src_ref=source,
            dst_ref=target,
            send_sem=self.send_sems.at[number],
            recv_sem=self.recv_sems.at[number],
            device_id=device,
            device_id_type=MESH,
        )
        copy.start()
        self.made.append(copy)
        return copy

    def finish(self):
        for copy in self.made:
            copy.wait_send()


def arrived(copies):
    for copy in copies:
        copy.wait_recv()


class Place:
    def __init__(self, n_box, n_node):
        self.n_box, self.n_node = n_box, n_node
        self.ny, self.nz, self.nc = grid_of(n_box)
        self.box, self.node = lax.axis_index("box"), lax.axis_index("node")
        self.core = self.box % self.nc
        self.z = self.box // self.nc % self.nz
        self.y = self.box // (self.nc * self.nz)

    def along_line(self, step):
        total = self.n_box * self.n_node
        other = (self.box * self.n_node + self.node + step + total) % total
        return (other // self.n_node, other % self.n_node)

    def next_node(self, step):
        return (self.node + step + self.n_node) % self.n_node

    def at_node(self, step):
        return (self.box, self.next_node(step))

    def at_box(self, step):
        return ((self.box + step + self.n_box) % self.n_box, self.node)

    def in_box(self, y, z, core):
        return ((y * self.nz + z) * self.nc + core, self.node)

    def peers_y(self):
        for step in range(1, self.ny):
            other = (self.y + step) % self.ny
            yield other, self.in_box(other, self.z, self.core)

    def peers_z(self):
        for step in range(1, self.nz):
            other = (self.z + step) % self.nz
            yield other, self.in_box(self.y, other, self.core)

    def peer_core(self):
        other = 1 - self.core
        return other, self.in_box(self.y, self.z, other)

    def peers_node(self):
        for step in range(1, self.n_node):
            yield self.next_node(step), self.at_node(step)

    def barrier(self, more):
        peers = [self.along_line(1), self.along_line(-1)] + more
        for peers_of in (self.peers_node, self.peers_y, self.peers_z):
            peers += [device for _, device in peers_of()]
        peers.append(self.peer_core()[1])
        barrier = pltpu.get_barrier_semaphore()
        for device in peers:
            pl.semaphore_signal(barrier, inc=1, device_id=device, device_id_type=MESH)
        pl.semaphore_wait(barrier, len(peers))


def send_faces(copies, here, yz_ref, x_ref, count):
    own, before, after = (pl.ds(count, count), pl.ds(0, count), pl.ds(2 * count, count))
    started = []
    for ref in (yz_ref, x_ref):
        started.append(copies.start(ref.at[own], ref.at[before], here.along_line(1)))
        started.append(copies.start(ref.at[own], ref.at[after], here.along_line(-1)))
    return started


def write_tiles(ref, box, tiles):
    for t in range(TILES):
        ref[box, :, 128 * t : 128 * (t + 1)] = tiles[t]


def first_sweep(boxes, u_ref, b_ref, d_ref, c_ref, yz_ref, x_ref):
    def one(box, carry):
        tiles = []
        for t in range(TILES):
            cut = slice(128 * t, 128 * (t + 1))
            scale = 0.8 / (6.0 + d_ref[box, :, cut])
            c_ref[box, :, cut] = scale
            tiles.append(scale * b_ref[box, :, cut])
        write_tiles(u_ref, box, tiles)
        put_faces(tiles, yz_ref, x_ref, boxes + box)
        return carry

    lax.fori_loop(0, boxes, one, 0)


def sweep_boxes(boxes, u_ref, b_ref, c_ref, ghosts, out_ref, faces, keep=None):
    yz_from, x_from, nbr_ref = ghosts

    def one(box, carry):
        tiles = tiles_of(u_ref, box)
        sums = beside(tiles, ghosts_of(yz_from, x_from, nbr_ref, box))
        fresh = []
        for t in range(TILES):
            cut = slice(128 * t, 128 * (t + 1))
            fresh.append(
                0.2 * tiles[t] + c_ref[box, :, cut] * (b_ref[box, :, cut] + sums[t])
            )
        if keep is not None:
            kept = keep(box)
            fresh = [t * kept for t in fresh]
        write_tiles(out_ref, box, fresh)
        if faces is not None:
            put_faces(fresh, faces[0], faces[1], boxes + box)
        return carry

    lax.fori_loop(0, boxes, one, 0)


def residual_boxes(boxes, u_ref, b_ref, d_ref, ghosts, r_ref, keep=None):
    yz_from, x_from, nbr_ref = ghosts

    def one(box, carry):
        tiles = tiles_of(u_ref, box)
        sums = beside(tiles, ghosts_of(yz_from, x_from, nbr_ref, box))
        for t in range(TILES):
            cut = slice(128 * t, 128 * (t + 1))
            left = b_ref[box, :, cut] - ((6.0 + d_ref[box, :, cut]) * tiles[t] - sums[t])
            r_ref[pl.ds(pl.multiple_of(box * 32, 32), 32), cut] = (
                left if keep is None else left * keep(box)
            )
        return carry

    lax.fori_loop(0, boxes, one, 0)


def down_kernel(
    n_box,
    n_node,
    fine_b,
    fine_d,
    count_ref,
    fine_nbr,
    cover_ref,
    source_ref,
    coarse_d,
    coarse_nbr,
    place_ref,
    bottom_d,
    fine_u,
    fine_c,
    coarse_u,
    coarse_b,
    coarse_c,
    reach,
    blocks_out,
    places_out,
    u_first,
    yz_fine_0,
    x_fine_0,
    yz_fine_1,
    x_fine_1,
    slab_c,
    rest_ref,
    octants,
    placed,
    lifted,
    found_at,
    cu_first,
    yz_coarse_0,
    x_coarse_0,
    yz_coarse_1,
    x_coarse_1,
    blocks,
    places,
    send_sems,
    recv_sems,
    local_sem,
):
    here = Place(n_box, n_node)
    copies = Copies(send_sems, recv_sems)
    boxes = fine_b.shape[0]
    here.barrier([here.at_box(1), here.at_box(-1), here.at_box(2), here.at_box(-2)])

    rows_x, rows_y = bottom_d.shape[0], bottom_d.shape[1]

    def scale_plane(x, carry):
        slab_c[x] = 0.8 / (6.0 + bottom_d[x])
        return carry

    lax.fori_loop(0, rows_x, scale_plane, 0)
    own_x, own_y = pl.ds(HALO, rows_x), pl.ds(Y_HALO, rows_y)
    own_copy = pltpu.make_async_copy(slab_c, reach.at[own_x, own_y], local_sem)
    own_copy.start()
    halo_y = [
        copies.start(
            slab_c.at[:, pl.ds(rows_y - Y_HALO, Y_HALO)],
            reach.at[own_x, pl.ds(0, Y_HALO)],
            here.at_node(1),
        ),
        copies.start(
            slab_c.at[:, pl.ds(0, Y_HALO)],
            reach.at[own_x, pl.ds(Y_HALO + rows_y, Y_HALO)],
            here.at_node(-1),
        ),
    ]

    first_sweep(boxes, u_first, fine_b, fine_d, fine_c, yz_fine_0, x_fine_0)
    faces = send_faces(copies, here, yz_fine_0, x_fine_0, boxes)

    for target in range(8 * n_node):
        slot = jnp.int32(-1)
        for box in range(boxes):
            slot = jnp.where(cover_ref[0, box] == target, box, slot)
        found_at[target] = slot

    own_copy.wait()
    arrived(halo_y)
    some = HALO - rows_x
    halo_x = [
        copies.start(reach.at[own_x], reach.at[pl.ds(HALO - rows_x, rows_x)], here.at_box(1)),
        copies.start(reach.at[own_x], reach.at[pl.ds(HALO + rows_x, rows_x)], here.at_box(-1)),
        copies.start(
            reach.at[pl.ds(HALO + rows_x - some, some)], reach.at[pl.ds(0, some)], here.at_box(2)
        ),
        copies.start(
            reach.at[pl.ds(HALO, some)],
            reach.at[pl.ds(HALO + 2 * rows_x, some)],
            here.at_box(-2),
        ),
    ]

    arrived(faces)
    sweep_boxes(
        boxes,
        u_first,
        fine_b,
        fine_c,
        (yz_fine_0, x_fine_0, fine_nbr),
        fine_u,
        (yz_fine_1, x_fine_1),
    )
    faces = send_faces(copies, here, yz_fine_1, x_fine_1, boxes)
    fold_yz = one_hot_of(
        (1024, 256), lambda r, l: (r // 64 == l // 16) & (r % 32 // 2 == l % 16)
    )
    fold_x = one_hot_of((16 * boxes, 32 * boxes), lambda r, l: l // 2 == r)
    arrived(faces)
    live = count_ref[0, 0]
    residual_boxes(
        boxes,
        fine_u,
        fine_b,
        fine_d,
        (yz_fine_1, x_fine_1, fine_nbr),
        rest_ref,
        lambda box: jnp.where(box < live, 1.0, 0.0).astype(F32),
    )
    cubes = pick_left(fold_x, pick_right(rest_ref[...], fold_yz)) * 0.5
    for box in range(boxes):
        octants[box] = cubes[16 * box : 16 * (box + 1)]

    def place_one(target, carry):
        slot = found_at[target]
        kept = jnp.where(slot >= 0, 1.0, 0.0).astype(F32)
        placed[target] = octants[jnp.maximum(slot, 0)] * kept
        return carry

    lax.fori_loop(0, 8 * n_node, place_one, 0)
    given = []
    for step, (other, device) in enumerate(here.peers_node()):
        given.append(
            copies.start(
                placed.at[pl.ds(pl.multiple_of(other * 8, 8), 8)], lifted.at[step], device
            )
        )
    spread = one_hot_of(
        (512, 512),
        lambda r, l: (r // 256 == l % 32 // 16) & (r % 256 // 16 == l // 32) & (r % 16 == l % 16),
    )
    arrived(given)
    total = placed[pl.ds(pl.multiple_of(here.node * 8, 8), 8)]
    for step in range(n_node - 1):
        total = total + lifted[step]
    pairs = jnp.concatenate(
        [jnp.concatenate([total[2 * k], total[2 * k + 1]], axis=1) for k in range(4)], axis=0
    )
    grown = pick_right(pairs, spread)
    for k in range(4):
        at_x, at_y = 16 * (k // 2), 512 * (k % 2)
        coarse_b[0, at_x : at_x + 16, at_y : at_y + 512] = (
            source_ref[0, at_x : at_x + 16, at_y : at_y + 512] + grown[16 * k : 16 * (k + 1)]
        )

    first_sweep(1, cu_first, coarse_b, coarse_d, coarse_c, yz_coarse_0, x_coarse_0)
    faces = send_faces(copies, here, yz_coarse_0, x_coarse_0, 1)
    arrived(faces)
    sweep_boxes(
        1,
        cu_first,
        coarse_b,
        coarse_c,
        (yz_coarse_0, x_coarse_0, coarse_nbr),
        coarse_u,
        (yz_coarse_1, x_coarse_1),
    )
    faces = send_faces(copies, here, yz_coarse_1, x_coarse_1, 1)
    fold_quarter = one_hot_of(
        (1024, 128), lambda r, l: (r // 128 == l % 64 // 8) & (r % 32 // 4 == l % 8)
    )
    arrived(faces)
    residual_boxes(
        1,
        coarse_u,
        coarse_b,
        coarse_d,
        (yz_coarse_1, x_coarse_1, coarse_nbr),
        rest_ref,
    )
    folded = pick_right(rest_ref[0:32], fold_quarter)
    early = pick_left(one_hot_of((8, 32), lambda r, l: l // 4 == r), folded)
    late = pick_left(one_hot_of((8, 32), lambda r, l: l // 4 == r + 4), folded)
    block = jnp.where(lanes_of((8, 128)) < 64, early, late) * 0.25
    y, z, core, node = here.y, here.z, here.core, here.node
    blocks[y, z, core, node] = block[0:4]
    places[y, z, core, node] = jnp.full((1, 128), place_ref[0], I32)

    def both(part, device):
        return [copies.start(part(ref), part(ref), device) for ref in (blocks, places)]

    waits = []
    for _, device in here.peers_node():
        waits += both(lambda ref: ref.at[y, z, core, node], device)
    arrived(waits)
    waits = []
    for _, device in here.peers_z():
        waits += both(lambda ref: ref.at[y, z, core], device)
    arrived(waits)
    waits = []
    for _, device in here.peers_y():
        waits += both(lambda ref: ref.at[y, :, core], device)
    arrived(waits)
    arrived(both(lambda ref: ref.at[:, :, core], here.peer_core()[1]))

    blocks_out[...] = blocks[...]
    row = jnp.zeros((1, 128), I32)
    lane = lanes_of((1, 128))
    number = 0
    for at_y in range(here.ny):
        for at_z in range(here.nz):
            for at_core in range(here.nc):
                for at_node in range(n_node):
                    row = jnp.where(lane == number, places[at_y, at_z, at_core, at_node], row)
                    number += 1
    places_out[...] = row

    arrived(halo_x)
    copies.finish()


def bottom_kernel(
    n_box, n_node, rows_x, rows_y, places, reach, blocks, out, scale, source, first, second
):
    deep, wide, long = reach.shape
    count = n_box * n_node
    per_side = long // 8
    at_x = lax.axis_index("box") * rows_x - HALO
    at_y = lax.axis_index("node") * rows_y - Y_HALO
    edge_y = per_side * 8
    tile_z = one_hot_of((128, long), lambda r, l: r % 8 == l % 8)
    untile_z = one_hot_of((long, 128), lambda r, l: r % 8 == l % 8)
    lane, row = lanes_of((8, 128)), rows_of((8, 128))
    block_z = lanes_of((64, long)) // 8

    def clear(x, carry):
        source[x] = jnp.zeros((wide, long), F32)
        return carry

    lax.fori_loop(0, source.shape[0], clear, 0)
    out[...] = jnp.zeros(out.shape, F32)

    def where_is(number):
        place = places[0, number]
        return (
            place // (per_side * per_side) * 8 - at_x,
            place // per_side % per_side * 8 - at_y,
            place % per_side,
        )

    def put(number, carry):
        x, y, z = where_is(number)

        @pl.when((x > -8) & (x < deep) & (y >= 0) & (y < wide))
        def _():
            block = blocks[number]
            parts = []
            for ix in range(8):
                spread = jnp.broadcast_to(block[ix % 4 : ix % 4 + 1], (8, 128))
                parts.append(jnp.where(lane // 8 == row + 8 * (ix // 4), spread, 0.0))
            tiled = pick_right(jnp.concatenate(parts, axis=0), tile_z)
            tiled = jnp.where(block_z == z, tiled, 0.0)
            rows = pl.ds(pl.multiple_of(y, 8), 8)
            for ix in range(8):
                source[x + ix + 8, rows, :] += tiled[8 * ix : 8 * (ix + 1)]

        return carry

    lax.fori_loop(0, count, put, 0)

    plane_y = rows_of((wide, long)) + at_y
    inside_y = (plane_y >= 0) & (plane_y < edge_y)

    def begin(x, carry):
        inside_x = jnp.where((at_x + x >= 0) & (at_x + x < rows_x * n_box), 1.0, 0.0)
        masked = jnp.where(inside_y, reach[x] * inside_x.astype(F32), 0.0)
        scale[x] = masked
        first[x] = masked * source[x + 8]
        return carry

    lax.fori_loop(0, deep, begin, 0)

    refs = (first, second)
    for sweep_no in range(HALO):
        left = HALO - 1 - sweep_no
        margin = (left + 7) // 8 * 8
        tall = rows_y + 2 * margin
        low = Y_HALO - margin
        here, there = refs[sweep_no % 2], refs[(sweep_no + 1) % 2]
        cut = slice(low, low + tall)
        z = lanes_of((tall, long))

        def plane(x, carry):
            mid = here[x, cut, :]
            around = here[x - 1, cut, :] + here[x + 1, cut, :]
            if low > 0:
                around += here[x, low - 1 : low + tall - 1, :]
                around += here[x, low + 1 : low + tall + 1, :]
            else:
                around += pltpu.roll(mid, 1, 0) + pltpu.roll(mid, tall - 1, 0)
            around += jnp.where(z == 0, 0.0, pltpu.roll(mid, 1, 1))
            around += jnp.where(z == long - 1, 0.0, pltpu.roll(mid, long - 1, 1))
            there[x, cut, :] = 0.2 * mid + scale[x, cut, :] * (source[x + 8, cut, :] + around)
            return carry

        lax.fori_loop(HALO - left, HALO + rows_x + left, plane, 0)
    solved = refs[HALO % 2]

    def take(number, carry):
        x, y, z = where_is(number)

        @pl.when((x == HALO) & (y >= Y_HALO) & (y < Y_HALO + rows_y))
        def _():
            rows = pl.ds(pl.multiple_of(y, 8), 8)
            stack = jnp.concatenate([solved[HALO + ix, rows, :] for ix in range(8)], axis=0)
            spread = pick_right(jnp.where(block_z == z, stack, 0.0), untile_z)
            lines = []
            for ix in range(8):
                mine = jnp.where(
                    lane // 8 == row + 8 * (ix // 4), spread[8 * ix : 8 * (ix + 1)], 0.0
                )
                lines.append(jnp.sum(mine, axis=0, keepdims=True))
            for ix in range(4):
                out[number, ix : ix + 1] = lines[ix] + lines[ix + 4]

        return carry

    lax.fori_loop(0, count, take, 0)


def up_kernel(
    n_box,
    n_node,
    parts,
    fine_u,
    fine_c,
    fine_b,
    count_ref,
    fine_nbr,
    cover_ref,
    coarse_u,
    coarse_b,
    coarse_c,
    coarse_nbr,
    fine_out,
    coarse_out,
    from_core,
    sum_core,
    from_y,
    sum_y,
    from_z,
    sum_z,
    from_node,
    own_block,
    cu_first,
    cu_second,
    yz_coarse_0,
    x_coarse_0,
    yz_coarse_1,
    x_coarse_1,
    octants,
    picked,
    u_first,
    u_second,
    yz_fine_0,
    x_fine_0,
    yz_fine_1,
    x_fine_1,
    send_sems,
    recv_sems,
):
    here = Place(n_box, n_node)
    copies = Copies(send_sems, recv_sems)
    boxes = fine_u.shape[0]
    here.barrier([])

    other, device = here.peer_core()
    arrived([copies.start(parts.at[:, :, other], from_core, device)])
    sum_core[...] = parts[:, :, here.core] + from_core[...]
    waits = [
        copies.start(sum_core.at[other], from_y.at[step], device)
        for step, (other, device) in enumerate(here.peers_y())
    ]
    arrived(waits)
    sum_y[...] = sum_core[here.y] + sum([from_y[step] for step in range(here.ny - 1)])
    waits = [
        copies.start(sum_y.at[other], from_z.at[step], device)
        for step, (other, device) in enumerate(here.peers_z())
    ]
    arrived(waits)
    sum_z[...] = sum_y[here.z] + sum([from_z[step] for step in range(here.nz - 1)])
    waits = [
        copies.start(sum_z.at[other], from_node.at[step], device)
        for step, (other, device) in enumerate(here.peers_node())
    ]
    grow_quarter = one_hot_of(
        (128, 1024), lambda r, l: r == l // 128 * 8 + l % 32 // 4
    )
    arrived(waits)
    block = sum_z[here.node] + sum([from_node[step] for step in range(n_node - 1)])
    own_block[0:4] = block
    own_block[4:8] = pltpu.roll(block, 64, 1)
    grown = pick_right(own_block[...], grow_quarter)
    grown = pick_left(one_hot_of((32, 8), lambda r, l: r // 4 == l), grown)
    cu_first[0] = coarse_u[0] + grown
    put_faces(tiles_of(cu_first, 0), yz_coarse_0, x_coarse_0, 1)
    faces = send_faces(copies, here, yz_coarse_0, x_coarse_0, 1)
    arrived(faces)
    sweep_boxes(
        1,
        cu_first,
        coarse_b,
        coarse_c,
        (yz_coarse_0, x_coarse_0, coarse_nbr),
        cu_second,
        (yz_coarse_1, x_coarse_1),
    )
    faces = send_faces(copies, here, yz_coarse_1, x_coarse_1, 1)
    split = one_hot_of(
        (512, 512),
        lambda r, l: (l // 256 == r % 32 // 16) & (l % 256 // 16 == r // 32) & (l % 16 == r % 16),
    )
    arrived(faces)
    sweep_boxes(
        1,
        cu_second,
        coarse_b,
        coarse_c,
        (yz_coarse_1, x_coarse_1, coarse_nbr),
        coarse_out,
        None,
    )

    quarters = jnp.concatenate(
        [
            coarse_out[0, 16 * (k // 2) : 16 * (k // 2) + 16, 512 * (k % 2) : 512 * (k % 2) + 512]
            for k in range(4)
        ],
        axis=0,
    )
    cubes = pick_right(quarters, split)
    base = pl.multiple_of(here.node * 8, 8)
    for k in range(8):
        octants[base + k] = cubes[16 * (k // 2) : 16 * (k // 2) + 16, 256 * (k % 2) : 256 * (k % 2) + 256]
    own = octants.at[pl.ds(base, 8)]
    waits = [copies.start(own, own, device) for _, device in here.peers_node()]
    grow_yz = one_hot_of(
        (256, 1024), lambda r, l: (l // 64 == r // 16) & (l % 32 // 2 == r % 16)
    )
    grow_x = one_hot_of((32 * boxes, 16 * boxes), lambda r, l: r // 2 == l)
    arrived(waits)
    for box in range(boxes):
        picked[16 * box : 16 * (box + 1)] = octants[cover_ref[0, box]]
    tall = pick_right(pick_left(grow_x, picked[...]), grow_yz)
    for box in range(boxes):
        u_first[box] = fine_u[box] + tall[32 * box : 32 * (box + 1)]

    def faces_of(box, carry):
        put_faces(tiles_of(u_first, box), yz_fine_0, x_fine_0, boxes + box)
        return carry

    lax.fori_loop(0, boxes, faces_of, 0)
    arrived(send_faces(copies, here, yz_fine_0, x_fine_0, boxes))
    sweep_boxes(
        boxes,
        u_first,
        fine_b,
        fine_c,
        (yz_fine_0, x_fine_0, fine_nbr),
        u_second,
        (yz_fine_1, x_fine_1),
    )
    arrived(send_faces(copies, here, yz_fine_1, x_fine_1, boxes))
    live = count_ref[0, 0]
    sweep_boxes(
        boxes,
        u_second,
        fine_b,
        fine_c,
        (yz_fine_1, x_fine_1, fine_nbr),
        fine_out,
        None,
        lambda box: jnp.where(box < live, 1.0, 0.0).astype(F32),
    )
    copies.finish()


VMEM, SMEM, ANY = (
    pl.BlockSpec(memory_space=pltpu.VMEM),
    pl.BlockSpec(memory_space=pltpu.SMEM),
    pl.BlockSpec(memory_space=pl.ANY),
)


def shards(
    n_box,
    n_node,
    fine_rhs,
    fine_diag,
    fine_count,
    fine_nbr,
    fine_cover,
    coarse_source,
    coarse_diag,
    coarse_nbr,
    coarse_place,
    bottom_diag,
):
    boxes = fine_rhs.shape[0]
    ny, nz, nc = grid_of(n_box)
    rows_x, rows_y, long = bottom_diag.shape
    deep, wide = rows_x + 2 * HALO, rows_y + 2 * Y_HALO
    count = n_box * n_node

    def like(shape, kind=F32):
        return jax.ShapeDtypeStruct(shape, kind)

    fine, coarse = (boxes, 32, 1024), (1, 32, 1024)
    grid = (ny, nz, nc, n_node)
    limit = 48 * 1024 * 1024
    fine_u, fine_c, coarse_u, coarse_b, coarse_c, reach, blocks, places = pl.pallas_call(
        functools.partial(down_kernel, n_box, n_node),
        out_shape=(
            like(fine),
            like(fine),
            like(coarse),
            like(coarse),
            like(coarse),
            like((deep, wide, long)),
            like(grid + (4, 128)),
            like((1, 128), I32),
        ),
        in_specs=[VMEM, VMEM, SMEM, SMEM, SMEM, VMEM, VMEM, SMEM, SMEM, VMEM],
        out_specs=(VMEM, VMEM, VMEM, VMEM, VMEM, ANY, VMEM, VMEM),
        scratch_shapes=[
            pltpu.VMEM(fine, F32),
            pltpu.VMEM((3 * boxes, 32, 128), F32),
            pltpu.VMEM((3 * boxes, 2, 1024), F32),
            pltpu.VMEM((3 * boxes, 32, 128), F32),
            pltpu.VMEM((3 * boxes, 2, 1024), F32),
            pltpu.VMEM((rows_x, rows_y, long), F32),
            pltpu.VMEM((32 * boxes, 1024), F32),
            pltpu.VMEM((boxes, 16, 256), F32),
            pltpu.VMEM((8 * n_node, 16, 256), F32),
            pltpu.VMEM((n_node - 1, 8, 16, 256), F32),
            pltpu.SMEM((8 * n_node,), I32),
            pltpu.VMEM(coarse, F32),
            pltpu.VMEM((3, 32, 128), F32),
            pltpu.VMEM((3, 2, 1024), F32),
            pltpu.VMEM((3, 32, 128), F32),
            pltpu.VMEM((3, 2, 1024), F32),
            pltpu.VMEM(grid + (4, 128), F32),
            pltpu.VMEM(grid + (1, 128), I32),
            pltpu.SemaphoreType.DMA((64,)),
            pltpu.SemaphoreType.DMA((64,)),
            pltpu.SemaphoreType.DMA,
        ],
        compiler_params=pltpu.CompilerParams(
            collective_id=0, has_side_effects=True, vmem_limit_bytes=limit
        ),
        name="down",
    )(
        fine_rhs,
        fine_diag,
        fine_count,
        fine_nbr,
        fine_cover,
        coarse_source,
        coarse_diag,
        coarse_nbr,
        coarse_place,
        bottom_diag,
    )
    parts = pl.pallas_call(
        functools.partial(bottom_kernel, n_box, n_node, rows_x, rows_y),
        out_shape=like((count, 4, 128)),
        in_specs=[SMEM, VMEM, VMEM],
        out_specs=VMEM,
        scratch_shapes=[
            pltpu.VMEM((deep, wide, long), F32),
            pltpu.VMEM((deep + 16, wide, long), F32),
            pltpu.VMEM((deep, wide, long), F32),
            pltpu.VMEM((deep, wide, long), F32),
        ],
        compiler_params=pltpu.CompilerParams(vmem_limit_bytes=limit),
        name="bottom",
    )(places, reach, blocks.reshape(count, 4, 128))
    fine_out, coarse_out = pl.pallas_call(
        functools.partial(up_kernel, n_box, n_node),
        out_shape=(like(fine), like(coarse)),
        in_specs=[VMEM, VMEM, VMEM, VMEM, SMEM, SMEM, SMEM, VMEM, VMEM, VMEM, SMEM],
        out_specs=(VMEM, VMEM),
        scratch_shapes=[
            pltpu.VMEM((ny, nz, n_node, 4, 128), F32),
            pltpu.VMEM((ny, nz, n_node, 4, 128), F32),
            pltpu.VMEM((ny - 1, nz, n_node, 4, 128), F32),
            pltpu.VMEM((nz, n_node, 4, 128), F32),
            pltpu.VMEM((nz - 1, n_node, 4, 128), F32),
            pltpu.VMEM((n_node, 4, 128), F32),
            pltpu.VMEM((n_node - 1, 4, 128), F32),
            pltpu.VMEM((8, 128), F32),
            pltpu.VMEM(coarse, F32),
            pltpu.VMEM(coarse, F32),
            pltpu.VMEM((3, 32, 128), F32),
            pltpu.VMEM((3, 2, 1024), F32),
            pltpu.VMEM((3, 32, 128), F32),
            pltpu.VMEM((3, 2, 1024), F32),
            pltpu.VMEM((8 * n_node, 16, 256), F32),
            pltpu.VMEM((16 * boxes, 256), F32),
            pltpu.VMEM(fine, F32),
            pltpu.VMEM(fine, F32),
            pltpu.VMEM((3 * boxes, 32, 128), F32),
            pltpu.VMEM((3 * boxes, 2, 1024), F32),
            pltpu.VMEM((3 * boxes, 32, 128), F32),
            pltpu.VMEM((3 * boxes, 2, 1024), F32),
            pltpu.SemaphoreType.DMA((48,)),
            pltpu.SemaphoreType.DMA((48,)),
        ],
        compiler_params=pltpu.CompilerParams(
            collective_id=1, has_side_effects=True, vmem_limit_bytes=limit
        ),
        name="up",
    )(
        parts.reshape(grid + (4, 128)),
        fine_u,
        fine_c,
        fine_rhs,
        fine_count,
        fine_nbr,
        fine_cover,
        coarse_u,
        coarse_b,
        coarse_c,
        coarse_nbr,
    )
    return fine_out, coarse_out


def solution(mesh):
    n_box, n_node = mesh.shape["box"], mesh.shape["node"]
    return jax.shard_map(
        functools.partial(shards, n_box, n_node),
        mesh=mesh,
        in_specs=(
            P(("box", "node"), None, None),
            P(("box", "node"), None, None),
            P("box", "node"),
            P(("box", "node"), None),
            P("box", "node"),
            P(("box", "node"), None, None),
            P(("box", "node"), None, None),
            P(("box", "node"), None),
            P(("box", "node")),
            P("box", "node", None),
        ),
        out_specs=(P(("box", "node"), None, None), P(("box", "node"), None, None)),
        check_vma=False,
    )
```

```python
import functools

import jax
import jax.numpy as jnp
from jax import lax
from jax.experimental import pallas as pl
from jax.experimental.pallas import tpu as pltpu
from jax.sharding import PartitionSpec as P

F32, BF16, I32 = jnp.float32, jnp.bfloat16, jnp.int32
MESH = pl.DeviceIdType.MESH
BOT_ITERS = 12
HALO = BOT_ITERS - 1
Y_HALO = 16
TILES = 8


def grid_of(n_box):
    return {32: (4, 4, 2), 8: (2, 2, 2)}[n_box]


def lanes_of(shape):
    return lax.broadcasted_iota(I32, shape, len(shape) - 1)


def rows_of(shape):
    return lax.broadcasted_iota(I32, shape, len(shape) - 2)


def thirds(a):
    high = a.astype(BF16)
    rest = a - high.astype(F32)
    middle = rest.astype(BF16)
    low = (rest - middle.astype(F32)).astype(BF16)
    return high, middle, low


def pick_right(a, one_hot):
    high, middle, low = [jnp.dot(t, one_hot, preferred_element_type=F32) for t in thirds(a)]
    return high + (middle + low)


def pick_left(one_hot, a):
    high, middle, low = [jnp.dot(one_hot, t, preferred_element_type=F32) for t in thirds(a)]
    return high + (middle + low)


def one_hot_of(shape, test):
    return jnp.where(test(rows_of(shape), lanes_of(shape)), 1.0, 0.0).astype(BF16)


def roll_lanes(a, shift):
    shift = shift % 128
    return a if shift == 0 else pltpu.roll(a, shift, 1)


def tiles_of(ref, box):
    return [ref[box, :, 128 * t : 128 * (t + 1)] for t in range(TILES)]


def pack_faces(tiles):
    lane = lanes_of((32, 128))
    within, quarter = lane & 31, lane >> 5
    first, last = tiles[0], tiles[-1]
    packed = jnp.where(
        quarter == 0,
        first,
        jnp.where(
            quarter == 1,
            jnp.where(within < 16, roll_lanes(first, 40), roll_lanes(first, 24)),
            jnp.where(
                quarter == 2,
                jnp.where(within < 16, roll_lanes(last, -24), roll_lanes(last, -40)),
                last,
            ),
        ),
    )
    for t in range(TILES):
        packed = jnp.where(within == t, roll_lanes(tiles[t], t), packed)
        packed = jnp.where(within == 31 - t, roll_lanes(tiles[t], -t), packed)
    return packed


def put_faces(tiles, yz_ref, x_ref, slot):
    yz_ref[slot] = pack_faces(tiles)
    for t in range(TILES):
        x_ref[slot, 0:1, 128 * t : 128 * (t + 1)] = tiles[t][0:1, :]
        x_ref[slot, 1:2, 128 * t : 128 * (t + 1)] = tiles[t][31:32, :]


def ghosts_of(yz_ref, x_ref, nbr_ref, box):
    def chosen(ref, face):
        which = nbr_ref[box, face]
        kept = jnp.where(which >= 0, 1.0, 0.0).astype(F32)
        return ref[jnp.maximum(which, 0)], kept

    def tile(face):
        value, kept = chosen(yz_ref, face)
        return value * kept

    x_low, low_kept = chosen(x_ref, 0)
    x_high, high_kept = chosen(x_ref, 1)
    return (
        x_low[1:2] * low_kept,
        x_high[0:1] * high_kept,
        tile(2),
        tile(3),
        tile(4),
        tile(5),
    )


def beside(tiles, ghosts):
    x_low, x_high, y_low, y_high, z_low, z_high = ghosts
    lane, row = lanes_of((32, 128)), rows_of((32, 128))
    within = lane & 31
    below = jnp.where(
        within < 8,
        roll_lanes(y_low, 56),
        jnp.where(within < 24, roll_lanes(y_low, 32), roll_lanes(y_low, 72)),
    )
    above = jnp.where(
        within < 8,
        roll_lanes(y_high, 56),
        jnp.where(within < 24, roll_lanes(y_high, 96), roll_lanes(y_high, 72)),
    )
    ups = [below] + [roll_lanes(t, 32) for t in tiles]
    downs = [roll_lanes(t, 96) for t in tiles] + [above]
    sums = []
    for t in range(TILES):
        cut = slice(128 * t, 128 * (t + 1))
        along_x = jnp.where(row == 0, x_low[:, cut], pltpu.roll(tiles[t], 1, 0)) + jnp.where(
            row == 31, x_high[:, cut], pltpu.roll(tiles[t], 31, 0)
        )
        along_y = jnp.where(lane < 32, ups[t], ups[t + 1]) + jnp.where(
            lane >= 96, downs[t + 1], downs[t]
        )
        along_z = jnp.where(
            within == 0, roll_lanes(z_low, t - 31), roll_lanes(tiles[t], 1)
        ) + jnp.where(within == 31, roll_lanes(z_high, 31 - t), roll_lanes(tiles[t], 127))
        sums.append(along_x + along_y + along_z)
    return sums


class Copies:
    def __init__(self, send_sems, recv_sems):
        self.send_sems, self.recv_sems, self.made = send_sems, recv_sems, []

    def start(self, source, target, device):
        number = len(self.made)
        copy = pltpu.make_async_remote_copy(
            src_ref=source,
            dst_ref=target,
            send_sem=self.send_sems.at[number],
            recv_sem=self.recv_sems.at[number],
            device_id=device,
            device_id_type=MESH,
        )
        copy.start()
        self.made.append(copy)
        return copy

    def finish(self):
        for copy in self.made:
            copy.wait_send()


def arrived(copies):
    for copy in copies:
        copy.wait_recv()


class Place:
    def __init__(self, n_box, n_node):
        self.n_box, self.n_node = n_box, n_node
        self.ny, self.nz, self.nc = grid_of(n_box)
        self.box, self.node = lax.axis_index("box"), lax.axis_index("node")
        self.chips = self.ny * self.nz * n_node
        self.core = self.box & 1
        self.z = (self.box >> 1) & (self.nz - 1)
        self.y = (self.box >> 1) >> (self.nz.bit_length() - 1)

    def along_line(self, step):
        total = self.n_box * self.n_node
        other = (self.box * self.n_node + self.node + step + total) % total
        return (other // self.n_node, other % self.n_node)

    def next_node(self, step):
        return (self.node + step + self.n_node) % self.n_node

    def at_node(self, step):
        return (self.box, self.next_node(step))

    def at_box(self, step):
        return ((self.box + step + self.n_box) % self.n_box, self.node)

    def mate(self):
        return (self.box ^ 1, self.node)

    def at_chip(self, step):
        x_bits = self.n_node.bit_length() - 1
        z_bits = self.nz.bit_length() - 1
        x = (self.node + step) & (self.n_node - 1)
        z = (self.z + (step >> x_bits)) & (self.nz - 1)
        y = (self.y + (step >> x_bits + z_bits)) & (self.ny - 1)
        return ((y * self.nz + z) * self.nc + self.core, x)

    def before_chip(self, step):
        x_bits = self.n_node.bit_length() - 1
        z_bits = self.nz.bit_length() - 1
        x = (self.node - (step & self.n_node - 1)) & (self.n_node - 1)
        z = (self.z - (step >> x_bits & self.nz - 1)) & (self.nz - 1)
        y = (self.y - (step >> x_bits + z_bits)) & (self.ny - 1)
        return ((y * self.nz + z) * self.nc + self.core, x)

    def peers_node(self):
        for step in range(1, self.n_node):
            yield self.next_node(step), self.at_node(step)

    def greet(self, more):
        peers = [self.along_line(1), self.along_line(-1)] + more
        peers += [device for _, device in self.peers_node()]
        peers.append(self.mate())
        barrier = pltpu.get_barrier_semaphore()
        for device in peers:
            pl.semaphore_signal(barrier, inc=1, device_id=device, device_id_type=MESH)

        def chip(step, carry):
            pl.semaphore_signal(
                barrier, inc=1, device_id=self.at_chip(step), device_id_type=MESH
            )
            return carry

        lax.fori_loop(1, self.chips, chip, 0)
        self.peer_count = len(peers) + self.chips - 1

    def greeted(self):
        pl.semaphore_wait(pltpu.get_barrier_semaphore(), self.peer_count)


class Swap:
    def __init__(self, here, yz_ref, x_ref, boxes, step, send_sems, recv_sems):
        self.here, self.refs, self.boxes, self.step = here, (yz_ref, x_ref), boxes, step
        self.send_sems, self.recv_sems = send_sems, recv_sems

    def copies(self, chunk):
        made = []
        for number in range(4):
            ref, later = self.refs[number // 2], 2 * (number % 2)
            at = chunk * self.step
            made.append(
                pltpu.make_async_remote_copy(
                    src_ref=ref.at[pl.ds(self.boxes + at, self.step)],
                    dst_ref=ref.at[pl.ds(later * self.boxes + at, self.step)],
                    send_sem=self.send_sems.at[chunk, number],
                    recv_sem=self.recv_sems.at[chunk, number],
                    device_id=self.here.along_line(1 - later),
                    device_id_type=MESH,
                )
            )
        return made

    def start(self, chunk):
        for copy in self.copies(chunk):
            copy.start()

    def arrived(self):
        for chunk in range(self.boxes // self.step):
            for copy in self.copies(chunk):
                copy.wait_recv()

    def finish(self):
        for chunk in range(self.boxes // self.step):
            for copy in self.copies(chunk):
                copy.wait_send()


def by_chunks(boxes, swap, one):
    step = min(boxes, 2)

    def some(chunk, carry):
        for number in range(step):
            one(chunk * step + number, 0)
        if swap is not None:
            swap.start(chunk)
        return carry

    lax.fori_loop(0, boxes // step, some, 0)


class Spread:
    def __init__(self, here, source, target, device, send_sems, recv_sems):
        self.here, self.source, self.target, self.device = here, source, target, device
        self.send_sems, self.recv_sems = send_sems, recv_sems

    def copy(self, step):
        return pltpu.make_async_remote_copy(
            src_ref=self.source(step),
            dst_ref=self.target(step),
            send_sem=self.send_sems.at[step],
            recv_sem=self.recv_sems.at[step],
            device_id=self.device(step),
            device_id_type=MESH,
        )

    def each(self, act):
        def one(step, carry):
            act(self.copy(step))
            return carry

        lax.fori_loop(1, self.here.chips, one, 0)

    def start(self):
        self.each(lambda copy: copy.start())

    def arrived(self):
        self.each(lambda copy: copy.wait_recv())

    def finish(self):
        self.each(lambda copy: copy.wait_send())


def write_tiles(ref, box, tiles):
    for t in range(TILES):
        ref[box, :, 128 * t : 128 * (t + 1)] = tiles[t]


def first_sweep(boxes, u_ref, b_ref, d_ref, c_ref, swap, ready=None):
    def one(box, carry):
        if ready is not None:
            ready(box)
        scales, tiles = [], []
        for t in range(TILES):
            cut = slice(128 * t, 128 * (t + 1))
            scales.append(0.8 / (6.0 + d_ref[box, :, cut]))
            tiles.append(scales[t] * b_ref[box, :, cut])
        write_tiles(c_ref, box, scales)
        write_tiles(u_ref, box, tiles)
        put_faces(tiles, *swap.refs, boxes + box)

    by_chunks(boxes, swap, one)


def sweep_boxes(boxes, u_ref, b_ref, c_ref, came, nbr_ref, out_ref, swap, keep=None):
    yz_from, x_from = came.refs

    def one(box, carry):
        tiles = tiles_of(u_ref, box)
        sums = beside(tiles, ghosts_of(yz_from, x_from, nbr_ref, box))
        fresh = []
        for t in range(TILES):
            cut = slice(128 * t, 128 * (t + 1))
            fresh.append(
                0.2 * tiles[t] + c_ref[box, :, cut] * (b_ref[box, :, cut] + sums[t])
            )
        if keep is not None:
            kept = keep(box)
            fresh = [t * kept for t in fresh]
        write_tiles(out_ref, box, fresh)
        if swap is not None:
            put_faces(fresh, *swap.refs, boxes + box)

    by_chunks(boxes, swap, one)


def residual_boxes(boxes, u_ref, b_ref, d_ref, came, nbr_ref, r_ref, keep=None):
    yz_from, x_from = came.refs

    def one(box, carry):
        tiles = tiles_of(u_ref, box)
        sums = beside(tiles, ghosts_of(yz_from, x_from, nbr_ref, box))
        rests = []
        for t in range(TILES):
            cut = slice(128 * t, 128 * (t + 1))
            left = b_ref[box, :, cut] - ((6.0 + d_ref[box, :, cut]) * tiles[t] - sums[t])
            rests.append(left if keep is None else left * keep(box))
        for t in range(TILES):
            r_ref[pl.ds(pl.multiple_of(box * 32, 32), 32), 128 * t : 128 * (t + 1)] = rests[t]

    by_chunks(boxes, None, one)


def down_kernel(
    n_box,
    n_node,
    fine_b_in,
    fine_d_in,
    count_ref,
    fine_nbr,
    cover_ref,
    source_in,
    coarse_d_in,
    coarse_nbr,
    place_ref,
    bottom_d_in,
    fine_u,
    fine_c,
    coarse_u,
    coarse_b,
    coarse_c,
    reach,
    blocks_out,
    places_out,
    fine_b,
    fine_d,
    source_ref,
    coarse_d,
    bottom_d,
    u_first,
    yz_fine_0,
    x_fine_0,
    yz_fine_1,
    x_fine_1,
    slab_c,
    rest_ref,
    octants,
    placed,
    lifted,
    found_at,
    cu_first,
    yz_coarse_0,
    x_coarse_0,
    yz_coarse_1,
    x_coarse_1,
    blocks,
    places,
    send_sems,
    recv_sems,
    local_sem,
    fine_sems,
    input_sems,
    fine_sent,
    fine_came,
    coarse_sent,
    coarse_came,
    spread_sent,
    spread_came,
):
    here = Place(n_box, n_node)
    copies = Copies(send_sems, recv_sems)
    boxes = fine_b.shape[0]

    def fine_input(box, number):
        pair = ((fine_b_in, fine_b), (fine_d_in, fine_d))[number]
        return pltpu.make_async_copy(pair[0].at[box], pair[1].at[box], fine_sems.at[number, box])

    for box in range(boxes):
        fine_input(box, 0).start()
        fine_input(box, 1).start()
    inputs = [
        pltpu.make_async_copy(source, target, input_sems.at[number])
        for number, (source, target) in enumerate(
            ((bottom_d_in, bottom_d), (source_in, source_ref), (coarse_d_in, coarse_d))
        )
    ]
    for copy in inputs:
        copy.start()
    here.greet([here.at_box(1), here.at_box(-1), here.at_box(2), here.at_box(-2)])

    def ready(box):
        fine_input(box, 0).wait()
        fine_input(box, 1).wait()

    core = here.core
    places[core, 0] = jnp.full((1, 128), place_ref[0], I32)
    fine_swaps = [
        Swap(here, yz, x, boxes, 2, fine_sent.at[number], fine_came.at[number])
        for number, (yz, x) in enumerate(((yz_fine_0, x_fine_0), (yz_fine_1, x_fine_1)))
    ]
    coarse_swaps = [
        Swap(here, yz, x, 1, 1, coarse_sent.at[number], coarse_came.at[number])
        for number, (yz, x) in enumerate(((yz_coarse_0, x_coarse_0), (yz_coarse_1, x_coarse_1)))
    ]
    spreads = [
        Spread(
            here,
            lambda step, ref=ref: ref.at[core, 0],
            lambda step, ref=ref: ref.at[core, step],
            here.at_chip,
            spread_sent.at[number],
            spread_came.at[number],
        )
        for number, ref in enumerate((places, blocks))
    ]

    here.greeted()
    first_sweep(boxes, u_first, fine_b, fine_d, fine_c, fine_swaps[0], ready)

    rows_x, rows_y = bottom_d.shape[0], bottom_d.shape[1]
    inputs[0].wait()

    part_z = one_hot_of((256, 256), lambda r, l: r == ((l & 127) << 1) + (l >> 7))

    def scale_plane(x, carry):
        slab_c[x] = pick_right(0.8 / (6.0 + bottom_d[x]), part_z)
        return carry

    lax.fori_loop(0, rows_x, scale_plane, 0)
    own_x, own_y = pl.ds(HALO, rows_x), pl.ds(Y_HALO, rows_y)
    own_copy = pltpu.make_async_copy(slab_c, reach.at[own_x, own_y], local_sem)
    own_copy.start()
    sides_y = (pl.ds(0, Y_HALO), pl.ds(Y_HALO + rows_y, Y_HALO))
    halo_y = [
        copies.start(
            slab_c.at[:, pl.ds(rows_y - Y_HALO, Y_HALO)],
            reach.at[own_x, sides_y[0]],
            here.at_node(1),
        ),
        copies.start(
            slab_c.at[:, pl.ds(0, Y_HALO)],
            reach.at[own_x, sides_y[1]],
            here.at_node(-1),
        ),
    ]
    some = HALO - rows_x
    to_x = (
        (1, 0, rows_x, HALO - rows_x),
        (-1, 0, rows_x, HALO + rows_x),
        (2, rows_x - some, some, 0),
        (-2, 0, some, HALO + 2 * rows_x),
    )
    halo_x = [
        copies.start(
            slab_c.at[pl.ds(first, wide)],
            reach.at[pl.ds(target, wide), own_y],
            here.at_box(step),
        )
        for step, first, wide, target in to_x
    ]
    spreads[0].start()

    for target in range(8 * n_node):
        slot = jnp.int32(-1)
        for box in range(boxes):
            slot = jnp.where(cover_ref[0, box] == target, box, slot)
        found_at[target] = slot

    own_copy.wait()
    arrived(halo_y)
    for step, first, wide, target in to_x:
        for side in sides_y:
            halo_x.append(
                copies.start(
                    reach.at[pl.ds(HALO + first, wide), side],
                    reach.at[pl.ds(target, wide), side],
                    here.at_box(step),
                )
            )

    fine_swaps[0].arrived()
    sweep_boxes(
        boxes, u_first, fine_b, fine_c, fine_swaps[0], fine_nbr, fine_u, fine_swaps[1]
    )
    spreads[0].arrived()
    mate_places = copies.start(places.at[core], places.at[core], here.mate())
    fold_yz = one_hot_of(
        (1024, 256), lambda r, l: (r >> 6 == l >> 4) & ((r & 31) >> 1 == (l & 15))
    )
    fold_x = one_hot_of((16 * boxes, 32 * boxes), lambda r, l: l >> 1 == r)
    fine_swaps[1].arrived()
    live = count_ref[0, 0]
    residual_boxes(
        boxes,
        fine_u,
        fine_b,
        fine_d,
        fine_swaps[1],
        fine_nbr,
        rest_ref,
        lambda box: jnp.where(box < live, 1.0, 0.0).astype(F32),
    )
    cubes = pick_left(fold_x, pick_right(rest_ref[...], fold_yz)) * 0.5
    for box in range(boxes):
        octants[box] = cubes[16 * box : 16 * (box + 1)]

    def place_one(target, carry):
        slot = found_at[target]
        kept = jnp.where(slot >= 0, 1.0, 0.0).astype(F32)
        placed[target] = octants[jnp.maximum(slot, 0)] * kept
        return carry

    lax.fori_loop(0, 8 * n_node, place_one, 0)
    given = []
    for step, (other, device) in enumerate(here.peers_node()):
        given.append(
            copies.start(
                placed.at[pl.ds(pl.multiple_of(other * 8, 8), 8)], lifted.at[step], device
            )
        )
    spread = one_hot_of(
        (512, 512),
        lambda r, l: (r >> 8 == (l >> 4 & 1)) & ((r >> 4 & 15) == l >> 5) & ((r & 15) == (l & 15)),
    )
    inputs[1].wait()
    inputs[2].wait()
    arrived(given)
    total = placed[pl.ds(pl.multiple_of(here.node * 8, 8), 8)]
    for step in range(n_node - 1):
        total = total + lifted[step]
    pairs = jnp.concatenate(
        [jnp.concatenate([total[2 * k], total[2 * k + 1]], axis=1) for k in range(4)], axis=0
    )
    grown = pick_right(pairs, spread)
    for k in range(4):
        at_x, at_y = 16 * (k // 2), 512 * (k % 2)
        coarse_b[0, at_x : at_x + 16, at_y : at_y + 512] = (
            source_ref[0, at_x : at_x + 16, at_y : at_y + 512] + grown[16 * k : 16 * (k + 1)]
        )

    first_sweep(1, cu_first, coarse_b, coarse_d, coarse_c, coarse_swaps[0])
    coarse_swaps[0].arrived()
    sweep_boxes(
        1, cu_first, coarse_b, coarse_c, coarse_swaps[0], coarse_nbr, coarse_u, coarse_swaps[1]
    )
    fold_quarter = one_hot_of(
        (1024, 128), lambda r, l: (r >> 7 == (l >> 3 & 7)) & ((r >> 2 & 7) == ((l & 3) << 1) + (l >> 2 & 1))
    )
    coarse_swaps[1].arrived()
    residual_boxes(1, coarse_u, coarse_b, coarse_d, coarse_swaps[1], coarse_nbr, rest_ref)
    folded = pick_right(rest_ref[0:32], fold_quarter)
    early = pick_left(one_hot_of((8, 32), lambda r, l: l >> 2 == r), folded)
    late = pick_left(one_hot_of((8, 32), lambda r, l: l >> 2 == r + 4), folded)
    block = jnp.where(lanes_of((8, 128)) < 64, early, late) * 0.25
    blocks[core, 0] = block[0:4]

    spreads[1].start()
    arrived([mate_places])
    row = jnp.zeros((1, 128), I32)
    lane = lanes_of((1, 128))
    for number in range(n_box * n_node):
        row = jnp.where(lane == number, places[number // here.chips, number % here.chips], row)
    places_out[...] = row
    spreads[1].arrived()
    arrived([copies.start(blocks.at[core], blocks.at[core], here.mate())])
    blocks_out[...] = blocks[...]

    arrived(halo_x)
    copies.finish()
    for sent in fine_swaps + coarse_swaps + spreads:
        sent.finish()


def bottom_kernel(
    n_box, n_node, rows_x, rows_y, places, reach, blocks, out, scale, source, first, second, hits, sems
):
    deep, wide, long = reach.shape
    count = n_box * n_node
    per_side = long // 8
    side_bits = per_side.bit_length() - 1
    box, node = lax.axis_index("box"), lax.axis_index("node")
    at_x, at_y = box * rows_x - HALO, node * rows_y - Y_HALO
    fills = [
        pltpu.make_async_copy(
            reach.at[:, :, 128 * half : 128 * (half + 1)],
            scale.at[half, pl.ds(8, deep)],
            sems.at[half],
        )
        for half in range(2)
    ]
    for copy in fills:
        copy.start()
    zeros = jnp.zeros((wide, 128), F32)

    def clear(x, carry):
        for half in range(2):
            source[half, x] = zeros
            first[half, x] = zeros
        return carry

    lax.fori_loop(8, 8 + deep, clear, 0, unroll=2)
    out[...] = jnp.zeros(out.shape, F32)

    def where_is(number):
        place = places[0, number]
        return (
            (place >> 2 * side_bits << 3) - at_x,
            ((place >> side_bits & per_side - 1) << 3) - at_y,
            place & per_side - 1,
        )

    def look(number, found):
        x, y, _ = where_is(number)
        hits[found] = number
        hit = (x > -8) & (x < deep) & (y >= 0) & (y < wide)
        return found + hit.astype(I32)

    found = lax.fori_loop(0, count, look, jnp.int32(0), unroll=8)

    for copy in fills:
        copy.wait()

    def empty(x, carry):
        for half in range(2):
            scale[half, x] = zeros
        return carry

    lax.fori_loop(8, 8 + jnp.maximum(-at_x, 0), empty, 0)
    lax.fori_loop(8 + jnp.minimum(rows_x * n_box - at_x, deep), 8 + deep, empty, 0)

    def empty_rows(start):
        def one(x, carry):
            for half in range(2):
                scale[half, x, start : start + Y_HALO] = jnp.zeros((Y_HALO, 128), F32)
            return carry

        lax.fori_loop(8, 8 + deep, one, 0)

    pl.when(node == 0)(lambda: empty_rows(0))
    pl.when(node == n_node - 1)(lambda: empty_rows(Y_HALO + rows_y))

    lane, row = lanes_of((8, 128)), rows_of((8, 128))

    def fan_out(value, step):
        for bit in (1, 2, 4):
            value = jnp.where((row & bit) != 0, roll_lanes(value, step * bit), value)
        return value

    def put(at, carry):
        number = hits[at]
        x, y, z = where_is(number)
        block = blocks[number]
        kept = (lane >> 2) == z
        rows = pl.ds(pl.multiple_of(y, 8), 8)
        spots = [(half, x + ix + 8, rows) for half in range(2) for ix in range(8)]
        before = [source[spot] for spot in spots]
        first_before = [first[spot] for spot in spots]
        scales = [scale[spot] for spot in spots]
        fanned = [
            fan_out(jnp.broadcast_to(block[ix % 4 : ix % 4 + 1], (8, 128)), -8) for ix in range(8)
        ]
        fresh = []
        for half in range(2):
            for ix in range(8):
                shift = (z << 2) + 128 - 4 * half + 64 * (ix // 4) & 127
                fresh.append(jnp.where(kept, pltpu.roll(fanned[ix], shift, 1), 0.0))
        for number, spot in enumerate(spots):
            source[spot] = before[number] + fresh[number]
            first[spot] = first_before[number] + fresh[number] * scales[number]
        return carry

    lax.fori_loop(0, found, put, 0)

    refs = (first, second)
    eight = (8, 128)
    lane = lanes_of(eight)
    for sweep_no in range(HALO):
        left = HALO - 1 - sweep_no
        margin = (left + 3) // 4 * 4
        low = Y_HALO - margin
        here, there = refs[sweep_no % 2], refs[(sweep_no + 1) % 2]

        def plane(x, carry):
            fresh = []
            for at in range(low, low + rows_y + 2 * margin, 8):
                cut = slice(at, at + 8)
                mids = [here[half, x, cut, :] for half in range(2)]
                turned = (
                    jnp.where(lane == 0, 0.0, pltpu.roll(mids[1], 1, 1)),
                    jnp.where(lane == 127, 0.0, pltpu.roll(mids[0], 127, 1)),
                )
                for half in range(2):
                    around = here[half, x - 1, cut, :] + here[half, x + 1, cut, :]
                    around += here[half, x, at - 1 : at + 7, :] + here[half, x, at + 1 : at + 9, :]
                    around += mids[1 - half] + turned[half]
                    value = 0.2 * mids[half] + scale[half, x, cut, :] * (
                        source[half, x, cut, :] + around
                    )
                    fresh.append((half, cut, value))
            for half, cut, value in fresh:
                there[half, x, cut, :] = value
            return carry

        lax.fori_loop(8 + HALO - left, 8 + HALO + rows_x + left, plane, 0)
    solved = refs[HALO % 2]

    def take(at, carry):
        number = hits[at]
        x, y, z = where_is(number)

        @pl.when((x == HALO) & (y >= Y_HALO) & (y < Y_HALO + rows_y))
        def _():
            rows = pl.ds(pl.multiple_of(y, 8), 8)
            back = 128 - (z << 2)
            lines = []
            for ix in range(8):
                even, odd = [
                    pltpu.roll(
                        solved[half, 8 + HALO + ix, rows, :],
                        back + 4 * half + 64 * (ix // 4) & 127,
                        1,
                    )
                    for half in range(2)
                ]
                turned = fan_out(jnp.where((lane & 4) == 0, even, odd), 8)
                mine = jnp.where((lane >> 3) == row + 8 * (ix // 4), turned, 0.0)
                lines.append(jnp.sum(mine, axis=0, keepdims=True))
            for ix in range(4):
                out[number, ix : ix + 1] = lines[ix] + lines[ix + 4]

        return carry

    lax.fori_loop(0, found, take, 0)


def up_kernel(
    n_box,
    n_node,
    parts,
    fine_u,
    fine_c,
    fine_b,
    count_ref,
    fine_nbr,
    cover_ref,
    coarse_u,
    coarse_b,
    coarse_c,
    coarse_nbr,
    fine_out,
    coarse_out,
    from_core,
    sum_core,
    from_chips,
    own_block,
    cu_first,
    cu_second,
    yz_coarse_0,
    x_coarse_0,
    yz_coarse_1,
    x_coarse_1,
    octants,
    picked,
    u_first,
    u_second,
    yz_fine_0,
    x_fine_0,
    yz_fine_1,
    x_fine_1,
    send_sems,
    recv_sems,
    fine_sent,
    fine_came,
    coarse_sent,
    coarse_came,
    spread_sent,
    spread_came,
):
    here = Place(n_box, n_node)
    copies = Copies(send_sems, recv_sems)
    boxes = fine_u.shape[0]
    core = here.core
    fine_swaps = [
        Swap(here, yz, x, boxes, 2, fine_sent.at[number], fine_came.at[number])
        for number, (yz, x) in enumerate(((yz_fine_0, x_fine_0), (yz_fine_1, x_fine_1)))
    ]
    coarse_swaps = [
        Swap(here, yz, x, 1, 1, coarse_sent.at[number], coarse_came.at[number])
        for number, (yz, x) in enumerate(((yz_coarse_0, x_coarse_0), (yz_coarse_1, x_coarse_1)))
    ]
    here.greet([])
    here.greeted()

    arrived([copies.start(parts.at[1 - core], from_core, here.mate())])
    sum_core[...] = parts[core] + from_core[...]
    spread = Spread(
        here,
        lambda step: sum_core.at[step],
        lambda step: from_chips.at[step],
        here.before_chip,
        spread_sent,
        spread_came,
    )
    from_chips[0] = sum_core[0]
    spread.start()
    grow_quarter = one_hot_of(
        (128, 1024), lambda r, l: r == (l >> 7 << 3) + (l >> 3 & 3) + (l >> 2 & 1) * 4
    )
    spread.arrived()
    block = jnp.sum(from_chips[...], axis=0)
    own_block[0:4] = block
    own_block[4:8] = pltpu.roll(block, 64, 1)
    grown = pick_right(own_block[...], grow_quarter)
    grown = pick_left(one_hot_of((32, 8), lambda r, l: r >> 2 == l), grown)
    cu_first[0] = coarse_u[0] + grown
    put_faces(tiles_of(cu_first, 0), yz_coarse_0, x_coarse_0, 1)
    coarse_swaps[0].start(0)
    coarse_swaps[0].arrived()
    sweep_boxes(
        1, cu_first, coarse_b, coarse_c, coarse_swaps[0], coarse_nbr, cu_second, coarse_swaps[1]
    )
    split = one_hot_of(
        (512, 512),
        lambda r, l: (l >> 8 == (r >> 4 & 1)) & ((l >> 4 & 15) == r >> 5) & ((l & 15) == (r & 15)),
    )
    coarse_swaps[1].arrived()
    sweep_boxes(
        1, cu_second, coarse_b, coarse_c, coarse_swaps[1], coarse_nbr, coarse_out, None
    )

    quarters = jnp.concatenate(
        [
            coarse_out[0, 16 * (k // 2) : 16 * (k // 2) + 16, 512 * (k % 2) : 512 * (k % 2) + 512]
            for k in range(4)
        ],
        axis=0,
    )
    cubes = pick_right(quarters, split)
    base = pl.multiple_of(here.node * 8, 8)
    for k in range(8):
        octants[base + k] = cubes[16 * (k // 2) : 16 * (k // 2) + 16, 256 * (k % 2) : 256 * (k % 2) + 256]
    own = octants.at[pl.ds(base, 8)]
    waits = [copies.start(own, own, device) for _, device in here.peers_node()]
    grow_yz = one_hot_of(
        (256, 1024), lambda r, l: (l >> 6 == r >> 4) & ((l >> 1 & 15) == (r & 15))
    )
    grow_x = one_hot_of((32 * boxes, 16 * boxes), lambda r, l: r >> 1 == l)
    arrived(waits)
    for box in range(boxes):
        picked[16 * box : 16 * (box + 1)] = octants[cover_ref[0, box]]
    tall = pick_right(pick_left(grow_x, picked[...]), grow_yz)
    for box in range(boxes):
        u_first[box] = fine_u[box] + tall[32 * box : 32 * (box + 1)]

    def faces_of(box, carry):
        put_faces(tiles_of(u_first, box), yz_fine_0, x_fine_0, boxes + box)

    by_chunks(boxes, fine_swaps[0], faces_of)
    fine_swaps[0].arrived()
    sweep_boxes(
        boxes, u_first, fine_b, fine_c, fine_swaps[0], fine_nbr, u_second, fine_swaps[1]
    )
    fine_swaps[1].arrived()
    live = count_ref[0, 0]
    sweep_boxes(
        boxes,
        u_second,
        fine_b,
        fine_c,
        fine_swaps[1],
        fine_nbr,
        fine_out,
        None,
        lambda box: jnp.where(box < live, 1.0, 0.0).astype(F32),
    )
    copies.finish()
    for sent in fine_swaps + coarse_swaps + [spread]:
        sent.finish()


VMEM, SMEM, ANY = (
    pl.BlockSpec(memory_space=pltpu.VMEM),
    pl.BlockSpec(memory_space=pltpu.SMEM),
    pl.BlockSpec(memory_space=pl.ANY),
)


def shards(
    n_box,
    n_node,
    fine_rhs,
    fine_diag,
    fine_count,
    fine_nbr,
    fine_cover,
    coarse_source,
    coarse_diag,
    coarse_nbr,
    coarse_place,
    bottom_diag,
):
    boxes = fine_rhs.shape[0]
    ny, nz, nc = grid_of(n_box)
    rows_x, rows_y, long = bottom_diag.shape
    deep, wide = rows_x + 2 * HALO, rows_y + 2 * Y_HALO
    count = n_box * n_node

    def like(shape, kind=F32):
        return jax.ShapeDtypeStruct(shape, kind)

    fine, coarse = (boxes, 32, 1024), (1, 32, 1024)
    chips = ny * nz * n_node
    grid = (nc, chips)
    limit = 48 * 1024 * 1024
    fine_u, fine_c, coarse_u, coarse_b, coarse_c, reach, blocks, places = pl.pallas_call(
        functools.partial(down_kernel, n_box, n_node),
        out_shape=(
            like(fine),
            like(fine),
            like(coarse),
            like(coarse),
            like(coarse),
            like((deep, wide, long)),
            like(grid + (4, 128)),
            like((1, 128), I32),
        ),
        in_specs=[ANY, ANY, SMEM, SMEM, SMEM, ANY, ANY, SMEM, SMEM, ANY],
        out_specs=(VMEM, VMEM, VMEM, VMEM, VMEM, ANY, VMEM, VMEM),
        scratch_shapes=[
            pltpu.VMEM(fine, F32),
            pltpu.VMEM(fine, F32),
            pltpu.VMEM(coarse, F32),
            pltpu.VMEM(coarse, F32),
            pltpu.VMEM((rows_x, rows_y, long), F32),
            pltpu.VMEM(fine, F32),
            pltpu.VMEM((3 * boxes, 32, 128), F32),
            pltpu.VMEM((3 * boxes, 2, 1024), F32),
            pltpu.VMEM((3 * boxes, 32, 128), F32),
            pltpu.VMEM((3 * boxes, 2, 1024), F32),
            pltpu.VMEM((rows_x, rows_y, long), F32),
            pltpu.VMEM((32 * boxes, 1024), F32),
            pltpu.VMEM((boxes, 16, 256), F32),
            pltpu.VMEM((8 * n_node, 16, 256), F32),
            pltpu.VMEM((n_node - 1, 8, 16, 256), F32),
            pltpu.SMEM((8 * n_node,), I32),
            pltpu.VMEM(coarse, F32),
            pltpu.VMEM((3, 32, 128), F32),
            pltpu.VMEM((3, 2, 1024), F32),
            pltpu.VMEM((3, 32, 128), F32),
            pltpu.VMEM((3, 2, 1024), F32),
            pltpu.VMEM(grid + (4, 128), F32),
            pltpu.VMEM(grid + (1, 128), I32),
            pltpu.SemaphoreType.DMA((64,)),
            pltpu.SemaphoreType.DMA((64,)),
            pltpu.SemaphoreType.DMA,
            pltpu.SemaphoreType.DMA((2, boxes)),
            pltpu.SemaphoreType.DMA((3,)),
            pltpu.SemaphoreType.DMA((2, boxes // 2, 4)),
            pltpu.SemaphoreType.DMA((2, boxes // 2, 4)),
            pltpu.SemaphoreType.DMA((2, 1, 4)),
            pltpu.SemaphoreType.DMA((2, 1, 4)),
            pltpu.SemaphoreType.DMA((2, chips)),
            pltpu.SemaphoreType.DMA((2, chips)),
        ],
        compiler_params=pltpu.CompilerParams(
            collective_id=0, has_side_effects=True, vmem_limit_bytes=limit
        ),
        name="down",
    )(
        fine_rhs,
        fine_diag,
        fine_count,
        fine_nbr,
        fine_cover,
        coarse_source,
        coarse_diag,
        coarse_nbr,
        coarse_place,
        bottom_diag,
    )
    parts = pl.pallas_call(
        functools.partial(bottom_kernel, n_box, n_node, rows_x, rows_y),
        out_shape=like((count, 4, 128)),
        in_specs=[SMEM, ANY, VMEM],
        out_specs=VMEM,
        scratch_shapes=[
            pltpu.VMEM((2, deep + 16, wide, 128), F32),
            pltpu.VMEM((2, deep + 16, wide, 128), F32),
            pltpu.VMEM((2, deep + 16, wide, 128), F32),
            pltpu.VMEM((2, deep + 16, wide, 128), F32),
            pltpu.SMEM((count + 1,), I32),
            pltpu.SemaphoreType.DMA((2,)),
        ],
        compiler_params=pltpu.CompilerParams(vmem_limit_bytes=limit),
        name="bottom",
    )(places, reach, blocks.reshape(count, 4, 128))
    fine_out, coarse_out = pl.pallas_call(
        functools.partial(up_kernel, n_box, n_node),
        out_shape=(like(fine), like(coarse)),
        in_specs=[VMEM, VMEM, VMEM, VMEM, SMEM, SMEM, SMEM, VMEM, VMEM, VMEM, SMEM],
        out_specs=(VMEM, VMEM),
        scratch_shapes=[
            pltpu.VMEM((chips, 4, 128), F32),
            pltpu.VMEM((chips, 4, 128), F32),
            pltpu.VMEM((chips, 4, 128), F32),
            pltpu.VMEM((8, 128), F32),
            pltpu.VMEM(coarse, F32),
            pltpu.VMEM(coarse, F32),
            pltpu.VMEM((3, 32, 128), F32),
            pltpu.VMEM((3, 2, 1024), F32),
            pltpu.VMEM((3, 32, 128), F32),
            pltpu.VMEM((3, 2, 1024), F32),
            pltpu.VMEM((8 * n_node, 16, 256), F32),
            pltpu.VMEM((16 * boxes, 256), F32),
            pltpu.VMEM(fine, F32),
            pltpu.VMEM(fine, F32),
            pltpu.VMEM((3 * boxes, 32, 128), F32),
            pltpu.VMEM((3 * boxes, 2, 1024), F32),
            pltpu.VMEM((3 * boxes, 32, 128), F32),
            pltpu.VMEM((3 * boxes, 2, 1024), F32),
            pltpu.SemaphoreType.DMA((8,)),
            pltpu.SemaphoreType.DMA((8,)),
            pltpu.SemaphoreType.DMA((2, boxes // 2, 4)),
            pltpu.SemaphoreType.DMA((2, boxes // 2, 4)),
            pltpu.SemaphoreType.DMA((2, 1, 4)),
            pltpu.SemaphoreType.DMA((2, 1, 4)),
            pltpu.SemaphoreType.DMA((chips,)),
            pltpu.SemaphoreType.DMA((chips,)),
        ],
        compiler_params=pltpu.CompilerParams(
            collective_id=1, has_side_effects=True, vmem_limit_bytes=limit
        ),
        name="up",
    )(
        parts.reshape(grid + (4, 128)),
        fine_u,
        fine_c,
        fine_rhs,
        fine_count,
        fine_nbr,
        fine_cover,
        coarse_u,
        coarse_b,
        coarse_c,
        coarse_nbr,
    )
    return fine_out, coarse_out


def solution(mesh):
    n_box, n_node = mesh.shape["box"], mesh.shape["node"]
    return jax.shard_map(
        functools.partial(shards, n_box, n_node),
        mesh=mesh,
        in_specs=(
            P(("box", "node"), None, None),
            P(("box", "node"), None, None),
            P("box", "node"),
            P(("box", "node"), None),
            P("box", "node"),
            P(("box", "node"), None, None),
            P(("box", "node"), None, None),
            P(("box", "node"), None),
            P(("box", "node")),
            P("box", "node", None),
        ),
        out_specs=(P(("box", "node"), None, None), P(("box", "node"), None, None)),
        check_vma=False,
    )
```

```python
import functools

import jax
import jax.numpy as jnp
from jax import lax
from jax.experimental import pallas as pl
from jax.experimental.pallas import tpu as pltpu
from jax.sharding import PartitionSpec as P

F32, BF16, I32 = jnp.float32, jnp.bfloat16, jnp.int32
MESH = pl.DeviceIdType.MESH
BOT_ITERS = 12
HALO = BOT_ITERS - 1
Y_HALO = 16
AT_ONCE = 4
TILES = 8


def grid_of(n_box):
    return {32: (4, 4, 2), 8: (2, 2, 2)}[n_box]


def lanes_of(shape):
    return lax.broadcasted_iota(I32, shape, len(shape) - 1)


def rows_of(shape):
    return lax.broadcasted_iota(I32, shape, len(shape) - 2)


def thirds(a):
    high = a.astype(BF16)
    rest = a - high.astype(F32)
    middle = rest.astype(BF16)
    low = (rest - middle.astype(F32)).astype(BF16)
    return high, middle, low


def pick_right(a, one_hot):
    high, middle, low = [jnp.dot(t, one_hot, preferred_element_type=F32) for t in thirds(a)]
    return high + (middle + low)


def pick_left(one_hot, a):
    high, middle, low = [jnp.dot(one_hot, t, preferred_element_type=F32) for t in thirds(a)]
    return high + (middle + low)


def one_hot_of(shape, test):
    return jnp.where(test(rows_of(shape), lanes_of(shape)), 1.0, 0.0).astype(BF16)


def roll_lanes(a, shift):
    shift = shift % 128
    return a if shift == 0 else pltpu.roll(a, shift, 1)


def tiles_of(ref, box):
    return [ref[box, :, 128 * t : 128 * (t + 1)] for t in range(TILES)]


def pack_faces(tiles):
    lane = lanes_of((32, 128))
    within, quarter = lane & 31, lane >> 5
    first, last = tiles[0], tiles[-1]
    packed = jnp.where(
        quarter == 0,
        first,
        jnp.where(
            quarter == 1,
            jnp.where(within < 16, roll_lanes(first, 40), roll_lanes(first, 24)),
            jnp.where(
                quarter == 2,
                jnp.where(within < 16, roll_lanes(last, -24), roll_lanes(last, -40)),
                last,
            ),
        ),
    )
    for t in range(TILES):
        packed = jnp.where(within == t, roll_lanes(tiles[t], t), packed)
        packed = jnp.where(within == 31 - t, roll_lanes(tiles[t], -t), packed)
    return packed


def put_faces(tiles, yz_ref, x_ref, slot):
    yz_ref[slot] = pack_faces(tiles)
    for t in range(TILES):
        x_ref[slot, 0:1, 128 * t : 128 * (t + 1)] = tiles[t][0:1, :]
        x_ref[slot, 1:2, 128 * t : 128 * (t + 1)] = tiles[t][31:32, :]


def ghosts_of(yz_ref, x_ref, nbr_ref, box):
    def chosen(ref, face):
        which = nbr_ref[box, face]
        kept = jnp.where(which >= 0, 1.0, 0.0).astype(F32)
        return ref[jnp.maximum(which, 0)], kept

    def tile(face):
        value, kept = chosen(yz_ref, face)
        return value * kept

    x_low, low_kept = chosen(x_ref, 0)
    x_high, high_kept = chosen(x_ref, 1)
    return (
        x_low[1:2] * low_kept,
        x_high[0:1] * high_kept,
        tile(2),
        tile(3),
        tile(4),
        tile(5),
    )


def beside(tiles, ghosts):
    x_low, x_high, y_low, y_high, z_low, z_high = ghosts
    lane, row = lanes_of((32, 128)), rows_of((32, 128))
    within = lane & 31
    below = jnp.where(
        within < 8,
        roll_lanes(y_low, 56),
        jnp.where(within < 24, roll_lanes(y_low, 32), roll_lanes(y_low, 72)),
    )
    above = jnp.where(
        within < 8,
        roll_lanes(y_high, 56),
        jnp.where(within < 24, roll_lanes(y_high, 96), roll_lanes(y_high, 72)),
    )
    ups = [below] + [roll_lanes(t, 32) for t in tiles]
    downs = [roll_lanes(t, 96) for t in tiles] + [above]
    sums = []
    for t in range(TILES):
        cut = slice(128 * t, 128 * (t + 1))
        along_x = jnp.where(row == 0, x_low[:, cut], pltpu.roll(tiles[t], 1, 0)) + jnp.where(
            row == 31, x_high[:, cut], pltpu.roll(tiles[t], 31, 0)
        )
        along_y = jnp.where(lane < 32, ups[t], ups[t + 1]) + jnp.where(
            lane >= 96, downs[t + 1], downs[t]
        )
        along_z = jnp.where(
            within == 0, roll_lanes(z_low, t - 31), roll_lanes(tiles[t], 1)
        ) + jnp.where(within == 31, roll_lanes(z_high, 31 - t), roll_lanes(tiles[t], 127))
        sums.append(along_x + along_y + along_z)
    return sums


def fan_out(value, step):
    row = rows_of((8, 128))
    for bit in (1, 2, 4):
        value = jnp.where((row & bit) != 0, roll_lanes(value, step * bit), value)
    return value


def swap_eights(value):
    lane = lanes_of((8, 128))
    result = jnp.zeros((8, 128), F32)
    for b in range(8):
        spread = fan_out(jnp.broadcast_to(value[b : b + 1], (8, 128)), -8)
        result = jnp.where((lane >> 3) == b, roll_lanes(spread, 8 * b), result)
    return result


class Copies:
    def __init__(self, send_sems, recv_sems):
        self.send_sems, self.recv_sems, self.made = send_sems, recv_sems, []

    def start(self, source, target, device):
        number = len(self.made)
        copy = pltpu.make_async_remote_copy(
            src_ref=source,
            dst_ref=target,
            send_sem=self.send_sems.at[number],
            recv_sem=self.recv_sems.at[number],
            device_id=device,
            device_id_type=MESH,
        )
        copy.start()
        self.made.append(copy)
        return copy

    def finish(self):
        for copy in self.made:
            copy.wait_send()


def arrived(copies):
    for copy in copies:
        copy.wait_recv()


class Place:
    def __init__(self, n_box, n_node):
        self.n_box, self.n_node = n_box, n_node
        self.ny, self.nz, self.nc = grid_of(n_box)
        self.box, self.node = lax.axis_index("box"), lax.axis_index("node")
        self.chips = self.ny * self.nz * n_node
        self.core = self.box & 1
        self.z = (self.box >> 1) & (self.nz - 1)
        self.y = (self.box >> 1) >> (self.nz.bit_length() - 1)

    def along_line(self, step):
        total = self.n_box * self.n_node
        other = (self.box * self.n_node + self.node + step + total) % total
        return (other // self.n_node, other % self.n_node)

    def next_node(self, step):
        return (self.node + step + self.n_node) % self.n_node

    def at_node(self, step):
        return (self.box, self.next_node(step))

    def at_box(self, step):
        return ((self.box + step + self.n_box) % self.n_box, self.node)

    def mate(self):
        return (self.box ^ 1, self.node)

    def at_chip(self, step):
        x_bits = self.n_node.bit_length() - 1
        z_bits = self.nz.bit_length() - 1
        x = (self.node + step) & (self.n_node - 1)
        z = (self.z + (step >> x_bits)) & (self.nz - 1)
        y = (self.y + (step >> x_bits + z_bits)) & (self.ny - 1)
        return ((y * self.nz + z) * self.nc + self.core, x)

    def before_chip(self, step):
        x_bits = self.n_node.bit_length() - 1
        z_bits = self.nz.bit_length() - 1
        x = (self.node - (step & self.n_node - 1)) & (self.n_node - 1)
        z = (self.z - (step >> x_bits & self.nz - 1)) & (self.nz - 1)
        y = (self.y - (step >> x_bits + z_bits)) & (self.ny - 1)
        return ((y * self.nz + z) * self.nc + self.core, x)

    def peers_node(self):
        for step in range(1, self.n_node):
            yield self.next_node(step), self.at_node(step)

    def greet(self, more):
        peers = [self.along_line(1), self.along_line(-1)] + more
        peers += [device for _, device in self.peers_node()]
        peers.append(self.mate())
        barrier = pltpu.get_barrier_semaphore()
        for device in peers:
            pl.semaphore_signal(barrier, inc=1, device_id=device, device_id_type=MESH)

        def chip(step, carry):
            pl.semaphore_signal(
                barrier, inc=1, device_id=self.at_chip(step), device_id_type=MESH
            )
            return carry

        lax.fori_loop(1, self.chips, chip, 0)
        self.peer_count = len(peers) + self.chips - 1

    def greeted(self):
        pl.semaphore_wait(pltpu.get_barrier_semaphore(), self.peer_count)


class Swap:
    def __init__(self, here, yz_ref, x_ref, boxes, step, send_sems, recv_sems):
        self.here, self.refs, self.boxes, self.step = here, (yz_ref, x_ref), boxes, step
        self.send_sems, self.recv_sems = send_sems, recv_sems

    def copies(self, chunk):
        made = []
        for number in range(4):
            ref, later = self.refs[number // 2], 2 * (number % 2)
            at = chunk * self.step
            made.append(
                pltpu.make_async_remote_copy(
                    src_ref=ref.at[pl.ds(self.boxes + at, self.step)],
                    dst_ref=ref.at[pl.ds(later * self.boxes + at, self.step)],
                    send_sem=self.send_sems.at[chunk, number],
                    recv_sem=self.recv_sems.at[chunk, number],
                    device_id=self.here.along_line(1 - later),
                    device_id_type=MESH,
                )
            )
        return made

    def start(self, chunk):
        for copy in self.copies(chunk):
            copy.start()

    def arrived(self):
        for chunk in range(self.boxes // self.step):
            for copy in self.copies(chunk):
                copy.wait_recv()

    def finish(self):
        for chunk in range(self.boxes // self.step):
            for copy in self.copies(chunk):
                copy.wait_send()


def by_chunks(boxes, swap, one):
    step = min(boxes, 2)

    def some(chunk, carry):
        for number in range(step):
            one(chunk * step + number, 0)
        if swap is not None and swap.step == step:
            swap.start(chunk)
        return carry

    lax.fori_loop(0, boxes // step, some, 0)


class Spread:
    def __init__(self, here, source, target, device, send_sems, recv_sems):
        self.here, self.source, self.target, self.device = here, source, target, device
        self.send_sems, self.recv_sems = send_sems, recv_sems

    def copy(self, step):
        return pltpu.make_async_remote_copy(
            src_ref=self.source(step),
            dst_ref=self.target(step),
            send_sem=self.send_sems.at[step],
            recv_sem=self.recv_sems.at[step],
            device_id=self.device(step),
            device_id_type=MESH,
        )

    def each(self, act):
        def one(step, carry):
            act(self.copy(step))
            return carry

        lax.fori_loop(1, self.here.chips, one, 0)

    def start(self):
        self.each(lambda copy: copy.start())

    def arrived(self):
        self.each(lambda copy: copy.wait_recv())

    def finish(self):
        self.each(lambda copy: copy.wait_send())


def write_tiles(ref, box, tiles):
    for t in range(TILES):
        ref[box, :, 128 * t : 128 * (t + 1)] = tiles[t]


def first_sweep(boxes, u_ref, b_ref, d_ref, c_ref, swap, ready=None):
    def one(box, carry):
        if ready is not None:
            ready(box)
        scales, tiles = [], []
        for t in range(TILES):
            cut = slice(128 * t, 128 * (t + 1))
            scales.append(0.8 / (6.0 + d_ref[box, :, cut]))
            tiles.append(scales[t] * b_ref[box, :, cut])
        write_tiles(c_ref, box, scales)
        write_tiles(u_ref, box, tiles)
        put_faces(tiles, *swap.refs, boxes + box)

    by_chunks(boxes, swap, one)


def sweep_boxes(boxes, u_ref, b_ref, c_ref, came, nbr_ref, out_ref, swap, keep=None):
    yz_from, x_from = came.refs

    def one(box, carry):
        tiles = tiles_of(u_ref, box)
        sums = beside(tiles, ghosts_of(yz_from, x_from, nbr_ref, box))
        fresh = []
        for t in range(TILES):
            cut = slice(128 * t, 128 * (t + 1))
            fresh.append(
                0.2 * tiles[t] + c_ref[box, :, cut] * (b_ref[box, :, cut] + sums[t])
            )
        if keep is not None:
            kept = keep(box)
            fresh = [t * kept for t in fresh]
        write_tiles(out_ref, box, fresh)
        if swap is not None:
            put_faces(fresh, *swap.refs, boxes + box)

    by_chunks(boxes, swap, one)


def residual_boxes(boxes, u_ref, b_ref, d_ref, came, nbr_ref, r_ref, keep=None):
    yz_from, x_from = came.refs

    def one(box, carry):
        tiles = tiles_of(u_ref, box)
        sums = beside(tiles, ghosts_of(yz_from, x_from, nbr_ref, box))
        rests = []
        for t in range(TILES):
            cut = slice(128 * t, 128 * (t + 1))
            left = b_ref[box, :, cut] - ((6.0 + d_ref[box, :, cut]) * tiles[t] - sums[t])
            rests.append(left if keep is None else left * keep(box))
        for t in range(TILES):
            r_ref[pl.ds(pl.multiple_of(box * 32, 32), 32), 128 * t : 128 * (t + 1)] = rests[t]

    by_chunks(boxes, None, one)


def down_kernel(
    n_box,
    n_node,
    fine_b_in,
    fine_d_in,
    count_ref,
    nbr_in,
    cover_in,
    source_in,
    coarse_d_in,
    coarse_nbr_in,
    place_ref,
    bottom_d_in,
    fine_u_out,
    fine_c_out,
    coarse_u_out,
    coarse_b_out,
    coarse_c_out,
    reach,
    blocks_out,
    places_out,
    fine_u,
    fine_c,
    coarse_u,
    coarse_b,
    coarse_c,
    fine_nbr,
    cover_ref,
    coarse_nbr,
    fine_b,
    fine_d,
    source_ref,
    coarse_d,
    bottom_d,
    u_first,
    yz_fine_0,
    x_fine_0,
    yz_fine_1,
    x_fine_1,
    slab_c,
    rest_ref,
    octants,
    placed,
    lifted,
    found_at,
    cu_first,
    yz_coarse_0,
    x_coarse_0,
    yz_coarse_1,
    x_coarse_1,
    blocks,
    places,
    send_sems,
    recv_sems,
    local_sem,
    fine_sems,
    input_sems,
    output_sems,
    fine_sent,
    fine_came,
    coarse_sent,
    coarse_came,
    spread_sent,
    spread_came,
):
    here = Place(n_box, n_node)
    copies = Copies(send_sems, recv_sems)
    boxes = fine_b.shape[0]

    def fine_input(box, number):
        pair = ((fine_b_in, fine_b), (fine_d_in, fine_d))[number]
        return pltpu.make_async_copy(pair[0].at[box], pair[1].at[box], fine_sems.at[number, box])

    for box in range(boxes):
        fine_input(box, 0).start()
        fine_input(box, 1).start()
    inputs = [
        pltpu.make_async_copy(source, target, input_sems.at[number])
        for number, (source, target) in enumerate(
            (
                (bottom_d_in, bottom_d),
                (source_in, source_ref),
                (coarse_d_in, coarse_d),
                (nbr_in, fine_nbr),
                (cover_in, cover_ref),
                (coarse_nbr_in, coarse_nbr),
            )
        )
    ]
    for copy in inputs:
        copy.start()
    here.greet([here.at_box(1), here.at_box(-1), here.at_box(2), here.at_box(-2)])

    def keep(source, target, number):
        copy = pltpu.make_async_copy(source, target, output_sems.at[number])
        copy.start()
        return copy

    def ready(box):
        fine_input(box, 0).wait()
        fine_input(box, 1).wait()

    core = here.core
    places[core, 0] = jnp.full((1, 128), place_ref[0], I32)
    fine_swaps = [
        Swap(here, yz, x, boxes, step, fine_sent.at[number], fine_came.at[number])
        for number, (yz, x, step) in enumerate(
            ((yz_fine_0, x_fine_0, boxes), (yz_fine_1, x_fine_1, 2))
        )
    ]
    coarse_swaps = [
        Swap(here, yz, x, 1, 1, coarse_sent.at[number], coarse_came.at[number])
        for number, (yz, x) in enumerate(((yz_coarse_0, x_coarse_0), (yz_coarse_1, x_coarse_1)))
    ]
    spreads = [
        Spread(
            here,
            lambda step, ref=ref: ref.at[core, 0],
            lambda step, ref=ref: ref.at[core, step],
            here.at_chip,
            spread_sent.at[number],
            spread_came.at[number],
        )
        for number, ref in enumerate((places, blocks))
    ]

    first_sweep(boxes, u_first, fine_b, fine_d, fine_c, fine_swaps[0], ready)
    kept = [keep(fine_c, fine_c_out, 0)]
    rows_x, rows_y = bottom_d.shape[0], bottom_d.shape[1]
    inputs[0].wait()
    part_z = one_hot_of((256, 256), lambda r, l: r == ((l & 127) << 1) + (l >> 7))

    def scale_plane(x, carry):
        slab_c[x] = pick_right(0.8 / (6.0 + bottom_d[x]), part_z)
        return carry

    lax.fori_loop(0, rows_x, scale_plane, 0)
    here.greeted()
    fine_swaps[0].start(0)
    own_x, own_y = pl.ds(HALO, rows_x), pl.ds(Y_HALO, rows_y)
    own_copy = pltpu.make_async_copy(slab_c, reach.at[own_x, own_y], local_sem)
    own_copy.start()
    sides_y = (pl.ds(0, Y_HALO), pl.ds(Y_HALO + rows_y, Y_HALO))
    halo_y = [
        copies.start(
            slab_c.at[:, pl.ds(rows_y - Y_HALO, Y_HALO)],
            reach.at[own_x, sides_y[0]],
            here.at_node(1),
        ),
        copies.start(
            slab_c.at[:, pl.ds(0, Y_HALO)],
            reach.at[own_x, sides_y[1]],
            here.at_node(-1),
        ),
    ]
    some = HALO - rows_x
    to_x = (
        (1, 0, rows_x, HALO - rows_x),
        (-1, 0, rows_x, HALO + rows_x),
        (2, rows_x - some, some, 0),
        (-2, 0, some, HALO + 2 * rows_x),
    )
    halo_x = [
        copies.start(
            slab_c.at[pl.ds(first, wide)],
            reach.at[pl.ds(target, wide), own_y],
            here.at_box(step),
        )
        for step, first, wide, target in to_x
    ]
    spreads[0].start()

    for copy in inputs[1:]:
        copy.wait()
    for target in range(8 * n_node):
        slot = jnp.int32(-1)
        for box in range(boxes):
            slot = jnp.where(cover_ref[0, box] == target, box, slot)
        found_at[target] = slot

    own_copy.wait()
    arrived(halo_y)
    for step, first, wide, target in to_x:
        for side in sides_y:
            halo_x.append(
                copies.start(
                    reach.at[pl.ds(HALO + first, wide), side],
                    reach.at[pl.ds(target, wide), side],
                    here.at_box(step),
                )
            )

    fine_swaps[0].arrived()
    sweep_boxes(
        boxes, u_first, fine_b, fine_c, fine_swaps[0], fine_nbr, fine_u, fine_swaps[1]
    )
    kept.append(keep(fine_u, fine_u_out, 1))
    spreads[0].arrived()
    mate_places = copies.start(places.at[core], places.at[core], here.mate())
    fold_yz = one_hot_of(
        (1024, 256), lambda r, l: (r >> 6 == l >> 4) & ((r & 31) >> 1 == (l & 15))
    )
    fold_x = one_hot_of((16 * boxes, 32 * boxes), lambda r, l: l >> 1 == r)
    fine_swaps[1].arrived()
    live = count_ref[0, 0]
    residual_boxes(
        boxes,
        fine_u,
        fine_b,
        fine_d,
        fine_swaps[1],
        fine_nbr,
        rest_ref,
        lambda box: jnp.where(box < live, 1.0, 0.0).astype(F32),
    )
    cubes = pick_left(fold_x, pick_right(rest_ref[...], fold_yz)) * 0.5
    for box in range(boxes):
        octants[box] = cubes[16 * box : 16 * (box + 1)]

    def place_one(target, carry):
        slot = found_at[target]
        kept = jnp.where(slot >= 0, 1.0, 0.0).astype(F32)
        placed[target] = octants[jnp.maximum(slot, 0)] * kept
        return carry

    lax.fori_loop(0, 8 * n_node, place_one, 0)
    given = []
    for step, (other, device) in enumerate(here.peers_node()):
        given.append(
            copies.start(
                placed.at[pl.ds(pl.multiple_of(other * 8, 8), 8)], lifted.at[step], device
            )
        )
    spread = one_hot_of(
        (512, 512),
        lambda r, l: (r >> 8 == (l >> 4 & 1)) & ((r >> 4 & 15) == l >> 5) & ((r & 15) == (l & 15)),
    )
    arrived(given)
    total = placed[pl.ds(pl.multiple_of(here.node * 8, 8), 8)]
    for step in range(n_node - 1):
        total = total + lifted[step]
    pairs = jnp.concatenate(
        [jnp.concatenate([total[2 * k], total[2 * k + 1]], axis=1) for k in range(4)], axis=0
    )
    grown = pick_right(pairs, spread)
    for k in range(4):
        at_x, at_y = 16 * (k // 2), 512 * (k % 2)
        coarse_b[0, at_x : at_x + 16, at_y : at_y + 512] = (
            source_ref[0, at_x : at_x + 16, at_y : at_y + 512] + grown[16 * k : 16 * (k + 1)]
        )

    first_sweep(1, cu_first, coarse_b, coarse_d, coarse_c, coarse_swaps[0])
    kept += [keep(coarse_b, coarse_b_out, 2), keep(coarse_c, coarse_c_out, 3)]
    coarse_swaps[0].arrived()
    sweep_boxes(
        1, cu_first, coarse_b, coarse_c, coarse_swaps[0], coarse_nbr, coarse_u, coarse_swaps[1]
    )
    kept.append(keep(coarse_u, coarse_u_out, 4))
    fold_quarter = one_hot_of(
        (1024, 128), lambda r, l: (r >> 7 == (l >> 3 & 7)) & ((r >> 2 & 7) == ((l & 3) << 1) + (l >> 2 & 1))
    )
    coarse_swaps[1].arrived()
    residual_boxes(1, coarse_u, coarse_b, coarse_d, coarse_swaps[1], coarse_nbr, rest_ref)
    folded = pick_right(rest_ref[0:32], fold_quarter)
    folded = pick_left(one_hot_of((8, 32), lambda r, l: l >> 2 == r), folded) * 0.25
    block = swap_eights(folded)
    late = pltpu.roll(block, 64, 1)
    blocks[core, 0] = jnp.where(lanes_of((4, 128)) < 64, block[0:4], late[4:8])

    spreads[1].start()
    arrived([mate_places])
    row = jnp.zeros((1, 128), I32)
    lane = lanes_of((1, 128))
    for number in range(n_box * n_node):
        row = jnp.where(lane == number, places[number // here.chips, number % here.chips], row)
    places_out[...] = row
    spreads[1].arrived()
    arrived([copies.start(blocks.at[core], blocks.at[core], here.mate())])
    kept.append(keep(blocks, blocks_out, 5))
    arrived(halo_x)
    copies.finish()
    for copy in kept:
        copy.wait()
    for sent in fine_swaps + coarse_swaps + spreads:
        sent.finish()


def bottom_kernel(
    n_box, n_node, rows_x, rows_y, places, reach, blocks_in, out, blocks, scale, source, first, second, hits, sems
):
    deep, wide, long = reach.shape
    count = n_box * n_node
    per_side = long // 8
    side_bits = per_side.bit_length() - 1
    box, node = lax.axis_index("box"), lax.axis_index("node")
    at_x, at_y = box * rows_x - HALO, node * rows_y - Y_HALO
    fills = [
        pltpu.make_async_copy(
            reach.at[:, :, 128 * half : 128 * (half + 1)],
            scale.at[half, pl.ds(8, deep)],
            sems.at[half],
        )
        for half in range(2)
    ]
    fills.append(pltpu.make_async_copy(blocks_in, blocks, sems.at[2]))
    for copy in fills:
        copy.start()
    zeros = jnp.zeros((wide, 128), F32)

    def clear(x, carry):
        for half in range(2):
            source[half, x] = zeros
            first[half, x] = zeros
        return carry

    lax.fori_loop(8, 8 + deep, clear, 0, unroll=2)
    out[...] = jnp.zeros(out.shape, F32)

    def where_is(number):
        place = places[0, number]
        return (
            (place >> 2 * side_bits << 3) - at_x,
            ((place >> side_bits & per_side - 1) << 3) - at_y,
            place & per_side - 1,
        )

    def look(number, found):
        x, y, _ = where_is(number)
        hits[found] = number
        hit = (x > -8) & (x < deep) & (y >= 0) & (y < wide)
        return found + hit.astype(I32)

    found = lax.fori_loop(0, count, look, jnp.int32(0), unroll=8)

    for copy in fills:
        copy.wait()

    def empty(x, carry):
        for half in range(2):
            scale[half, x] = zeros
        return carry

    lax.fori_loop(8, 8 + jnp.maximum(-at_x, 0), empty, 0)
    lax.fori_loop(8 + jnp.minimum(rows_x * n_box - at_x, deep), 8 + deep, empty, 0)

    def empty_rows(start):
        def one(x, carry):
            for half in range(2):
                scale[half, x, start : start + Y_HALO] = jnp.zeros((Y_HALO, 128), F32)
            return carry

        lax.fori_loop(8, 8 + deep, one, 0)

    pl.when(node == 0)(lambda: empty_rows(0))
    pl.when(node == n_node - 1)(lambda: empty_rows(Y_HALO + rows_y))

    lane, row = lanes_of((8, 128)), rows_of((8, 128))

    def put(at, carry):
        number = hits[at]
        x, y, z = where_is(number)
        block = blocks[number]
        kept = (lane >> 2) == z
        rows = pl.ds(pl.multiple_of(y, 8), 8)
        spots = [(half, x + ix + 8, rows) for half in range(2) for ix in range(8)]
        before = [source[spot] for spot in spots]
        first_before = [first[spot] for spot in spots]
        scales = [scale[spot] for spot in spots]
        whole = jnp.concatenate([block, pltpu.roll(block, 64, 1)], axis=0)
        fresh = []
        for half in range(2):
            for ix in range(8):
                shift = (z << 2) + 128 - 4 * half - 8 * ix & 127
                fresh.append(jnp.where(kept, pltpu.roll(whole, shift, 1), 0.0))
        for number, spot in enumerate(spots):
            source[spot] = before[number] + fresh[number]
            first[spot] = first_before[number] + fresh[number] * scales[number]
        return carry

    lax.fori_loop(0, found, put, 0)

    refs = (first, second)
    eight = (8, 128)
    lane = lanes_of(eight)
    for sweep_no in range(HALO):
        left = HALO - 1 - sweep_no
        margin = (left + 3) // 4 * 4
        low = Y_HALO - margin
        here, there = refs[sweep_no % 2], refs[(sweep_no + 1) % 2]

        def planes(group, carry):
            fresh = []
            for number in range(AT_ONCE):
                x = 8 + HALO - left + AT_ONCE * group + number
                for at in range(low, low + rows_y + 2 * margin, 8):
                    cut = slice(at, at + 8)
                    mids = [here[half, x, cut, :] for half in range(2)]
                    turned = (
                        jnp.where(lane == 0, 0.0, pltpu.roll(mids[1], 1, 1)),
                        jnp.where(lane == 127, 0.0, pltpu.roll(mids[0], 127, 1)),
                    )
                    for half in range(2):
                        around = here[half, x - 1, cut, :] + here[half, x + 1, cut, :]
                        around += here[half, x, at - 1 : at + 7, :]
                        around += here[half, x, at + 1 : at + 9, :]
                        around += mids[1 - half] + turned[half]
                        value = 0.2 * mids[half] + scale[half, x, cut, :] * (
                            source[half, x, cut, :] + around
                        )
                        fresh.append((half, x, cut, value))
            for half, x, cut, value in fresh:
                there[half, x, cut, :] = value
            return carry

        lax.fori_loop(0, (rows_x + 2 * left + AT_ONCE - 1) // AT_ONCE, planes, 0)
    solved = refs[HALO % 2]

    def take(at, carry):
        number = hits[at]
        x, y, z = where_is(number)

        @pl.when((x == HALO) & (y >= Y_HALO) & (y < Y_HALO + rows_y))
        def _():
            rows = pl.ds(pl.multiple_of(y, 8), 8)
            back = 128 - (z << 2)
            gathered = jnp.zeros(eight, F32)
            for ix in range(8):
                for half in range(2):
                    turned = pltpu.roll(
                        solved[half, 8 + HALO + ix, rows, :], back + 4 * half + 8 * ix & 127, 1
                    )
                    gathered = jnp.where((lane >> 2) == 2 * ix + half, turned, gathered)
            late = pltpu.roll(gathered, 64, 1)
            out[number] = jnp.where(lanes_of((4, 128)) < 64, gathered[0:4], late[4:8])

        return carry

    lax.fori_loop(0, found, take, 0)


def up_kernel(
    n_box,
    n_node,
    parts_in,
    fine_u_in,
    fine_c_in,
    fine_b_in,
    count_ref,
    nbr_in,
    cover_in,
    coarse_u_in,
    coarse_b_in,
    coarse_c_in,
    coarse_nbr_in,
    fine_out,
    coarse_out,
    fine_u,
    fine_c,
    fine_b,
    fine_nbr,
    cover_ref,
    coarse_u,
    coarse_b,
    coarse_c,
    coarse_nbr,
    own_parts,
    input_sems,
    from_core,
    sum_core,
    from_chips,
    own_block,
    cu_first,
    cu_second,
    yz_coarse_0,
    x_coarse_0,
    yz_coarse_1,
    x_coarse_1,
    octants,
    picked,
    u_first,
    u_second,
    yz_fine_0,
    x_fine_0,
    yz_fine_1,
    x_fine_1,
    send_sems,
    recv_sems,
    fine_sent,
    fine_came,
    coarse_sent,
    coarse_came,
    spread_sent,
    spread_came,
):
    here = Place(n_box, n_node)
    copies = Copies(send_sems, recv_sems)
    boxes = fine_u.shape[0]
    core = here.core
    inputs = [
        pltpu.make_async_copy(source, target, input_sems.at[number])
        for number, (source, target) in enumerate(
            (
                (parts_in.at[core], own_parts),
                (coarse_u_in, coarse_u),
                (coarse_b_in, coarse_b),
                (coarse_c_in, coarse_c),
                (coarse_nbr_in, coarse_nbr),
                (nbr_in, fine_nbr),
                (cover_in, cover_ref),
                (fine_u_in, fine_u),
                (fine_c_in, fine_c),
                (fine_b_in, fine_b),
            )
        )
    ]
    for copy in inputs:
        copy.start()
    fine_swaps = [
        Swap(here, yz, x, boxes, 2, fine_sent.at[number], fine_came.at[number])
        for number, (yz, x) in enumerate(((yz_fine_0, x_fine_0), (yz_fine_1, x_fine_1)))
    ]
    coarse_swaps = [
        Swap(here, yz, x, 1, 1, coarse_sent.at[number], coarse_came.at[number])
        for number, (yz, x) in enumerate(((yz_coarse_0, x_coarse_0), (yz_coarse_1, x_coarse_1)))
    ]
    here.greet([])
    here.greeted()

    from_mate = copies.start(parts_in.at[1 - core], from_core, here.mate())
    for copy in inputs:
        copy.wait()
    arrived([from_mate])
    sum_core[...] = own_parts[...] + from_core[...]
    spread = Spread(
        here,
        lambda step: sum_core.at[step],
        lambda step: from_chips.at[step],
        here.before_chip,
        spread_sent,
        spread_came,
    )
    from_chips[0] = sum_core[0]
    spread.start()
    grow_quarter = one_hot_of(
        (128, 1024), lambda r, l: r == (l >> 7 << 3) + (l >> 3 & 3) + (l >> 2 & 1) * 4
    )
    spread.arrived()
    block = jnp.sum(from_chips[...], axis=0)
    own_block[0:4] = block
    own_block[4:8] = pltpu.roll(block, 64, 1)
    grown = pick_right(swap_eights(own_block[...]), grow_quarter)
    grown = pick_left(one_hot_of((32, 8), lambda r, l: r >> 2 == l), grown)
    cu_first[0] = coarse_u[0] + grown
    put_faces(tiles_of(cu_first, 0), yz_coarse_0, x_coarse_0, 1)
    coarse_swaps[0].start(0)
    coarse_swaps[0].arrived()
    sweep_boxes(
        1, cu_first, coarse_b, coarse_c, coarse_swaps[0], coarse_nbr, cu_second, coarse_swaps[1]
    )
    split = one_hot_of(
        (512, 512),
        lambda r, l: (l >> 8 == (r >> 4 & 1)) & ((l >> 4 & 15) == r >> 5) & ((l & 15) == (r & 15)),
    )
    coarse_swaps[1].arrived()
    sweep_boxes(
        1, cu_second, coarse_b, coarse_c, coarse_swaps[1], coarse_nbr, coarse_out, None
    )

    quarters = jnp.concatenate(
        [
            coarse_out[0, 16 * (k // 2) : 16 * (k // 2) + 16, 512 * (k % 2) : 512 * (k % 2) + 512]
            for k in range(4)
        ],
        axis=0,
    )
    cubes = pick_right(quarters, split)
    base = pl.multiple_of(here.node * 8, 8)
    for k in range(8):
        octants[base + k] = cubes[16 * (k // 2) : 16 * (k // 2) + 16, 256 * (k % 2) : 256 * (k % 2) + 256]
    own = octants.at[pl.ds(base, 8)]
    waits = [copies.start(own, own, device) for _, device in here.peers_node()]
    grow_yz = one_hot_of(
        (256, 1024), lambda r, l: (l >> 6 == r >> 4) & ((l >> 1 & 15) == (r & 15))
    )
    grow_x = one_hot_of((32 * boxes, 16 * boxes), lambda r, l: r >> 1 == l)
    arrived(waits)
    for box in range(boxes):
        picked[16 * box : 16 * (box + 1)] = octants[cover_ref[0, box]]
    tall = pick_right(pick_left(grow_x, picked[...]), grow_yz)
    for box in range(boxes):
        u_first[box] = fine_u[box] + tall[32 * box : 32 * (box + 1)]

    def faces_of(box, carry):
        put_faces(tiles_of(u_first, box), yz_fine_0, x_fine_0, boxes + box)

    by_chunks(boxes, fine_swaps[0], faces_of)
    fine_swaps[0].arrived()
    sweep_boxes(
        boxes, u_first, fine_b, fine_c, fine_swaps[0], fine_nbr, u_second, fine_swaps[1]
    )
    fine_swaps[1].arrived()
    live = count_ref[0, 0]
    sweep_boxes(
        boxes,
        u_second,
        fine_b,
        fine_c,
        fine_swaps[1],
        fine_nbr,
        fine_out,
        None,
        lambda box: jnp.where(box < live, 1.0, 0.0).astype(F32),
    )
    copies.finish()
    for sent in fine_swaps + coarse_swaps + [spread]:
        sent.finish()


VMEM, SMEM, ANY = (
    pl.BlockSpec(memory_space=pltpu.VMEM),
    pl.BlockSpec(memory_space=pltpu.SMEM),
    pl.BlockSpec(memory_space=pl.ANY),
)


def shards(
    n_box,
    n_node,
    fine_rhs,
    fine_diag,
    fine_count,
    fine_nbr,
    fine_cover,
    coarse_source,
    coarse_diag,
    coarse_nbr,
    coarse_place,
    bottom_diag,
):
    boxes = fine_rhs.shape[0]
    ny, nz, nc = grid_of(n_box)
    rows_x, rows_y, long = bottom_diag.shape
    deep, wide = rows_x + 2 * HALO, rows_y + 2 * Y_HALO
    count = n_box * n_node

    def like(shape, kind=F32):
        return jax.ShapeDtypeStruct(shape, kind)

    fine, coarse = (boxes, 32, 1024), (1, 32, 1024)
    chips = ny * nz * n_node
    grid = (nc, chips)
    limit = 62 * 1024 * 1024
    fine_u, fine_c, coarse_u, coarse_b, coarse_c, reach, blocks, places = pl.pallas_call(
        functools.partial(down_kernel, n_box, n_node),
        out_shape=(
            like(fine),
            like(fine),
            like(coarse),
            like(coarse),
            like(coarse),
            like((deep, wide, long)),
            like(grid + (4, 128)),
            like((1, 128), I32),
        ),
        in_specs=[ANY, ANY, SMEM, ANY, ANY, ANY, ANY, ANY, SMEM, ANY],
        out_specs=(ANY, ANY, ANY, ANY, ANY, ANY, ANY, VMEM),
        scratch_shapes=[
            pltpu.VMEM(fine, F32),
            pltpu.VMEM(fine, F32),
            pltpu.VMEM(coarse, F32),
            pltpu.VMEM(coarse, F32),
            pltpu.VMEM(coarse, F32),
            pltpu.SMEM((boxes, 6), I32),
            pltpu.SMEM((1, boxes), I32),
            pltpu.SMEM((1, 6), I32),
            pltpu.VMEM(fine, F32),
            pltpu.VMEM(fine, F32),
            pltpu.VMEM(coarse, F32),
            pltpu.VMEM(coarse, F32),
            pltpu.VMEM((rows_x, rows_y, long), F32),
            pltpu.VMEM(fine, F32),
            pltpu.VMEM((3 * boxes, 32, 128), F32),
            pltpu.VMEM((3 * boxes, 2, 1024), F32),
            pltpu.VMEM((3 * boxes, 32, 128), F32),
            pltpu.VMEM((3 * boxes, 2, 1024), F32),
            pltpu.VMEM((rows_x, rows_y, long), F32),
            pltpu.VMEM((32 * boxes, 1024), F32),
            pltpu.VMEM((boxes, 16, 256), F32),
            pltpu.VMEM((8 * n_node, 16, 256), F32),
            pltpu.VMEM((n_node - 1, 8, 16, 256), F32),
            pltpu.SMEM((8 * n_node,), I32),
            pltpu.VMEM(coarse, F32),
            pltpu.VMEM((3, 32, 128), F32),
            pltpu.VMEM((3, 2, 1024), F32),
            pltpu.VMEM((3, 32, 128), F32),
            pltpu.VMEM((3, 2, 1024), F32),
            pltpu.VMEM(grid + (4, 128), F32),
            pltpu.VMEM(grid + (1, 128), I32),
            pltpu.SemaphoreType.DMA((64,)),
            pltpu.SemaphoreType.DMA((64,)),
            pltpu.SemaphoreType.DMA,
            pltpu.SemaphoreType.DMA((2, boxes)),
            pltpu.SemaphoreType.DMA((6,)),
            pltpu.SemaphoreType.DMA((6,)),
            pltpu.SemaphoreType.DMA((2, boxes // 2, 4)),
            pltpu.SemaphoreType.DMA((2, boxes // 2, 4)),
            pltpu.SemaphoreType.DMA((2, 1, 4)),
            pltpu.SemaphoreType.DMA((2, 1, 4)),
            pltpu.SemaphoreType.DMA((2, chips)),
            pltpu.SemaphoreType.DMA((2, chips)),
        ],
        compiler_params=pltpu.CompilerParams(
            collective_id=0, has_side_effects=True, vmem_limit_bytes=limit
        ),
        name="down",
    )(
        fine_rhs,
        fine_diag,
        fine_count,
        fine_nbr,
        fine_cover,
        coarse_source,
        coarse_diag,
        coarse_nbr,
        coarse_place,
        bottom_diag,
    )
    parts = pl.pallas_call(
        functools.partial(bottom_kernel, n_box, n_node, rows_x, rows_y),
        out_shape=like((count, 4, 128)),
        in_specs=[SMEM, ANY, ANY],
        out_specs=VMEM,
        scratch_shapes=[
            pltpu.VMEM((count, 4, 128), F32),
            pltpu.VMEM((2, deep + 16, wide, 128), F32),
            pltpu.VMEM((2, deep + 16, wide, 128), F32),
            pltpu.VMEM((2, deep + 16, wide, 128), F32),
            pltpu.VMEM((2, deep + 16, wide, 128), F32),
            pltpu.SMEM((count + 1,), I32),
            pltpu.SemaphoreType.DMA((3,)),
        ],
        compiler_params=pltpu.CompilerParams(vmem_limit_bytes=limit),
        name="bottom",
    )(places, reach, blocks.reshape(count, 4, 128))
    fine_out, coarse_out = pl.pallas_call(
        functools.partial(up_kernel, n_box, n_node),
        out_shape=(like(fine), like(coarse)),
        in_specs=[ANY, ANY, ANY, ANY, SMEM, ANY, ANY, ANY, ANY, ANY, ANY],
        out_specs=(VMEM, VMEM),
        scratch_shapes=[
            pltpu.VMEM(fine, F32),
            pltpu.VMEM(fine, F32),
            pltpu.VMEM(fine, F32),
            pltpu.SMEM((boxes, 6), I32),
            pltpu.SMEM((1, boxes), I32),
            pltpu.VMEM(coarse, F32),
            pltpu.VMEM(coarse, F32),
            pltpu.VMEM(coarse, F32),
            pltpu.SMEM((1, 6), I32),
            pltpu.VMEM((chips, 4, 128), F32),
            pltpu.SemaphoreType.DMA((10,)),
            pltpu.VMEM((chips, 4, 128), F32),
            pltpu.VMEM((chips, 4, 128), F32),
            pltpu.VMEM((chips, 4, 128), F32),
            pltpu.VMEM((8, 128), F32),
            pltpu.VMEM(coarse, F32),
            pltpu.VMEM(coarse, F32),
            pltpu.VMEM((3, 32, 128), F32),
            pltpu.VMEM((3, 2, 1024), F32),
            pltpu.VMEM((3, 32, 128), F32),
            pltpu.VMEM((3, 2, 1024), F32),
            pltpu.VMEM((8 * n_node, 16, 256), F32),
            pltpu.VMEM((16 * boxes, 256), F32),
            pltpu.VMEM(fine, F32),
            pltpu.VMEM(fine, F32),
            pltpu.VMEM((3 * boxes, 32, 128), F32),
            pltpu.VMEM((3 * boxes, 2, 1024), F32),
            pltpu.VMEM((3 * boxes, 32, 128), F32),
            pltpu.VMEM((3 * boxes, 2, 1024), F32),
            pltpu.SemaphoreType.DMA((8,)),
            pltpu.SemaphoreType.DMA((8,)),
            pltpu.SemaphoreType.DMA((2, boxes // 2, 4)),
            pltpu.SemaphoreType.DMA((2, boxes // 2, 4)),
            pltpu.SemaphoreType.DMA((2, 1, 4)),
            pltpu.SemaphoreType.DMA((2, 1, 4)),
            pltpu.SemaphoreType.DMA((chips,)),
            pltpu.SemaphoreType.DMA((chips,)),
        ],
        compiler_params=pltpu.CompilerParams(
            collective_id=1, has_side_effects=True, vmem_limit_bytes=limit
        ),
        name="up",
    )(
        parts.reshape(grid + (4, 128)),
        fine_u,
        fine_c,
        fine_rhs,
        fine_count,
        fine_nbr,
        fine_cover,
        coarse_u,
        coarse_b,
        coarse_c,
        coarse_nbr,
    )
    return fine_out, coarse_out


def solution(mesh):
    n_box, n_node = mesh.shape["box"], mesh.shape["node"]
    return jax.shard_map(
        functools.partial(shards, n_box, n_node),
        mesh=mesh,
        in_specs=(
            P(("box", "node"), None, None),
            P(("box", "node"), None, None),
            P("box", "node"),
            P(("box", "node"), None),
            P("box", "node"),
            P(("box", "node"), None, None),
            P(("box", "node"), None, None),
            P(("box", "node"), None),
            P(("box", "node")),
            P("box", "node", None),
        ),
        out_specs=(P(("box", "node"), None, None), P(("box", "node"), None, None)),
        check_vma=False,
    )
```

```python
import functools

import jax
import jax.numpy as jnp
from jax import lax
from jax.experimental import pallas as pl
from jax.experimental.pallas import tpu as pltpu
from jax.sharding import PartitionSpec as P

F32, BF16, I32 = jnp.float32, jnp.bfloat16, jnp.int32
MESH = pl.DeviceIdType.MESH
BOT_ITERS = 12
HALO = BOT_ITERS - 1
Y_HALO = 16
AT_ONCE = 4
TILES = 8


def grid_of(n_box):
    return {32: (4, 4, 2), 8: (2, 2, 2)}[n_box]


def lanes_of(shape):
    return lax.broadcasted_iota(I32, shape, len(shape) - 1)


def rows_of(shape):
    return lax.broadcasted_iota(I32, shape, len(shape) - 2)


def thirds(a):
    high = a.astype(BF16)
    rest = a - high.astype(F32)
    middle = rest.astype(BF16)
    low = (rest - middle.astype(F32)).astype(BF16)
    return high, middle, low


def pick_right(a, one_hot):
    high, middle, low = [jnp.dot(t, one_hot, preferred_element_type=F32) for t in thirds(a)]
    return high + (middle + low)


def pick_left(one_hot, a):
    high, middle, low = [jnp.dot(one_hot, t, preferred_element_type=F32) for t in thirds(a)]
    return high + (middle + low)


def one_hot_of(shape, test):
    return jnp.where(test(rows_of(shape), lanes_of(shape)), 1.0, 0.0).astype(BF16)


def roll_lanes(a, shift):
    shift = shift % 128
    return a if shift == 0 else pltpu.roll(a, shift, 1)


def tiles_of(ref, box):
    return [ref[box, :, 128 * t : 128 * (t + 1)] for t in range(TILES)]


def pack_faces(tiles):
    lane = lanes_of((32, 128))
    within, quarter = lane & 31, lane >> 5
    first, last = tiles[0], tiles[-1]
    packed = jnp.where(
        quarter == 0,
        first,
        jnp.where(
            quarter == 1,
            roll_lanes(first, 48),
            jnp.where(quarter == 2, roll_lanes(last, -16), last),
        ),
    )
    for t in range(TILES):
        packed = jnp.where((within >> 1) == t, roll_lanes(tiles[t], 2 * t + 1), packed)
    return packed


def put_faces(tiles, yz_ref, x_ref, slot):
    yz_ref[slot] = pack_faces(tiles)
    for t in range(TILES):
        x_ref[slot, 0:1, 128 * t : 128 * (t + 1)] = tiles[t][0:1, :]
        x_ref[slot, 1:2, 128 * t : 128 * (t + 1)] = tiles[t][31:32, :]


def ghosts_of(yz_ref, x_ref, nbr_ref, box):
    def chosen(ref, face):
        which = nbr_ref[box, face]
        kept = jnp.where(which >= 0, 1.0, 0.0).astype(F32)
        return ref[jnp.maximum(which, 0)], kept

    def tile(face):
        value, kept = chosen(yz_ref, face)
        return value * kept

    x_low, low_kept = chosen(x_ref, 0)
    x_high, high_kept = chosen(x_ref, 1)
    return (
        x_low[1:2] * low_kept,
        x_high[0:1] * high_kept,
        tile(2),
        tile(3),
        tile(4),
        tile(5),
    )


def beside_inside(tiles):
    lane, row = lanes_of((32, 128)), rows_of((32, 128))
    within = lane & 31
    nothing = jnp.zeros((32, 128), F32)
    ups = [nothing] + [roll_lanes(t, 32) for t in tiles]
    downs = [roll_lanes(t, 96) for t in tiles] + [nothing]
    sums = []
    for t in range(TILES):
        along_x = jnp.where(row == 0, 0.0, pltpu.roll(tiles[t], 1, 0)) + jnp.where(
            row == 31, 0.0, pltpu.roll(tiles[t], 31, 0)
        )
        along_y = jnp.where(lane < 32, ups[t], ups[t + 1]) + jnp.where(
            lane >= 96, downs[t + 1], downs[t]
        )
        along_z = jnp.where(within == 0, 0.0, roll_lanes(tiles[t], 1)) + jnp.where(
            within == 31, 0.0, roll_lanes(tiles[t], 127)
        )
        sums.append(along_x + along_y + along_z)
    return sums


def with_ghosts(sums, ghosts):
    x_low, x_high, y_low, y_high, z_low, z_high = ghosts
    lane, row = lanes_of((32, 128)), rows_of((8, 128))
    within = lane & 31
    below = jnp.where(within < 16, roll_lanes(y_low, 48), roll_lanes(y_low, 32))
    above = jnp.where(within < 16, roll_lanes(y_high, 48), roll_lanes(y_high, 96))
    both = jnp.where((lane & 1) == 0, z_low, roll_lanes(z_high, 62))
    edge = (within == 0) | (within == 31)
    full = []
    for t in range(TILES):
        cut = slice(128 * t, 128 * (t + 1))
        value = sums[t] + jnp.where(edge, roll_lanes(both, -32 - 2 * t), 0.0)
        if t == 0:
            value += jnp.where(lane < 32, below, 0.0)
        if t == TILES - 1:
            value += jnp.where(lane >= 96, above, 0.0)
        full.append(
            jnp.concatenate(
                [
                    value[0:8] + jnp.where(row == 0, x_low[:, cut], 0.0),
                    value[8:24],
                    value[24:32] + jnp.where(row == 7, x_high[:, cut], 0.0),
                ],
                axis=0,
            )
        )
    return full


def fan_out(value, step):
    row = rows_of((8, 128))
    for bit in (1, 2, 4):
        value = jnp.where((row & bit) != 0, roll_lanes(value, step * bit), value)
    return value


def swap_eights(value):
    lane = lanes_of((8, 128))
    result = jnp.zeros((8, 128), F32)
    for b in range(8):
        spread = fan_out(jnp.broadcast_to(value[b : b + 1], (8, 128)), -8)
        result = jnp.where((lane >> 3) == b, roll_lanes(spread, 8 * b), result)
    return result


class Copies:
    def __init__(self, send_sems, recv_sems):
        self.send_sems, self.recv_sems, self.made = send_sems, recv_sems, []

    def start(self, source, target, device):
        number = len(self.made)
        copy = pltpu.make_async_remote_copy(
            src_ref=source,
            dst_ref=target,
            send_sem=self.send_sems.at[number],
            recv_sem=self.recv_sems.at[number],
            device_id=device,
            device_id_type=MESH,
        )
        copy.start()
        self.made.append(copy)
        return copy

    def finish(self):
        for copy in self.made:
            copy.wait_send()


def arrived(copies):
    for copy in copies:
        copy.wait_recv()


class Place:
    def __init__(self, n_box, n_node):
        self.n_box, self.n_node = n_box, n_node
        self.ny, self.nz, self.nc = grid_of(n_box)
        self.box, self.node = lax.axis_index("box"), lax.axis_index("node")
        self.chips = self.ny * self.nz * n_node
        self.core = self.box & 1
        self.z = (self.box >> 1) & (self.nz - 1)
        self.y = (self.box >> 1) >> (self.nz.bit_length() - 1)

    def along_line(self, step):
        total = self.n_box * self.n_node
        other = (self.box * self.n_node + self.node + step + total) % total
        return (other // self.n_node, other % self.n_node)

    def next_node(self, step):
        return (self.node + step + self.n_node) % self.n_node

    def at_node(self, step):
        return (self.box, self.next_node(step))

    def at_box(self, step):
        return ((self.box + step + self.n_box) % self.n_box, self.node)

    def mate(self):
        return (self.box ^ 1, self.node)

    def at_chip(self, step):
        x_bits = self.n_node.bit_length() - 1
        z_bits = self.nz.bit_length() - 1
        x = (self.node + step) & (self.n_node - 1)
        z = (self.z + (step >> x_bits)) & (self.nz - 1)
        y = (self.y + (step >> x_bits + z_bits)) & (self.ny - 1)
        return ((y * self.nz + z) * self.nc + self.core, x)

    def before_chip(self, step):
        x_bits = self.n_node.bit_length() - 1
        z_bits = self.nz.bit_length() - 1
        x = (self.node - (step & self.n_node - 1)) & (self.n_node - 1)
        z = (self.z - (step >> x_bits & self.nz - 1)) & (self.nz - 1)
        y = (self.y - (step >> x_bits + z_bits)) & (self.ny - 1)
        return ((y * self.nz + z) * self.nc + self.core, x)

    def peers_node(self):
        for step in range(1, self.n_node):
            yield self.next_node(step), self.at_node(step)

    def greet(self, more):
        peers = [self.along_line(1), self.along_line(-1)] + more
        peers += [device for _, device in self.peers_node()]
        peers.append(self.mate())
        barrier = pltpu.get_barrier_semaphore()
        for device in peers:
            pl.semaphore_signal(barrier, inc=1, device_id=device, device_id_type=MESH)

        def chip(step, carry):
            pl.semaphore_signal(
                barrier, inc=1, device_id=self.at_chip(step), device_id_type=MESH
            )
            return carry

        lax.fori_loop(1, self.chips, chip, 0)
        self.peer_count = len(peers) + self.chips - 1

    def greeted(self):
        pl.semaphore_wait(pltpu.get_barrier_semaphore(), self.peer_count)


class Swap:
    def __init__(self, here, yz_ref, x_ref, boxes, step, send_sems, recv_sems):
        self.here, self.refs, self.boxes, self.step = here, (yz_ref, x_ref), boxes, step
        self.send_sems, self.recv_sems = send_sems, recv_sems

    def copies(self, chunk):
        made = []
        for number in range(4):
            ref, later = self.refs[number // 2], 2 * (number % 2)
            at = chunk * self.step
            made.append(
                pltpu.make_async_remote_copy(
                    src_ref=ref.at[pl.ds(self.boxes + at, self.step)],
                    dst_ref=ref.at[pl.ds(later * self.boxes + at, self.step)],
                    send_sem=self.send_sems.at[chunk, number],
                    recv_sem=self.recv_sems.at[chunk, number],
                    device_id=self.here.along_line(1 - later),
                    device_id_type=MESH,
                )
            )
        return made

    def start(self, chunk):
        for copy in self.copies(chunk):
            copy.start()

    def arrived(self):
        for chunk in range(self.boxes // self.step):
            for copy in self.copies(chunk):
                copy.wait_recv()

    def finish(self):
        for chunk in range(self.boxes // self.step):
            for copy in self.copies(chunk):
                copy.wait_send()


def by_chunks(boxes, swap, one):
    step = min(boxes, 2)

    def some(chunk, carry):
        for number in range(step):
            one(chunk * step + number, 0)
        if swap is not None and swap.step == step:
            swap.start(chunk)
        return carry

    lax.fori_loop(0, boxes // step, some, 0)


class Store:
    def __init__(self, source, target, boxes, step, sems):
        self.source, self.target, self.boxes, self.step = source, target, boxes, step
        self.sems = sems

    def copy(self, chunk):
        part = pl.ds(chunk * self.step, self.step)
        return pltpu.make_async_copy(
            self.source.at[part], self.target.at[part], self.sems.at[chunk]
        )

    def start(self, chunk):
        self.copy(chunk).start()

    def finish(self):
        for chunk in range(self.boxes // self.step):
            self.copy(chunk).wait()


class Spread:
    def __init__(self, here, source, target, device, send_sems, recv_sems):
        self.here, self.source, self.target, self.device = here, source, target, device
        self.send_sems, self.recv_sems = send_sems, recv_sems

    def copy(self, step):
        return pltpu.make_async_remote_copy(
            src_ref=self.source(step),
            dst_ref=self.target(step),
            send_sem=self.send_sems.at[step],
            recv_sem=self.recv_sems.at[step],
            device_id=self.device(step),
            device_id_type=MESH,
        )

    def each(self, act):
        def one(step, carry):
            act(self.copy(step))
            return carry

        lax.fori_loop(1, self.here.chips, one, 0)

    def start(self):
        self.each(lambda copy: copy.start())

    def arrived(self):
        self.each(lambda copy: copy.wait_recv())

    def finish(self):
        self.each(lambda copy: copy.wait_send())


def write_tiles(ref, box, tiles):
    for t in range(TILES):
        ref[box, :, 128 * t : 128 * (t + 1)] = tiles[t]


def first_sweep(boxes, u_ref, b_ref, d_ref, c_ref, swap, ready=None):
    def one(box, carry):
        if ready is not None:
            ready(box)
        scales, tiles = [], []
        for t in range(TILES):
            cut = slice(128 * t, 128 * (t + 1))
            scales.append(0.8 / (6.0 + d_ref[box, :, cut]))
            tiles.append(scales[t] * b_ref[box, :, cut])
        write_tiles(c_ref, box, scales)
        write_tiles(u_ref, box, tiles)
        put_faces(tiles, *swap.refs, boxes + box)

    by_chunks(boxes, swap, one)


def inside_boxes(boxes, u_ref, b_ref, sum_ref):
    def one(box, carry):
        tiles = tiles_of(u_ref, box)
        sums = beside_inside(tiles)
        sources = tiles_of(b_ref, box)
        write_tiles(sum_ref, box, [sources[t] + sums[t] for t in range(TILES)])

    by_chunks(boxes, None, one)


def sweep_boxes(
    boxes, u_ref, sum_ref, c_ref, came, nbr_ref, out_ref, swap, keep=None, store=None
):
    yz_from, x_from = came.refs

    def one(box, carry):
        tiles = tiles_of(u_ref, box)
        sums = with_ghosts(tiles_of(sum_ref, box), ghosts_of(yz_from, x_from, nbr_ref, box))
        fresh = []
        for t in range(TILES):
            cut = slice(128 * t, 128 * (t + 1))
            fresh.append(0.2 * tiles[t] + c_ref[box, :, cut] * sums[t])
        if keep is not None:
            kept = keep(box)
            fresh = [t * kept for t in fresh]
        write_tiles(out_ref, box, fresh)
        if swap is not None:
            put_faces(fresh, *swap.refs, boxes + box)

    by_chunks(boxes, store if swap is None else swap, one)


def residual_boxes(boxes, u_ref, sum_ref, d_ref, came, nbr_ref, r_ref, keep=None):
    yz_from, x_from = came.refs

    def one(box, carry):
        tiles = tiles_of(u_ref, box)
        sums = with_ghosts(tiles_of(sum_ref, box), ghosts_of(yz_from, x_from, nbr_ref, box))
        rests = []
        for t in range(TILES):
            cut = slice(128 * t, 128 * (t + 1))
            left = sums[t] - (6.0 + d_ref[box, :, cut]) * tiles[t]
            rests.append(left if keep is None else left * keep(box))
        for t in range(TILES):
            r_ref[pl.ds(pl.multiple_of(box * 32, 32), 32), 128 * t : 128 * (t + 1)] = rests[t]

    by_chunks(boxes, None, one)


def down_kernel(
    n_box,
    n_node,
    fine_b_in,
    fine_d_in,
    count_ref,
    nbr_in,
    cover_in,
    source_in,
    coarse_d_in,
    coarse_nbr_in,
    place_ref,
    bottom_d_in,
    fine_u_out,
    fine_c_out,
    coarse_u_out,
    coarse_b_out,
    coarse_c_out,
    reach,
    blocks_out,
    places_out,
    fine_u,
    fine_c,
    coarse_u,
    coarse_b,
    coarse_c,
    fine_nbr,
    cover_ref,
    coarse_nbr,
    fine_b,
    fine_d,
    source_ref,
    coarse_d,
    bottom_d,
    u_first,
    fine_sum,
    coarse_sum,
    yz_fine_0,
    x_fine_0,
    yz_fine_1,
    x_fine_1,
    slab_c,
    rest_ref,
    octants,
    placed,
    lifted,
    found_at,
    cu_first,
    yz_coarse_0,
    x_coarse_0,
    yz_coarse_1,
    x_coarse_1,
    blocks,
    places,
    send_sems,
    recv_sems,
    local_sem,
    fine_sems,
    input_sems,
    output_sems,
    fine_sent,
    fine_came,
    coarse_sent,
    coarse_came,
    spread_sent,
    spread_came,
):
    here = Place(n_box, n_node)
    copies = Copies(send_sems, recv_sems)
    boxes = fine_b.shape[0]

    def fine_input(box, number):
        pair = ((fine_b_in, fine_b), (fine_d_in, fine_d))[number]
        return pltpu.make_async_copy(pair[0].at[box], pair[1].at[box], fine_sems.at[number, box])

    for box in range(boxes):
        fine_input(box, 0).start()
        fine_input(box, 1).start()
    inputs = [
        pltpu.make_async_copy(source, target, input_sems.at[number])
        for number, (source, target) in enumerate(
            (
                (bottom_d_in, bottom_d),
                (source_in, source_ref),
                (coarse_d_in, coarse_d),
                (nbr_in, fine_nbr),
                (cover_in, cover_ref),
                (coarse_nbr_in, coarse_nbr),
            )
        )
    ]
    for copy in inputs:
        copy.start()
    here.greet([here.at_box(1), here.at_box(-1), here.at_box(2), here.at_box(-2)])

    def keep(source, target, number):
        copy = pltpu.make_async_copy(source, target, output_sems.at[number])
        copy.start()
        return copy

    def ready(box):
        fine_input(box, 0).wait()
        fine_input(box, 1).wait()

    core = here.core
    places[core, 0] = jnp.full((1, 128), place_ref[0], I32)
    fine_swaps = [
        Swap(here, yz, x, boxes, step, fine_sent.at[number], fine_came.at[number])
        for number, (yz, x, step) in enumerate(
            ((yz_fine_0, x_fine_0, boxes), (yz_fine_1, x_fine_1, 2))
        )
    ]
    coarse_swaps = [
        Swap(here, yz, x, 1, 1, coarse_sent.at[number], coarse_came.at[number])
        for number, (yz, x) in enumerate(((yz_coarse_0, x_coarse_0), (yz_coarse_1, x_coarse_1)))
    ]
    spreads = [
        Spread(
            here,
            lambda step, ref=ref: ref.at[core, 0],
            lambda step, ref=ref: ref.at[core, step],
            here.at_chip,
            spread_sent.at[number],
            spread_came.at[number],
        )
        for number, ref in enumerate((places, blocks))
    ]

    first_sweep(boxes, u_first, fine_b, fine_d, fine_c, fine_swaps[0], ready)
    kept = [keep(fine_c, fine_c_out, 0)]
    rows_x, rows_y = bottom_d.shape[0], bottom_d.shape[1]
    inputs[0].wait()
    part_z = one_hot_of((256, 256), lambda r, l: r == ((l & 127) << 1) + (l >> 7))

    def scale_plane(x, carry):
        slab_c[x] = pick_right(0.8 / (6.0 + bottom_d[x]), part_z)
        return carry

    lax.fori_loop(0, rows_x, scale_plane, 0)
    here.greeted()
    fine_swaps[0].start(0)
    own_x, own_y = pl.ds(HALO, rows_x), pl.ds(Y_HALO, rows_y)
    own_copy = pltpu.make_async_copy(slab_c, reach.at[own_x, own_y], local_sem)
    own_copy.start()
    sides_y = (pl.ds(0, Y_HALO), pl.ds(Y_HALO + rows_y, Y_HALO))
    halo_y = [
        copies.start(
            slab_c.at[:, pl.ds(rows_y - Y_HALO, Y_HALO)],
            reach.at[own_x, sides_y[0]],
            here.at_node(1),
        ),
        copies.start(
            slab_c.at[:, pl.ds(0, Y_HALO)],
            reach.at[own_x, sides_y[1]],
            here.at_node(-1),
        ),
    ]
    some = HALO - rows_x
    to_x = (
        (1, 0, rows_x, HALO - rows_x),
        (-1, 0, rows_x, HALO + rows_x),
        (2, rows_x - some, some, 0),
        (-2, 0, some, HALO + 2 * rows_x),
    )
    halo_x = [
        copies.start(
            slab_c.at[pl.ds(first, wide)],
            reach.at[pl.ds(target, wide), own_y],
            here.at_box(step),
        )
        for step, first, wide, target in to_x
    ]
    spreads[0].start()

    for copy in inputs[1:]:
        copy.wait()
    for target in range(8 * n_node):
        slot = jnp.int32(-1)
        for box in range(boxes):
            slot = jnp.where(cover_ref[0, box] == target, box, slot)
        found_at[target] = slot

    own_copy.wait()
    arrived(halo_y)
    for step, first, wide, target in to_x:
        for side in sides_y:
            halo_x.append(
                copies.start(
                    reach.at[pl.ds(HALO + first, wide), side],
                    reach.at[pl.ds(target, wide), side],
                    here.at_box(step),
                )
            )

    inside_boxes(boxes, u_first, fine_b, fine_sum)
    fine_swaps[0].arrived()
    sweep_boxes(
        boxes, u_first, fine_sum, fine_c, fine_swaps[0], fine_nbr, fine_u, fine_swaps[1]
    )
    kept.append(keep(fine_u, fine_u_out, 1))
    spreads[0].arrived()
    mate_places = copies.start(places.at[core], places.at[core], here.mate())
    fold_yz = one_hot_of(
        (1024, 256), lambda r, l: (r >> 6 == l >> 4) & ((r & 31) >> 1 == (l & 15))
    )
    fold_x = one_hot_of((16 * boxes, 32 * boxes), lambda r, l: l >> 1 == r)
    inside_boxes(boxes, fine_u, fine_b, fine_sum)
    fine_swaps[1].arrived()
    live = count_ref[0, 0]
    residual_boxes(
        boxes,
        fine_u,
        fine_sum,
        fine_d,
        fine_swaps[1],
        fine_nbr,
        rest_ref,
        lambda box: jnp.where(box < live, 1.0, 0.0).astype(F32),
    )
    cubes = pick_left(fold_x, pick_right(rest_ref[...], fold_yz)) * 0.5
    for box in range(boxes):
        octants[box] = cubes[16 * box : 16 * (box + 1)]

    def place_one(target, carry):
        slot = found_at[target]
        kept = jnp.where(slot >= 0, 1.0, 0.0).astype(F32)
        placed[target] = octants[jnp.maximum(slot, 0)] * kept
        return carry

    lax.fori_loop(0, 8 * n_node, place_one, 0)
    given = []
    for step, (other, device) in enumerate(here.peers_node()):
        given.append(
            copies.start(
                placed.at[pl.ds(pl.multiple_of(other * 8, 8), 8)], lifted.at[step], device
            )
        )
    spread = one_hot_of(
        (512, 512),
        lambda r, l: (r >> 8 == (l >> 4 & 1)) & ((r >> 4 & 15) == l >> 5) & ((r & 15) == (l & 15)),
    )
    arrived(given)
    total = placed[pl.ds(pl.multiple_of(here.node * 8, 8), 8)]
    for step in range(n_node - 1):
        total = total + lifted[step]
    pairs = jnp.concatenate(
        [jnp.concatenate([total[2 * k], total[2 * k + 1]], axis=1) for k in range(4)], axis=0
    )
    grown = pick_right(pairs, spread)
    for k in range(4):
        at_x, at_y = 16 * (k // 2), 512 * (k % 2)
        coarse_b[0, at_x : at_x + 16, at_y : at_y + 512] = (
            source_ref[0, at_x : at_x + 16, at_y : at_y + 512] + grown[16 * k : 16 * (k + 1)]
        )

    first_sweep(1, cu_first, coarse_b, coarse_d, coarse_c, coarse_swaps[0])
    kept += [keep(coarse_b, coarse_b_out, 2), keep(coarse_c, coarse_c_out, 3)]
    inside_boxes(1, cu_first, coarse_b, coarse_sum)
    coarse_swaps[0].arrived()
    sweep_boxes(
        1, cu_first, coarse_sum, coarse_c, coarse_swaps[0], coarse_nbr, coarse_u, coarse_swaps[1]
    )
    kept.append(keep(coarse_u, coarse_u_out, 4))
    fold_quarter = one_hot_of(
        (1024, 128), lambda r, l: (r >> 7 == (l >> 3 & 7)) & ((r >> 2 & 7) == ((l & 3) << 1) + (l >> 2 & 1))
    )
    inside_boxes(1, coarse_u, coarse_b, coarse_sum)
    coarse_swaps[1].arrived()
    residual_boxes(1, coarse_u, coarse_sum, coarse_d, coarse_swaps[1], coarse_nbr, rest_ref)
    folded = pick_right(rest_ref[0:32], fold_quarter)
    folded = pick_left(one_hot_of((8, 32), lambda r, l: l >> 2 == r), folded) * 0.25
    block = swap_eights(folded)
    late = pltpu.roll(block, 64, 1)
    blocks[core, 0] = jnp.where(lanes_of((4, 128)) < 64, block[0:4], late[4:8])

    spreads[1].start()
    arrived([mate_places])
    row = jnp.zeros((1, 128), I32)
    lane = lanes_of((1, 128))
    for number in range(n_box * n_node):
        row = jnp.where(lane == number, places[number // here.chips, number % here.chips], row)
    places_out[...] = row
    spreads[1].arrived()
    arrived([copies.start(blocks.at[core], blocks.at[core], here.mate())])
    kept.append(keep(blocks, blocks_out, 5))
    arrived(halo_x)
    copies.finish()
    for copy in kept:
        copy.wait()
    for sent in fine_swaps + coarse_swaps + spreads:
        sent.finish()


def bottom_kernel(
    n_box, n_node, rows_x, rows_y, places, reach, blocks_in, out, blocks, scale, source, first, second, hits, sems
):
    deep, wide, long = reach.shape
    count = n_box * n_node
    per_side = long // 8
    side_bits = per_side.bit_length() - 1
    box, node = lax.axis_index("box"), lax.axis_index("node")
    at_x, at_y = box * rows_x - HALO, node * rows_y - Y_HALO
    fills = [
        pltpu.make_async_copy(
            reach.at[:, :, 128 * half : 128 * (half + 1)],
            scale.at[half, pl.ds(8, deep)],
            sems.at[half],
        )
        for half in range(2)
    ]
    fills.append(pltpu.make_async_copy(blocks_in, blocks, sems.at[2]))
    for copy in fills:
        copy.start()
    zeros = jnp.zeros((wide, 128), F32)

    def clear(x, carry):
        for half in range(2):
            source[half, x] = zeros
            first[half, x] = zeros
        return carry

    lax.fori_loop(8, 8 + deep, clear, 0, unroll=2)
    out[...] = jnp.zeros(out.shape, F32)

    def where_is(number):
        place = places[0, number]
        return (
            (place >> 2 * side_bits << 3) - at_x,
            ((place >> side_bits & per_side - 1) << 3) - at_y,
            place & per_side - 1,
        )

    def look(number, found):
        x, y, _ = where_is(number)
        hits[found] = number
        hit = (x > -8) & (x < deep) & (y >= 0) & (y < wide)
        return found + hit.astype(I32)

    found = lax.fori_loop(0, count, look, jnp.int32(0), unroll=8)

    for copy in fills:
        copy.wait()

    def empty(x, carry):
        for half in range(2):
            scale[half, x] = zeros
        return carry

    lax.fori_loop(8, 8 + jnp.maximum(-at_x, 0), empty, 0)
    lax.fori_loop(8 + jnp.minimum(rows_x * n_box - at_x, deep), 8 + deep, empty, 0)

    def empty_rows(start):
        def one(x, carry):
            for half in range(2):
                scale[half, x, start : start + Y_HALO] = jnp.zeros((Y_HALO, 128), F32)
            return carry

        lax.fori_loop(8, 8 + deep, one, 0)

    pl.when(node == 0)(lambda: empty_rows(0))
    pl.when(node == n_node - 1)(lambda: empty_rows(Y_HALO + rows_y))

    lane, row = lanes_of((8, 128)), rows_of((8, 128))

    def put(at, carry):
        number = hits[at]
        x, y, z = where_is(number)
        block = blocks[number]
        kept = (lane >> 2) == z
        rows = pl.ds(pl.multiple_of(y, 8), 8)
        spots = [(half, x + ix + 8, rows) for half in range(2) for ix in range(8)]
        before = [source[spot] for spot in spots]
        first_before = [first[spot] for spot in spots]
        scales = [scale[spot] for spot in spots]
        whole = jnp.concatenate([block, pltpu.roll(block, 64, 1)], axis=0)
        fresh = []
        for half in range(2):
            for ix in range(8):
                shift = (z << 2) + 128 - 4 * half - 8 * ix & 127
                fresh.append(jnp.where(kept, pltpu.roll(whole, shift, 1), 0.0))
        for number, spot in enumerate(spots):
            source[spot] = before[number] + fresh[number]
            first[spot] = first_before[number] + fresh[number] * scales[number]
        return carry

    lax.fori_loop(0, found, put, 0)

    refs = (first, second)
    eight = (8, 128)
    lane = lanes_of(eight)
    for sweep_no in range(HALO):
        left = HALO - 1 - sweep_no
        margin = (left + 3) // 4 * 4
        low = Y_HALO - margin
        here, there = refs[sweep_no % 2], refs[(sweep_no + 1) % 2]

        def planes(group, carry):
            fresh = []
            for number in range(AT_ONCE):
                x = 8 + HALO - left + AT_ONCE * group + number
                for at in range(low, low + rows_y + 2 * margin, 8):
                    cut = slice(at, at + 8)
                    mids = [here[half, x, cut, :] for half in range(2)]
                    turned = (
                        jnp.where(lane == 0, 0.0, pltpu.roll(mids[1], 1, 1)),
                        jnp.where(lane == 127, 0.0, pltpu.roll(mids[0], 127, 1)),
                    )
                    for half in range(2):
                        around = here[half, x - 1, cut, :] + here[half, x + 1, cut, :]
                        around += here[half, x, at - 1 : at + 7, :]
                        around += here[half, x, at + 1 : at + 9, :]
                        around += mids[1 - half] + turned[half]
                        value = 0.2 * mids[half] + scale[half, x, cut, :] * (
                            source[half, x, cut, :] + around
                        )
                        fresh.append((half, x, cut, value))
            for half, x, cut, value in fresh:
                there[half, x, cut, :] = value
            return carry

        lax.fori_loop(0, (rows_x + 2 * left + AT_ONCE - 1) // AT_ONCE, planes, 0)
    solved = refs[HALO % 2]

    def take(at, carry):
        number = hits[at]
        x, y, z = where_is(number)

        @pl.when((x == HALO) & (y >= Y_HALO) & (y < Y_HALO + rows_y))
        def _():
            rows = pl.ds(pl.multiple_of(y, 8), 8)
            back = 128 - (z << 2)
            gathered = jnp.zeros(eight, F32)
            for ix in range(8):
                for half in range(2):
                    turned = pltpu.roll(
                        solved[half, 8 + HALO + ix, rows, :], back + 4 * half + 8 * ix & 127, 1
                    )
                    gathered = jnp.where((lane >> 2) == 2 * ix + half, turned, gathered)
            late = pltpu.roll(gathered, 64, 1)
            out[number] = jnp.where(lanes_of((4, 128)) < 64, gathered[0:4], late[4:8])

        return carry

    lax.fori_loop(0, found, take, 0)


def up_kernel(
    n_box,
    n_node,
    parts_in,
    fine_u_in,
    fine_c_in,
    fine_b_in,
    count_ref,
    nbr_in,
    cover_in,
    coarse_u_in,
    coarse_b_in,
    coarse_c_in,
    coarse_nbr_in,
    fine_to,
    coarse_to,
    fine_out,
    coarse_out,
    output_sems,
    fine_u,
    fine_c,
    fine_b,
    fine_nbr,
    cover_ref,
    coarse_u,
    coarse_b,
    coarse_c,
    coarse_nbr,
    own_parts,
    input_sems,
    from_core,
    sum_core,
    from_chips,
    own_block,
    cu_first,
    cu_second,
    yz_coarse_0,
    x_coarse_0,
    yz_coarse_1,
    x_coarse_1,
    octants,
    picked,
    u_first,
    u_second,
    fine_sum,
    coarse_sum,
    yz_fine_0,
    x_fine_0,
    yz_fine_1,
    x_fine_1,
    send_sems,
    recv_sems,
    fine_sent,
    fine_came,
    coarse_sent,
    coarse_came,
    spread_sent,
    spread_came,
):
    here = Place(n_box, n_node)
    copies = Copies(send_sems, recv_sems)
    boxes = fine_u.shape[0]
    core = here.core
    inputs = [
        pltpu.make_async_copy(source, target, input_sems.at[number])
        for number, (source, target) in enumerate(
            (
                (parts_in.at[core], own_parts),
                (coarse_u_in, coarse_u),
                (coarse_b_in, coarse_b),
                (coarse_c_in, coarse_c),
                (coarse_nbr_in, coarse_nbr),
                (nbr_in, fine_nbr),
                (cover_in, cover_ref),
                (fine_u_in, fine_u),
                (fine_c_in, fine_c),
                (fine_b_in, fine_b),
            )
        )
    ]
    for copy in inputs:
        copy.start()
    fine_swaps = [
        Swap(here, yz, x, boxes, 2, fine_sent.at[number], fine_came.at[number])
        for number, (yz, x) in enumerate(((yz_fine_0, x_fine_0), (yz_fine_1, x_fine_1)))
    ]
    coarse_swaps = [
        Swap(here, yz, x, 1, 1, coarse_sent.at[number], coarse_came.at[number])
        for number, (yz, x) in enumerate(((yz_coarse_0, x_coarse_0), (yz_coarse_1, x_coarse_1)))
    ]
    here.greet([])
    here.greeted()

    from_mate = copies.start(parts_in.at[1 - core], from_core, here.mate())
    for copy in inputs:
        copy.wait()
    arrived([from_mate])
    sum_core[...] = own_parts[...] + from_core[...]
    spread = Spread(
        here,
        lambda step: sum_core.at[step],
        lambda step: from_chips.at[step],
        here.before_chip,
        spread_sent,
        spread_came,
    )
    from_chips[0] = sum_core[0]
    spread.start()
    grow_quarter = one_hot_of(
        (128, 1024), lambda r, l: r == (l >> 7 << 3) + (l >> 3 & 3) + (l >> 2 & 1) * 4
    )
    spread.arrived()
    block = jnp.sum(from_chips[...], axis=0)
    own_block[0:4] = block
    own_block[4:8] = pltpu.roll(block, 64, 1)
    grown = pick_right(swap_eights(own_block[...]), grow_quarter)
    grown = pick_left(one_hot_of((32, 8), lambda r, l: r >> 2 == l), grown)
    cu_first[0] = coarse_u[0] + grown
    put_faces(tiles_of(cu_first, 0), yz_coarse_0, x_coarse_0, 1)
    coarse_swaps[0].start(0)
    inside_boxes(1, cu_first, coarse_b, coarse_sum)
    coarse_swaps[0].arrived()
    sweep_boxes(
        1, cu_first, coarse_sum, coarse_c, coarse_swaps[0], coarse_nbr, cu_second, coarse_swaps[1]
    )
    split = one_hot_of(
        (512, 512),
        lambda r, l: (l >> 8 == (r >> 4 & 1)) & ((l >> 4 & 15) == r >> 5) & ((l & 15) == (r & 15)),
    )
    inside_boxes(1, cu_second, coarse_b, coarse_sum)
    coarse_swaps[1].arrived()
    sweep_boxes(
        1, cu_second, coarse_sum, coarse_c, coarse_swaps[1], coarse_nbr, coarse_out, None
    )
    coarse_store = Store(coarse_out, coarse_to, 1, 1, output_sems.at[pl.ds(boxes // 2, 1)])
    coarse_store.start(0)

    quarters = jnp.concatenate(
        [
            coarse_out[0, 16 * (k // 2) : 16 * (k // 2) + 16, 512 * (k % 2) : 512 * (k % 2) + 512]
            for k in range(4)
        ],
        axis=0,
    )
    cubes = pick_right(quarters, split)
    base = pl.multiple_of(here.node * 8, 8)
    for k in range(8):
        octants[base + k] = cubes[16 * (k // 2) : 16 * (k // 2) + 16, 256 * (k % 2) : 256 * (k % 2) + 256]
    own = octants.at[pl.ds(base, 8)]
    waits = [copies.start(own, own, device) for _, device in here.peers_node()]
    grow_yz = one_hot_of(
        (256, 1024), lambda r, l: (l >> 6 == r >> 4) & ((l >> 1 & 15) == (r & 15))
    )
    grow_x = one_hot_of((32 * boxes, 16 * boxes), lambda r, l: r >> 1 == l)
    arrived(waits)
    for box in range(boxes):
        picked[16 * box : 16 * (box + 1)] = octants[cover_ref[0, box]]
    tall = pick_right(pick_left(grow_x, picked[...]), grow_yz)
    for box in range(boxes):
        u_first[box] = fine_u[box] + tall[32 * box : 32 * (box + 1)]

    def faces_of(box, carry):
        put_faces(tiles_of(u_first, box), yz_fine_0, x_fine_0, boxes + box)

    by_chunks(boxes, fine_swaps[0], faces_of)
    inside_boxes(boxes, u_first, fine_b, fine_sum)
    fine_swaps[0].arrived()
    sweep_boxes(
        boxes, u_first, fine_sum, fine_c, fine_swaps[0], fine_nbr, u_second, fine_swaps[1]
    )
    inside_boxes(boxes, u_second, fine_b, fine_sum)
    fine_swaps[1].arrived()
    live = count_ref[0, 0]
    fine_store = Store(fine_out, fine_to, boxes, 2, output_sems)
    sweep_boxes(
        boxes,
        u_second,
        fine_sum,
        fine_c,
        fine_swaps[1],
        fine_nbr,
        fine_out,
        None,
        lambda box: jnp.where(box < live, 1.0, 0.0).astype(F32),
        fine_store,
    )
    copies.finish()
    for sent in fine_swaps + coarse_swaps + [spread, fine_store, coarse_store]:
        sent.finish()


def hand_on_kernel(fine_from, coarse_from, fine_to, coarse_to, fine_held, coarse_held, came, sent):
    boxes = fine_from.shape[0]
    paths = [
        (fine_from.at[box], fine_held.at[box], fine_to.at[box], came.at[box], sent.at[box])
        for box in range(boxes)
    ]
    paths.append((coarse_from, coarse_held, coarse_to, came.at[boxes], sent.at[boxes]))
    ins = [pltpu.make_async_copy(a, b, sem) for a, b, _, sem, _ in paths]
    outs = [pltpu.make_async_copy(b, c, sem) for _, b, c, _, sem in paths]
    for copy in ins:
        copy.start()
    for coming, going in zip(ins, outs):
        coming.wait()
        going.start()
    for copy in outs:
        copy.wait()


VMEM, SMEM, ANY = (
    pl.BlockSpec(memory_space=pltpu.VMEM),
    pl.BlockSpec(memory_space=pltpu.SMEM),
    pl.BlockSpec(memory_space=pl.ANY),
)


def shards(
    n_box,
    n_node,
    fine_rhs,
    fine_diag,
    fine_count,
    fine_nbr,
    fine_cover,
    coarse_source,
    coarse_diag,
    coarse_nbr,
    coarse_place,
    bottom_diag,
):
    boxes = fine_rhs.shape[0]
    ny, nz, nc = grid_of(n_box)
    rows_x, rows_y, long = bottom_diag.shape
    deep, wide = rows_x + 2 * HALO, rows_y + 2 * Y_HALO
    count = n_box * n_node

    def like(shape, kind=F32):
        return jax.ShapeDtypeStruct(shape, kind)

    fine, coarse = (boxes, 32, 1024), (1, 32, 1024)
    chips = ny * nz * n_node
    grid = (nc, chips)
    limit = 62 * 1024 * 1024
    fine_u, fine_c, coarse_u, coarse_b, coarse_c, reach, blocks, places = pl.pallas_call(
        functools.partial(down_kernel, n_box, n_node),
        out_shape=(
            like(fine),
            like(fine),
            like(coarse),
            like(coarse),
            like(coarse),
            like((deep, wide, long)),
            like(grid + (4, 128)),
            like((1, 128), I32),
        ),
        in_specs=[ANY, ANY, SMEM, ANY, ANY, ANY, ANY, ANY, SMEM, ANY],
        out_specs=(ANY, ANY, ANY, ANY, ANY, ANY, ANY, VMEM),
        scratch_shapes=[
            pltpu.VMEM(fine, F32),
            pltpu.VMEM(fine, F32),
            pltpu.VMEM(coarse, F32),
            pltpu.VMEM(coarse, F32),
            pltpu.VMEM(coarse, F32),
            pltpu.SMEM((boxes, 6), I32),
            pltpu.SMEM((1, boxes), I32),
            pltpu.SMEM((1, 6), I32),
            pltpu.VMEM(fine, F32),
            pltpu.VMEM(fine, F32),
            pltpu.VMEM(coarse, F32),
            pltpu.VMEM(coarse, F32),
            pltpu.VMEM((rows_x, rows_y, long), F32),
            pltpu.VMEM(fine, F32),
            pltpu.VMEM(fine, F32),
            pltpu.VMEM(coarse, F32),
            pltpu.VMEM((3 * boxes, 32, 128), F32),
            pltpu.VMEM((3 * boxes, 2, 1024), F32),
            pltpu.VMEM((3 * boxes, 32, 128), F32),
            pltpu.VMEM((3 * boxes, 2, 1024), F32),
            pltpu.VMEM((rows_x, rows_y, long), F32),
            pltpu.VMEM((32 * boxes, 1024), F32),
            pltpu.VMEM((boxes, 16, 256), F32),
            pltpu.VMEM((8 * n_node, 16, 256), F32),
            pltpu.VMEM((n_node - 1, 8, 16, 256), F32),
            pltpu.SMEM((8 * n_node,), I32),
            pltpu.VMEM(coarse, F32),
            pltpu.VMEM((3, 32, 128), F32),
            pltpu.VMEM((3, 2, 1024), F32),
            pltpu.VMEM((3, 32, 128), F32),
            pltpu.VMEM((3, 2, 1024), F32),
            pltpu.VMEM(grid + (4, 128), F32),
            pltpu.VMEM(grid + (1, 128), I32),
            pltpu.SemaphoreType.DMA((64,)),
            pltpu.SemaphoreType.DMA((64,)),
            pltpu.SemaphoreType.DMA,
            pltpu.SemaphoreType.DMA((2, boxes)),
            pltpu.SemaphoreType.DMA((6,)),
            pltpu.SemaphoreType.DMA((6,)),
            pltpu.SemaphoreType.DMA((2, boxes // 2, 4)),
            pltpu.SemaphoreType.DMA((2, boxes // 2, 4)),
            pltpu.SemaphoreType.DMA((2, 1, 4)),
            pltpu.SemaphoreType.DMA((2, 1, 4)),
            pltpu.SemaphoreType.DMA((2, chips)),
            pltpu.SemaphoreType.DMA((2, chips)),
        ],
        compiler_params=pltpu.CompilerParams(
            collective_id=0, has_side_effects=True, vmem_limit_bytes=limit
        ),
        name="down",
    )(
        fine_rhs,
        fine_diag,
        fine_count,
        fine_nbr,
        fine_cover,
        coarse_source,
        coarse_diag,
        coarse_nbr,
        coarse_place,
        bottom_diag,
    )
    parts = pl.pallas_call(
        functools.partial(bottom_kernel, n_box, n_node, rows_x, rows_y),
        out_shape=like((count, 4, 128)),
        in_specs=[SMEM, ANY, ANY],
        out_specs=VMEM,
        scratch_shapes=[
            pltpu.VMEM((count, 4, 128), F32),
            pltpu.VMEM((2, deep + 16, wide, 128), F32),
            pltpu.VMEM((2, deep + 16, wide, 128), F32),
            pltpu.VMEM((2, deep + 16, wide, 128), F32),
            pltpu.VMEM((2, deep + 16, wide, 128), F32),
            pltpu.SMEM((count + 1,), I32),
            pltpu.SemaphoreType.DMA((3,)),
        ],
        compiler_params=pltpu.CompilerParams(vmem_limit_bytes=limit),
        name="bottom",
    )(places, reach, blocks.reshape(count, 4, 128))
    fine_out, coarse_out = pl.pallas_call(
        functools.partial(up_kernel, n_box, n_node),
        out_shape=(like(fine), like(coarse)),
        in_specs=[ANY, ANY, ANY, ANY, SMEM, ANY, ANY, ANY, ANY, ANY, ANY],
        out_specs=(ANY, ANY),
        scratch_shapes=[
            pltpu.VMEM(fine, F32),
            pltpu.VMEM(coarse, F32),
            pltpu.SemaphoreType.DMA((boxes // 2 + 1,)),
            pltpu.VMEM(fine, F32),
            pltpu.VMEM(fine, F32),
            pltpu.VMEM(fine, F32),
            pltpu.SMEM((boxes, 6), I32),
            pltpu.SMEM((1, boxes), I32),
            pltpu.VMEM(coarse, F32),
            pltpu.VMEM(coarse, F32),
            pltpu.VMEM(coarse, F32),
            pltpu.SMEM((1, 6), I32),
            pltpu.VMEM((chips, 4, 128), F32),
            pltpu.SemaphoreType.DMA((10,)),
            pltpu.VMEM((chips, 4, 128), F32),
            pltpu.VMEM((chips, 4, 128), F32),
            pltpu.VMEM((chips, 4, 128), F32),
            pltpu.VMEM((8, 128), F32),
            pltpu.VMEM(coarse, F32),
            pltpu.VMEM(coarse, F32),
            pltpu.VMEM((3, 32, 128), F32),
            pltpu.VMEM((3, 2, 1024), F32),
            pltpu.VMEM((3, 32, 128), F32),
            pltpu.VMEM((3, 2, 1024), F32),
            pltpu.VMEM((8 * n_node, 16, 256), F32),
            pltpu.VMEM((16 * boxes, 256), F32),
            pltpu.VMEM(fine, F32),
            pltpu.VMEM(fine, F32),
            pltpu.VMEM(fine, F32),
            pltpu.VMEM(coarse, F32),
            pltpu.VMEM((3 * boxes, 32, 128), F32),
            pltpu.VMEM((3 * boxes, 2, 1024), F32),
            pltpu.VMEM((3 * boxes, 32, 128), F32),
            pltpu.VMEM((3 * boxes, 2, 1024), F32),
            pltpu.SemaphoreType.DMA((8,)),
            pltpu.SemaphoreType.DMA((8,)),
            pltpu.SemaphoreType.DMA((2, boxes // 2, 4)),
            pltpu.SemaphoreType.DMA((2, boxes // 2, 4)),
            pltpu.SemaphoreType.DMA((2, 1, 4)),
            pltpu.SemaphoreType.DMA((2, 1, 4)),
            pltpu.SemaphoreType.DMA((chips,)),
            pltpu.SemaphoreType.DMA((chips,)),
        ],
        compiler_params=pltpu.CompilerParams(
            collective_id=1, has_side_effects=True, vmem_limit_bytes=limit
        ),
        name="up",
    )(
        parts.reshape(grid + (4, 128)),
        fine_u,
        fine_c,
        fine_rhs,
        fine_count,
        fine_nbr,
        fine_cover,
        coarse_u,
        coarse_b,
        coarse_c,
        coarse_nbr,
    )
    return pl.pallas_call(
        hand_on_kernel,
        out_shape=(like(fine), like(coarse)),
        in_specs=[ANY, ANY],
        out_specs=(ANY, ANY),
        scratch_shapes=[
            pltpu.VMEM(fine, F32),
            pltpu.VMEM(coarse, F32),
            pltpu.SemaphoreType.DMA((boxes + 1,)),
            pltpu.SemaphoreType.DMA((boxes + 1,)),
        ],
        compiler_params=pltpu.CompilerParams(vmem_limit_bytes=limit),
        name="hand_on",
    )(fine_out, coarse_out)


def solution(mesh):
    n_box, n_node = mesh.shape["box"], mesh.shape["node"]
    return jax.shard_map(
        functools.partial(shards, n_box, n_node),
        mesh=mesh,
        in_specs=(
            P(("box", "node"), None, None),
            P(("box", "node"), None, None),
            P("box", "node"),
            P(("box", "node"), None),
            P("box", "node"),
            P(("box", "node"), None, None),
            P(("box", "node"), None, None),
            P(("box", "node"), None),
            P(("box", "node")),
            P("box", "node", None),
        ),
        out_specs=(P(("box", "node"), None, None), P(("box", "node"), None, None)),
        check_vma=False,
    )
```

```python
import functools

import jax
import jax.numpy as jnp
from jax import lax
from jax.experimental import pallas as pl
from jax.experimental.pallas import tpu as pltpu
from jax.sharding import PartitionSpec as P

F32, BF16, I32 = jnp.float32, jnp.bfloat16, jnp.int32
MESH = pl.DeviceIdType.MESH
BOT_ITERS = 12
HALO = BOT_ITERS - 1
Y_HALO = 16
AT_ONCE = 4
TILES = 8


def grid_of(n_box):
    return {32: (4, 4, 2), 8: (2, 2, 2)}[n_box]


def lanes_of(shape):
    return lax.broadcasted_iota(I32, shape, len(shape) - 1)


def rows_of(shape):
    return lax.broadcasted_iota(I32, shape, len(shape) - 2)


def thirds(a):
    high = a.astype(BF16)
    rest = a - high.astype(F32)
    middle = rest.astype(BF16)
    low = (rest - middle.astype(F32)).astype(BF16)
    return high, middle, low


def pick_right(a, one_hot):
    high, middle, low = [jnp.dot(t, one_hot, preferred_element_type=F32) for t in thirds(a)]
    return high + (middle + low)


def pick_left(one_hot, a):
    high, middle, low = [jnp.dot(one_hot, t, preferred_element_type=F32) for t in thirds(a)]
    return high + (middle + low)


def one_hot_of(shape, test):
    return jnp.where(test(rows_of(shape), lanes_of(shape)), 1.0, 0.0).astype(BF16)


def roll_lanes(a, shift):
    shift = shift % 128
    return a if shift == 0 else pltpu.roll(a, shift, 1)


def tiles_of(ref, box):
    return [ref[box, :, 128 * t : 128 * (t + 1)] for t in range(TILES)]


def pack_faces(tiles):
    lane = lanes_of((32, 128))
    within, quarter = lane & 31, lane >> 5
    first, last = tiles[0], tiles[-1]
    packed = jnp.where(
        quarter == 0,
        first,
        jnp.where(
            quarter == 1,
            roll_lanes(first, 48),
            jnp.where(quarter == 2, roll_lanes(last, -16), last),
        ),
    )
    for t in range(TILES):
        packed = jnp.where((within >> 1) == t, roll_lanes(tiles[t], 2 * t + 1), packed)
    return packed


def put_faces(tiles, yz_ref, x_ref, slot):
    yz_ref[slot] = pack_faces(tiles)
    for t in range(TILES):
        x_ref[slot, 0:1, 128 * t : 128 * (t + 1)] = tiles[t][0:1, :]
        x_ref[slot, 1:2, 128 * t : 128 * (t + 1)] = tiles[t][31:32, :]


def ghosts_of(yz_ref, x_ref, nbr_ref, box):
    def chosen(ref, face):
        which = nbr_ref[box, face]
        kept = jnp.where(which >= 0, 1.0, 0.0).astype(F32)
        return ref[jnp.maximum(which, 0)], kept

    def tile(face):
        value, kept = chosen(yz_ref, face)
        return value * kept

    x_low, low_kept = chosen(x_ref, 0)
    x_high, high_kept = chosen(x_ref, 1)
    return (
        x_low[1:2] * low_kept,
        x_high[0:1] * high_kept,
        tile(2),
        tile(3),
        tile(4),
        tile(5),
    )


def beside_inside(tiles):
    lane, row = lanes_of((32, 128)), rows_of((32, 128))
    within = lane & 31
    nothing = jnp.zeros((32, 128), F32)
    ups = [nothing] + [roll_lanes(t, 32) for t in tiles]
    downs = [roll_lanes(t, 96) for t in tiles] + [nothing]
    sums = []
    for t in range(TILES):
        along_x = jnp.where(row == 0, 0.0, pltpu.roll(tiles[t], 1, 0)) + jnp.where(
            row == 31, 0.0, pltpu.roll(tiles[t], 31, 0)
        )
        along_y = jnp.where(lane < 32, ups[t], ups[t + 1]) + jnp.where(
            lane >= 96, downs[t + 1], downs[t]
        )
        along_z = jnp.where(within == 0, 0.0, roll_lanes(tiles[t], 1)) + jnp.where(
            within == 31, 0.0, roll_lanes(tiles[t], 127)
        )
        sums.append(along_x + along_y + along_z)
    return sums


def with_ghosts(sums, ghosts):
    x_low, x_high, y_low, y_high, z_low, z_high = ghosts
    lane, row = lanes_of((32, 128)), rows_of((8, 128))
    within = lane & 31
    below = jnp.where(within < 16, roll_lanes(y_low, 48), roll_lanes(y_low, 32))
    above = jnp.where(within < 16, roll_lanes(y_high, 48), roll_lanes(y_high, 96))
    both = jnp.where((lane & 1) == 0, z_low, roll_lanes(z_high, 62))
    edge = (within == 0) | (within == 31)
    full = []
    for t in range(TILES):
        cut = slice(128 * t, 128 * (t + 1))
        value = sums[t] + jnp.where(edge, roll_lanes(both, -32 - 2 * t), 0.0)
        if t == 0:
            value += jnp.where(lane < 32, below, 0.0)
        if t == TILES - 1:
            value += jnp.where(lane >= 96, above, 0.0)
        full.append(
            jnp.concatenate(
                [
                    value[0:8] + jnp.where(row == 0, x_low[:, cut], 0.0),
                    value[8:24],
                    value[24:32] + jnp.where(row == 7, x_high[:, cut], 0.0),
                ],
                axis=0,
            )
        )
    return full


def fan_out(value, step):
    row = rows_of((8, 128))
    for bit in (1, 2, 4):
        value = jnp.where((row & bit) != 0, roll_lanes(value, step * bit), value)
    return value


def swap_eights(value):
    lane = lanes_of((8, 128))
    result = jnp.zeros((8, 128), F32)
    for b in range(8):
        spread = fan_out(jnp.broadcast_to(value[b : b + 1], (8, 128)), -8)
        result = jnp.where((lane >> 3) == b, roll_lanes(spread, 8 * b), result)
    return result


class Copies:
    def __init__(self, send_sems, recv_sems):
        self.send_sems, self.recv_sems, self.made = send_sems, recv_sems, []

    def start(self, source, target, device):
        number = len(self.made)
        copy = pltpu.make_async_remote_copy(
            src_ref=source,
            dst_ref=target,
            send_sem=self.send_sems.at[number],
            recv_sem=self.recv_sems.at[number],
            device_id=device,
            device_id_type=MESH,
        )
        copy.start()
        self.made.append(copy)
        return copy

    def finish(self):
        for copy in self.made:
            copy.wait_send()


def arrived(copies):
    for copy in copies:
        copy.wait_recv()


class Place:
    def __init__(self, n_box, n_node):
        self.n_box, self.n_node = n_box, n_node
        self.ny, self.nz, self.nc = grid_of(n_box)
        self.box, self.node = lax.axis_index("box"), lax.axis_index("node")
        self.chips = self.ny * self.nz * n_node
        self.core = self.box & 1
        self.z = (self.box >> 1) & (self.nz - 1)
        self.y = (self.box >> 1) >> (self.nz.bit_length() - 1)

    def along_line(self, step):
        total = self.n_box * self.n_node
        other = (self.box * self.n_node + self.node + step + total) % total
        return (other // self.n_node, other % self.n_node)

    def next_node(self, step):
        return (self.node + step + self.n_node) % self.n_node

    def at_node(self, step):
        return (self.box, self.next_node(step))

    def at_box(self, step):
        return ((self.box + step + self.n_box) % self.n_box, self.node)

    def mate(self):
        return (self.box ^ 1, self.node)

    def at_chip(self, step):
        x_bits = self.n_node.bit_length() - 1
        z_bits = self.nz.bit_length() - 1
        x = (self.node + step) & (self.n_node - 1)
        z = (self.z + (step >> x_bits)) & (self.nz - 1)
        y = (self.y + (step >> x_bits + z_bits)) & (self.ny - 1)
        return ((y * self.nz + z) * self.nc + self.core, x)

    def before_chip(self, step):
        x_bits = self.n_node.bit_length() - 1
        z_bits = self.nz.bit_length() - 1
        x = (self.node - (step & self.n_node - 1)) & (self.n_node - 1)
        z = (self.z - (step >> x_bits & self.nz - 1)) & (self.nz - 1)
        y = (self.y - (step >> x_bits + z_bits)) & (self.ny - 1)
        return ((y * self.nz + z) * self.nc + self.core, x)

    def peers_node(self):
        for step in range(1, self.n_node):
            yield self.next_node(step), self.at_node(step)

    def greet(self, more):
        peers = [self.along_line(1), self.along_line(-1)] + more
        peers += [device for _, device in self.peers_node()]
        peers.append(self.mate())
        barrier = pltpu.get_barrier_semaphore()
        for device in peers:
            pl.semaphore_signal(barrier, inc=1, device_id=device, device_id_type=MESH)

        def chip(step, carry):
            pl.semaphore_signal(
                barrier, inc=1, device_id=self.at_chip(step), device_id_type=MESH
            )
            return carry

        lax.fori_loop(1, self.chips, chip, 0, unroll=7)
        self.peer_count = len(peers) + self.chips - 1

    def greeted(self):
        pl.semaphore_wait(pltpu.get_barrier_semaphore(), self.peer_count)


class Swap:
    def __init__(self, here, yz_ref, x_ref, boxes, step, send_sems, recv_sems):
        self.here, self.refs, self.boxes, self.step = here, (yz_ref, x_ref), boxes, step
        self.send_sems, self.recv_sems = send_sems, recv_sems

    def copies(self, chunk):
        made = []
        for number in range(4):
            ref, later = self.refs[number // 2], 2 * (number % 2)
            at = chunk * self.step
            made.append(
                pltpu.make_async_remote_copy(
                    src_ref=ref.at[pl.ds(self.boxes + at, self.step)],
                    dst_ref=ref.at[pl.ds(later * self.boxes + at, self.step)],
                    send_sem=self.send_sems.at[chunk, number],
                    recv_sem=self.recv_sems.at[chunk, number],
                    device_id=self.here.along_line(1 - later),
                    device_id_type=MESH,
                )
            )
        return made

    def start(self, chunk):
        for copy in self.copies(chunk):
            copy.start()

    def arrived(self):
        for chunk in range(self.boxes // self.step):
            for copy in self.copies(chunk):
                copy.wait_recv()

    def finish(self):
        for chunk in range(self.boxes // self.step):
            for copy in self.copies(chunk):
                copy.wait_send()


def by_chunks(boxes, swap, one):
    step = min(boxes, 2)

    def some(chunk, carry):
        for number in range(step):
            one(chunk * step + number, 0)
        if swap is not None and swap.step == step:
            swap.start(chunk)
        return carry

    lax.fori_loop(0, boxes // step, some, 0)


class Store:
    def __init__(self, source, target, boxes, step, sems):
        self.source, self.target, self.boxes, self.step = source, target, boxes, step
        self.sems = sems

    def copy(self, chunk):
        part = pl.ds(chunk * self.step, self.step)
        return pltpu.make_async_copy(
            self.source.at[part], self.target.at[part], self.sems.at[chunk]
        )

    def start(self, chunk):
        self.copy(chunk).start()

    def finish(self):
        for chunk in range(self.boxes // self.step):
            self.copy(chunk).wait()


class Spread:
    def __init__(self, here, source, target, landed, device, send_sem, recv_sem):
        self.here, self.source, self.target, self.device = here, source, target, device
        self.landed, self.send_sem, self.recv_sem = landed, send_sem, recv_sem

    def copy(self, source, target, device):
        return pltpu.make_async_remote_copy(
            src_ref=source,
            dst_ref=target,
            send_sem=self.send_sem,
            recv_sem=self.recv_sem,
            device_id=device,
            device_id_type=MESH,
        )

    def start(self):
        def one(step, carry):
            self.copy(self.source(step), self.target(step), self.device(step)).start()
            return carry

        lax.fori_loop(1, self.here.chips, one, 0, unroll=7)

    def whole(self):
        return self.copy(self.landed, self.landed, self.here.mate())

    def arrived(self):
        self.whole().wait_recv()

    def finish(self):
        self.whole().wait_send()


def write_tiles(ref, box, tiles):
    for t in range(TILES):
        ref[box, :, 128 * t : 128 * (t + 1)] = tiles[t]


def first_sweep(boxes, u_ref, b_ref, d_ref, c_ref, swap, ready=None):
    def one(box, carry):
        if ready is not None:
            ready(box)
        scales, tiles = [], []
        for t in range(TILES):
            cut = slice(128 * t, 128 * (t + 1))
            scales.append(0.8 / (6.0 + d_ref[box, :, cut]))
            tiles.append(scales[t] * b_ref[box, :, cut])
        write_tiles(c_ref, box, scales)
        write_tiles(u_ref, box, tiles)
        put_faces(tiles, *swap.refs, boxes + box)

    by_chunks(boxes, swap, one)


def inside_boxes(boxes, u_ref, b_ref, sum_ref):
    def one(box, carry):
        tiles = tiles_of(u_ref, box)
        sums = beside_inside(tiles)
        sources = tiles_of(b_ref, box)
        write_tiles(sum_ref, box, [sources[t] + sums[t] for t in range(TILES)])

    by_chunks(boxes, None, one)


def sweep_boxes(
    boxes, u_ref, sum_ref, c_ref, came, nbr_ref, out_ref, swap, keep=None, store=None
):
    yz_from, x_from = came.refs

    def one(box, carry):
        tiles = tiles_of(u_ref, box)
        sums = with_ghosts(tiles_of(sum_ref, box), ghosts_of(yz_from, x_from, nbr_ref, box))
        fresh = []
        for t in range(TILES):
            cut = slice(128 * t, 128 * (t + 1))
            fresh.append(0.2 * tiles[t] + c_ref[box, :, cut] * sums[t])
        if keep is not None:
            kept = keep(box)
            fresh = [t * kept for t in fresh]
        write_tiles(out_ref, box, fresh)
        if swap is not None:
            put_faces(fresh, *swap.refs, boxes + box)

    by_chunks(boxes, store if swap is None else swap, one)


def residual_boxes(boxes, u_ref, sum_ref, d_ref, came, nbr_ref, r_ref, keep=None):
    yz_from, x_from = came.refs

    def one(box, carry):
        tiles = tiles_of(u_ref, box)
        sums = with_ghosts(tiles_of(sum_ref, box), ghosts_of(yz_from, x_from, nbr_ref, box))
        rests = []
        for t in range(TILES):
            cut = slice(128 * t, 128 * (t + 1))
            left = sums[t] - (6.0 + d_ref[box, :, cut]) * tiles[t]
            rests.append(left if keep is None else left * keep(box))
        for t in range(TILES):
            r_ref[pl.ds(pl.multiple_of(box * 32, 32), 32), 128 * t : 128 * (t + 1)] = rests[t]

    by_chunks(boxes, None, one)


def down_kernel(
    n_box,
    n_node,
    fine_b_in,
    fine_d_in,
    count_ref,
    nbr_in,
    cover_in,
    source_in,
    coarse_d_in,
    coarse_nbr_in,
    place_ref,
    bottom_d_in,
    fine_u_out,
    fine_c_out,
    coarse_u_out,
    coarse_b_out,
    coarse_c_out,
    reach,
    blocks_out,
    places_out,
    fine_u,
    fine_c,
    coarse_u,
    coarse_b,
    coarse_c,
    fine_nbr,
    cover_ref,
    coarse_nbr,
    fine_b,
    fine_d,
    source_ref,
    coarse_d,
    bottom_d,
    u_first,
    fine_sum,
    coarse_sum,
    yz_fine_0,
    x_fine_0,
    yz_fine_1,
    x_fine_1,
    slab_c,
    rest_ref,
    octants,
    placed,
    lifted,
    found_at,
    cu_first,
    yz_coarse_0,
    x_coarse_0,
    yz_coarse_1,
    x_coarse_1,
    blocks,
    places,
    send_sems,
    recv_sems,
    local_sem,
    fine_sems,
    input_sems,
    output_sems,
    fine_sent,
    fine_came,
    coarse_sent,
    coarse_came,
    spread_sent,
    spread_came,
):
    here = Place(n_box, n_node)
    copies = Copies(send_sems, recv_sems)
    boxes = fine_b.shape[0]

    def fine_input(box, number):
        pair = ((fine_b_in, fine_b), (fine_d_in, fine_d))[number]
        return pltpu.make_async_copy(pair[0].at[box], pair[1].at[box], fine_sems.at[number, box])

    for box in range(boxes):
        fine_input(box, 0).start()
        fine_input(box, 1).start()
    inputs = [
        pltpu.make_async_copy(source, target, input_sems.at[number])
        for number, (source, target) in enumerate(
            (
                (bottom_d_in, bottom_d),
                (source_in, source_ref),
                (coarse_d_in, coarse_d),
                (nbr_in, fine_nbr),
                (cover_in, cover_ref),
                (coarse_nbr_in, coarse_nbr),
            )
        )
    ]
    for copy in inputs:
        copy.start()
    here.greet([here.at_box(1), here.at_box(-1), here.at_box(2), here.at_box(-2)])

    def keep(source, target, number):
        copy = pltpu.make_async_copy(source, target, output_sems.at[number])
        copy.start()
        return copy

    def ready(box):
        fine_input(box, 0).wait()
        fine_input(box, 1).wait()

    core = here.core
    places[core, 0] = jnp.full((1, 128), place_ref[0], I32)
    fine_swaps = [
        Swap(here, yz, x, boxes, step, fine_sent.at[number], fine_came.at[number])
        for number, (yz, x, step) in enumerate(
            ((yz_fine_0, x_fine_0, boxes), (yz_fine_1, x_fine_1, 2))
        )
    ]
    coarse_swaps = [
        Swap(here, yz, x, 1, 1, coarse_sent.at[number], coarse_came.at[number])
        for number, (yz, x) in enumerate(((yz_coarse_0, x_coarse_0), (yz_coarse_1, x_coarse_1)))
    ]
    spreads = [
        Spread(
            here,
            lambda step, ref=ref: ref.at[core, 0],
            lambda step, ref=ref: ref.at[core, step],
            ref.at[core, pl.ds(1, here.chips - 1)],
            here.at_chip,
            spread_sent.at[number],
            spread_came.at[number],
        )
        for number, ref in enumerate((places, blocks))
    ]

    first_sweep(boxes, u_first, fine_b, fine_d, fine_c, fine_swaps[0], ready)
    kept = [keep(fine_c, fine_c_out, 0)]
    rows_x, rows_y = bottom_d.shape[0], bottom_d.shape[1]
    inputs[0].wait()
    part_z = one_hot_of((256, 256), lambda r, l: r == ((l & 127) << 1) + (l >> 7))

    def scale_plane(x, carry):
        slab_c[x] = pick_right(0.8 / (6.0 + bottom_d[x]), part_z)
        return carry

    lax.fori_loop(0, rows_x, scale_plane, 0)
    here.greeted()
    fine_swaps[0].start(0)
    own_x, own_y = pl.ds(HALO, rows_x), pl.ds(Y_HALO, rows_y)
    own_copy = pltpu.make_async_copy(slab_c, reach.at[own_x, own_y], local_sem)
    own_copy.start()
    sides_y = (pl.ds(0, Y_HALO), pl.ds(Y_HALO + rows_y, Y_HALO))
    some = HALO - rows_x
    to_x = (
        (1, 0, rows_x, HALO - rows_x),
        (-1, 0, rows_x, HALO + rows_x),
        (2, rows_x - some, some, 0),
        (-2, 0, some, HALO + 2 * rows_x),
    )
    halo_x = [
        copies.start(
            slab_c.at[pl.ds(first, wide)],
            reach.at[pl.ds(target, wide), own_y],
            here.at_box(step),
        )
        for step, first, wide, target in to_x
    ]
    spreads[0].start()

    for copy in inputs[1:]:
        copy.wait()
    for target in range(8 * n_node):
        slot = jnp.int32(-1)
        for box in range(boxes):
            slot = jnp.where(cover_ref[0, box] == target, box, slot)
        found_at[target] = slot

    own_copy.wait()

    inside_boxes(boxes, u_first, fine_b, fine_sum)
    fine_swaps[0].arrived()
    sweep_boxes(
        boxes, u_first, fine_sum, fine_c, fine_swaps[0], fine_nbr, fine_u, fine_swaps[1]
    )
    kept.append(keep(fine_u, fine_u_out, 1))
    spreads[0].arrived()
    mate_places = copies.start(places.at[core], places.at[core], here.mate())
    fold_yz = one_hot_of(
        (1024, 256), lambda r, l: (r >> 6 == l >> 4) & ((r & 31) >> 1 == (l & 15))
    )
    fold_x = one_hot_of((16 * boxes, 32 * boxes), lambda r, l: l >> 1 == r)
    inside_boxes(boxes, fine_u, fine_b, fine_sum)
    fine_swaps[1].arrived()
    live = count_ref[0, 0]
    residual_boxes(
        boxes,
        fine_u,
        fine_sum,
        fine_d,
        fine_swaps[1],
        fine_nbr,
        rest_ref,
        lambda box: jnp.where(box < live, 1.0, 0.0).astype(F32),
    )
    cubes = pick_left(fold_x, pick_right(rest_ref[...], fold_yz)) * 0.5
    for box in range(boxes):
        octants[box] = cubes[16 * box : 16 * (box + 1)]

    def place_one(target, carry):
        slot = found_at[target]
        kept = jnp.where(slot >= 0, 1.0, 0.0).astype(F32)
        placed[target] = octants[jnp.maximum(slot, 0)] * kept
        return carry

    lax.fori_loop(0, 8 * n_node, place_one, 0)
    given = []
    for step, (other, device) in enumerate(here.peers_node()):
        given.append(
            copies.start(
                placed.at[pl.ds(pl.multiple_of(other * 8, 8), 8)], lifted.at[step], device
            )
        )
    spread = one_hot_of(
        (512, 512),
        lambda r, l: (r >> 8 == (l >> 4 & 1)) & ((r >> 4 & 15) == l >> 5) & ((r & 15) == (l & 15)),
    )
    arrived(given)
    halo_y = [
        copies.start(
            slab_c.at[:, pl.ds(rows_y - Y_HALO, Y_HALO)],
            reach.at[own_x, sides_y[0]],
            here.at_node(1),
        ),
        copies.start(
            slab_c.at[:, pl.ds(0, Y_HALO)],
            reach.at[own_x, sides_y[1]],
            here.at_node(-1),
        ),
    ]
    total = placed[pl.ds(pl.multiple_of(here.node * 8, 8), 8)]
    for step in range(n_node - 1):
        total = total + lifted[step]
    pairs = jnp.concatenate(
        [jnp.concatenate([total[2 * k], total[2 * k + 1]], axis=1) for k in range(4)], axis=0
    )
    grown = pick_right(pairs, spread)
    for k in range(4):
        at_x, at_y = 16 * (k // 2), 512 * (k % 2)
        coarse_b[0, at_x : at_x + 16, at_y : at_y + 512] = (
            source_ref[0, at_x : at_x + 16, at_y : at_y + 512] + grown[16 * k : 16 * (k + 1)]
        )

    first_sweep(1, cu_first, coarse_b, coarse_d, coarse_c, coarse_swaps[0])
    kept += [keep(coarse_b, coarse_b_out, 2), keep(coarse_c, coarse_c_out, 3)]
    inside_boxes(1, cu_first, coarse_b, coarse_sum)
    coarse_swaps[0].arrived()
    sweep_boxes(
        1, cu_first, coarse_sum, coarse_c, coarse_swaps[0], coarse_nbr, coarse_u, coarse_swaps[1]
    )
    kept.append(keep(coarse_u, coarse_u_out, 4))
    fold_quarter = one_hot_of(
        (1024, 128), lambda r, l: (r >> 7 == (l >> 3 & 7)) & ((r >> 2 & 7) == ((l & 3) << 1) + (l >> 2 & 1))
    )
    inside_boxes(1, coarse_u, coarse_b, coarse_sum)
    arrived(halo_y)
    for step, first, wide, target in to_x:
        for side in sides_y:
            halo_x.append(
                copies.start(
                    reach.at[pl.ds(HALO + first, wide), side],
                    reach.at[pl.ds(target, wide), side],
                    here.at_box(step),
                )
            )
    coarse_swaps[1].arrived()
    residual_boxes(1, coarse_u, coarse_sum, coarse_d, coarse_swaps[1], coarse_nbr, rest_ref)
    folded = pick_right(rest_ref[0:32], fold_quarter)
    folded = pick_left(one_hot_of((8, 32), lambda r, l: l >> 2 == r), folded) * 0.25
    block = swap_eights(folded)
    late = pltpu.roll(block, 64, 1)
    blocks[core, 0] = jnp.where(lanes_of((4, 128)) < 64, block[0:4], late[4:8])

    spreads[1].start()
    arrived([mate_places])
    row = jnp.zeros((1, 128), I32)
    lane = lanes_of((1, 128))
    for number in range(n_box * n_node):
        row = jnp.where(lane == number, places[number // here.chips, number % here.chips], row)
    places_out[...] = row
    spreads[1].arrived()
    arrived([copies.start(blocks.at[core], blocks.at[core], here.mate())])
    kept.append(keep(blocks, blocks_out, 5))
    arrived(halo_x)
    copies.finish()
    for copy in kept:
        copy.wait()
    for sent in fine_swaps + coarse_swaps + spreads:
        sent.finish()


def bottom_kernel(
    n_box, n_node, rows_x, rows_y, places, reach, blocks_in, out, blocks, scale, source, first, second, hits, sems
):
    deep, wide, long = reach.shape
    count = n_box * n_node
    per_side = long // 8
    side_bits = per_side.bit_length() - 1
    box, node = lax.axis_index("box"), lax.axis_index("node")
    at_x, at_y = box * rows_x - HALO, node * rows_y - Y_HALO
    fills = [
        pltpu.make_async_copy(
            reach.at[:, :, 128 * half : 128 * (half + 1)],
            scale.at[half, pl.ds(8, deep)],
            sems.at[half],
        )
        for half in range(2)
    ]
    fills.append(pltpu.make_async_copy(blocks_in, blocks, sems.at[2]))
    for copy in fills:
        copy.start()
    zeros = jnp.zeros((wide, 128), F32)

    def clear(x, carry):
        for half in range(2):
            source[half, x] = zeros
            first[half, x] = zeros
        return carry

    lax.fori_loop(8, 8 + deep, clear, 0, unroll=2)
    out[...] = jnp.zeros(out.shape, F32)

    def where_is(number):
        place = places[0, number]
        return (
            (place >> 2 * side_bits << 3) - at_x,
            ((place >> side_bits & per_side - 1) << 3) - at_y,
            place & per_side - 1,
        )

    def look(number, found):
        x, y, _ = where_is(number)
        hits[found] = number
        hit = (x > -8) & (x < deep) & (y >= 0) & (y < wide)
        return found + hit.astype(I32)

    found = lax.fori_loop(0, count, look, jnp.int32(0), unroll=8)

    for copy in fills:
        copy.wait()

    def empty(x, carry):
        for half in range(2):
            scale[half, x] = zeros
        return carry

    lax.fori_loop(8, 8 + jnp.maximum(-at_x, 0), empty, 0)
    lax.fori_loop(8 + jnp.minimum(rows_x * n_box - at_x, deep), 8 + deep, empty, 0)

    def empty_rows(start):
        def one(x, carry):
            for half in range(2):
                scale[half, x, start : start + Y_HALO] = jnp.zeros((Y_HALO, 128), F32)
            return carry

        lax.fori_loop(8, 8 + deep, one, 0)

    pl.when(node == 0)(lambda: empty_rows(0))
    pl.when(node == n_node - 1)(lambda: empty_rows(Y_HALO + rows_y))

    lane, row = lanes_of((8, 128)), rows_of((8, 128))

    def put(at, carry):
        number = hits[at]
        x, y, z = where_is(number)
        block = blocks[number]
        kept = (lane >> 2) == z
        rows = pl.ds(pl.multiple_of(y, 8), 8)
        spots = [(half, x + ix + 8, rows) for half in range(2) for ix in range(8)]
        before = [source[spot] for spot in spots]
        first_before = [first[spot] for spot in spots]
        scales = [scale[spot] for spot in spots]
        whole = jnp.concatenate([block, pltpu.roll(block, 64, 1)], axis=0)
        fresh = []
        for half in range(2):
            for ix in range(8):
                shift = (z << 2) + 128 - 4 * half - 8 * ix & 127
                fresh.append(jnp.where(kept, pltpu.roll(whole, shift, 1), 0.0))
        for number, spot in enumerate(spots):
            source[spot] = before[number] + fresh[number]
            first[spot] = first_before[number] + fresh[number] * scales[number]
        return carry

    lax.fori_loop(0, found, put, 0)

    refs = (first, second)
    eight = (8, 128)
    lane = lanes_of(eight)
    for sweep_no in range(HALO):
        left = HALO - 1 - sweep_no
        margin = (left + 3) // 4 * 4
        low = Y_HALO - margin
        here, there = refs[sweep_no % 2], refs[(sweep_no + 1) % 2]

        def planes(group, carry):
            fresh = []
            for number in range(AT_ONCE):
                x = 8 + HALO - left + AT_ONCE * group + number
                for at in range(low, low + rows_y + 2 * margin, 8):
                    cut = slice(at, at + 8)
                    mids = [here[half, x, cut, :] for half in range(2)]
                    turned = (
                        jnp.where(lane == 0, 0.0, pltpu.roll(mids[1], 1, 1)),
                        jnp.where(lane == 127, 0.0, pltpu.roll(mids[0], 127, 1)),
                    )
                    for half in range(2):
                        around = here[half, x - 1, cut, :] + here[half, x + 1, cut, :]
                        around += here[half, x, at - 1 : at + 7, :]
                        around += here[half, x, at + 1 : at + 9, :]
                        around += mids[1 - half] + turned[half]
                        value = 0.2 * mids[half] + scale[half, x, cut, :] * (
                            source[half, x, cut, :] + around
                        )
                        fresh.append((half, x, cut, value))
            for half, x, cut, value in fresh:
                there[half, x, cut, :] = value
            return carry

        lax.fori_loop(0, (rows_x + 2 * left + AT_ONCE - 1) // AT_ONCE, planes, 0)
    solved = refs[HALO % 2]

    def take(at, carry):
        number = hits[at]
        x, y, z = where_is(number)

        @pl.when((x == HALO) & (y >= Y_HALO) & (y < Y_HALO + rows_y))
        def _():
            rows = pl.ds(pl.multiple_of(y, 8), 8)
            back = 128 - (z << 2)
            gathered = jnp.zeros(eight, F32)
            for ix in range(8):
                for half in range(2):
                    turned = pltpu.roll(
                        solved[half, 8 + HALO + ix, rows, :], back + 4 * half + 8 * ix & 127, 1
                    )
                    gathered = jnp.where((lane >> 2) == 2 * ix + half, turned, gathered)
            late = pltpu.roll(gathered, 64, 1)
            out[number] = jnp.where(lanes_of((4, 128)) < 64, gathered[0:4], late[4:8])

        return carry

    lax.fori_loop(0, found, take, 0)


def up_kernel(
    n_box,
    n_node,
    parts_in,
    fine_u_in,
    fine_c_in,
    fine_b_in,
    count_ref,
    nbr_in,
    cover_in,
    coarse_u_in,
    coarse_b_in,
    coarse_c_in,
    coarse_nbr_in,
    fine_to,
    coarse_to,
    fine_out,
    coarse_out,
    output_sems,
    fine_u,
    fine_c,
    fine_b,
    fine_nbr,
    cover_ref,
    coarse_u,
    coarse_b,
    coarse_c,
    coarse_nbr,
    own_parts,
    input_sems,
    from_core,
    sum_core,
    from_chips,
    own_block,
    cu_first,
    cu_second,
    yz_coarse_0,
    x_coarse_0,
    yz_coarse_1,
    x_coarse_1,
    octants,
    picked,
    u_first,
    u_second,
    fine_sum,
    coarse_sum,
    yz_fine_0,
    x_fine_0,
    yz_fine_1,
    x_fine_1,
    send_sems,
    recv_sems,
    fine_sent,
    fine_came,
    coarse_sent,
    coarse_came,
    spread_sent,
    spread_came,
):
    here = Place(n_box, n_node)
    copies = Copies(send_sems, recv_sems)
    boxes = fine_u.shape[0]
    core = here.core
    inputs = [
        pltpu.make_async_copy(source, target, input_sems.at[number])
        for number, (source, target) in enumerate(
            (
                (parts_in.at[core], own_parts),
                (coarse_u_in, coarse_u),
                (coarse_b_in, coarse_b),
                (coarse_c_in, coarse_c),
                (coarse_nbr_in, coarse_nbr),
                (nbr_in, fine_nbr),
                (cover_in, cover_ref),
                (fine_u_in, fine_u),
                (fine_c_in, fine_c),
                (fine_b_in, fine_b),
            )
        )
    ]
    for copy in inputs:
        copy.start()
    fine_swaps = [
        Swap(here, yz, x, boxes, 2, fine_sent.at[number], fine_came.at[number])
        for number, (yz, x) in enumerate(((yz_fine_0, x_fine_0), (yz_fine_1, x_fine_1)))
    ]
    coarse_swaps = [
        Swap(here, yz, x, 1, 1, coarse_sent.at[number], coarse_came.at[number])
        for number, (yz, x) in enumerate(((yz_coarse_0, x_coarse_0), (yz_coarse_1, x_coarse_1)))
    ]
    here.greet([])
    here.greeted()

    from_mate = copies.start(parts_in.at[1 - core], from_core, here.mate())
    for copy in inputs:
        copy.wait()
    arrived([from_mate])
    sum_core[...] = own_parts[...] + from_core[...]
    spread = Spread(
        here,
        lambda step: sum_core.at[step],
        lambda step: from_chips.at[step],
        from_chips.at[pl.ds(1, here.chips - 1)],
        here.before_chip,
        spread_sent,
        spread_came,
    )
    from_chips[0] = sum_core[0]
    spread.start()
    grow_quarter = one_hot_of(
        (128, 1024), lambda r, l: r == (l >> 7 << 3) + (l >> 3 & 3) + (l >> 2 & 1) * 4
    )
    spread.arrived()
    block = jnp.sum(from_chips[...], axis=0)
    own_block[0:4] = block
    own_block[4:8] = pltpu.roll(block, 64, 1)
    grown = pick_right(swap_eights(own_block[...]), grow_quarter)
    grown = pick_left(one_hot_of((32, 8), lambda r, l: r >> 2 == l), grown)
    cu_first[0] = coarse_u[0] + grown
    put_faces(tiles_of(cu_first, 0), yz_coarse_0, x_coarse_0, 1)
    coarse_swaps[0].start(0)
    inside_boxes(1, cu_first, coarse_b, coarse_sum)
    coarse_swaps[0].arrived()
    sweep_boxes(
        1, cu_first, coarse_sum, coarse_c, coarse_swaps[0], coarse_nbr, cu_second, coarse_swaps[1]
    )
    split = one_hot_of(
        (512, 512),
        lambda r, l: (l >> 8 == (r >> 4 & 1)) & ((l >> 4 & 15) == r >> 5) & ((l & 15) == (r & 15)),
    )
    inside_boxes(1, cu_second, coarse_b, coarse_sum)
    coarse_swaps[1].arrived()
    sweep_boxes(
        1, cu_second, coarse_sum, coarse_c, coarse_swaps[1], coarse_nbr, coarse_out, None
    )
    coarse_store = Store(coarse_out, coarse_to, 1, 1, output_sems.at[pl.ds(boxes // 2, 1)])
    coarse_store.start(0)

    quarters = jnp.concatenate(
        [
            coarse_out[0, 16 * (k // 2) : 16 * (k // 2) + 16, 512 * (k % 2) : 512 * (k % 2) + 512]
            for k in range(4)
        ],
        axis=0,
    )
    cubes = pick_right(quarters, split)
    base = pl.multiple_of(here.node * 8, 8)
    for k in range(8):
        octants[base + k] = cubes[16 * (k // 2) : 16 * (k // 2) + 16, 256 * (k % 2) : 256 * (k % 2) + 256]
    own = octants.at[pl.ds(base, 8)]
    waits = [copies.start(own, own, device) for _, device in here.peers_node()]
    grow_yz = one_hot_of(
        (256, 1024), lambda r, l: (l >> 6 == r >> 4) & ((l >> 1 & 15) == (r & 15))
    )
    grow_x = one_hot_of((32 * boxes, 16 * boxes), lambda r, l: r >> 1 == l)
    arrived(waits)
    for box in range(boxes):
        picked[16 * box : 16 * (box + 1)] = octants[cover_ref[0, box]]
    tall = pick_right(pick_left(grow_x, picked[...]), grow_yz)
    for box in range(boxes):
        u_first[box] = fine_u[box] + tall[32 * box : 32 * (box + 1)]

    def faces_of(box, carry):
        put_faces(tiles_of(u_first, box), yz_fine_0, x_fine_0, boxes + box)

    by_chunks(boxes, fine_swaps[0], faces_of)
    inside_boxes(boxes, u_first, fine_b, fine_sum)
    fine_swaps[0].arrived()
    sweep_boxes(
        boxes, u_first, fine_sum, fine_c, fine_swaps[0], fine_nbr, u_second, fine_swaps[1]
    )
    inside_boxes(boxes, u_second, fine_b, fine_sum)
    fine_swaps[1].arrived()
    live = count_ref[0, 0]
    fine_store = Store(fine_out, fine_to, boxes, 2, output_sems)
    sweep_boxes(
        boxes,
        u_second,
        fine_sum,
        fine_c,
        fine_swaps[1],
        fine_nbr,
        fine_out,
        None,
        lambda box: jnp.where(box < live, 1.0, 0.0).astype(F32),
        fine_store,
    )
    copies.finish()
    for sent in fine_swaps + coarse_swaps + [spread, fine_store, coarse_store]:
        sent.finish()


def hand_on_kernel(fine_from, coarse_from, fine_to, coarse_to, fine_held, coarse_held, came, sent):
    boxes = fine_from.shape[0]
    paths = [
        (fine_from.at[box], fine_held.at[box], fine_to.at[box], came.at[box], sent.at[box])
        for box in range(boxes)
    ]
    paths.append((coarse_from, coarse_held, coarse_to, came.at[boxes], sent.at[boxes]))
    ins = [pltpu.make_async_copy(a, b, sem) for a, b, _, sem, _ in paths]
    outs = [pltpu.make_async_copy(b, c, sem) for _, b, c, _, sem in paths]
    for copy in ins:
        copy.start()
    for coming, going in zip(ins, outs):
        coming.wait()
        going.start()
    for copy in outs:
        copy.wait()


VMEM, SMEM, ANY = (
    pl.BlockSpec(memory_space=pltpu.VMEM),
    pl.BlockSpec(memory_space=pltpu.SMEM),
    pl.BlockSpec(memory_space=pl.ANY),
)


def shards(
    n_box,
    n_node,
    fine_rhs,
    fine_diag,
    fine_count,
    fine_nbr,
    fine_cover,
    coarse_source,
    coarse_diag,
    coarse_nbr,
    coarse_place,
    bottom_diag,
):
    boxes = fine_rhs.shape[0]
    ny, nz, nc = grid_of(n_box)
    rows_x, rows_y, long = bottom_diag.shape
    deep, wide = rows_x + 2 * HALO, rows_y + 2 * Y_HALO
    count = n_box * n_node

    def like(shape, kind=F32):
        return jax.ShapeDtypeStruct(shape, kind)

    fine, coarse = (boxes, 32, 1024), (1, 32, 1024)
    chips = ny * nz * n_node
    grid = (nc, chips)
    limit = 62 * 1024 * 1024
    fine_u, fine_c, coarse_u, coarse_b, coarse_c, reach, blocks, places = pl.pallas_call(
        functools.partial(down_kernel, n_box, n_node),
        out_shape=(
            like(fine),
            like(fine),
            like(coarse),
            like(coarse),
            like(coarse),
            like((deep, wide, long)),
            like(grid + (4, 128)),
            like((1, 128), I32),
        ),
        in_specs=[ANY, ANY, SMEM, ANY, ANY, ANY, ANY, ANY, SMEM, ANY],
        out_specs=(ANY, ANY, ANY, ANY, ANY, ANY, ANY, VMEM),
        scratch_shapes=[
            pltpu.VMEM(fine, F32),
            pltpu.VMEM(fine, F32),
            pltpu.VMEM(coarse, F32),
            pltpu.VMEM(coarse, F32),
            pltpu.VMEM(coarse, F32),
            pltpu.SMEM((boxes, 6), I32),
            pltpu.SMEM((1, boxes), I32),
            pltpu.SMEM((1, 6), I32),
            pltpu.VMEM(fine, F32),
            pltpu.VMEM(fine, F32),
            pltpu.VMEM(coarse, F32),
            pltpu.VMEM(coarse, F32),
            pltpu.VMEM((rows_x, rows_y, long), F32),
            pltpu.VMEM(fine, F32),
            pltpu.VMEM(fine, F32),
            pltpu.VMEM(coarse, F32),
            pltpu.VMEM((3 * boxes, 32, 128), F32),
            pltpu.VMEM((3 * boxes, 2, 1024), F32),
            pltpu.VMEM((3 * boxes, 32, 128), F32),
            pltpu.VMEM((3 * boxes, 2, 1024), F32),
            pltpu.VMEM((rows_x, rows_y, long), F32),
            pltpu.VMEM((32 * boxes, 1024), F32),
            pltpu.VMEM((boxes, 16, 256), F32),
            pltpu.VMEM((8 * n_node, 16, 256), F32),
            pltpu.VMEM((n_node - 1, 8, 16, 256), F32),
            pltpu.SMEM((8 * n_node,), I32),
            pltpu.VMEM(coarse, F32),
            pltpu.VMEM((3, 32, 128), F32),
            pltpu.VMEM((3, 2, 1024), F32),
            pltpu.VMEM((3, 32, 128), F32),
            pltpu.VMEM((3, 2, 1024), F32),
            pltpu.VMEM(grid + (4, 128), F32),
            pltpu.VMEM(grid + (1, 128), I32),
            pltpu.SemaphoreType.DMA((64,)),
            pltpu.SemaphoreType.DMA((64,)),
            pltpu.SemaphoreType.DMA,
            pltpu.SemaphoreType.DMA((2, boxes)),
            pltpu.SemaphoreType.DMA((6,)),
            pltpu.SemaphoreType.DMA((6,)),
            pltpu.SemaphoreType.DMA((2, boxes // 2, 4)),
            pltpu.SemaphoreType.DMA((2, boxes // 2, 4)),
            pltpu.SemaphoreType.DMA((2, 1, 4)),
            pltpu.SemaphoreType.DMA((2, 1, 4)),
            pltpu.SemaphoreType.DMA((2,)),
            pltpu.SemaphoreType.DMA((2,)),
        ],
        compiler_params=pltpu.CompilerParams(
            collective_id=0, has_side_effects=True, vmem_limit_bytes=limit
        ),
        name="down",
    )(
        fine_rhs,
        fine_diag,
        fine_count,
        fine_nbr,
        fine_cover,
        coarse_source,
        coarse_diag,
        coarse_nbr,
        coarse_place,
        bottom_diag,
    )
    parts = pl.pallas_call(
        functools.partial(bottom_kernel, n_box, n_node, rows_x, rows_y),
        out_shape=like((count, 4, 128)),
        in_specs=[SMEM, ANY, ANY],
        out_specs=VMEM,
        scratch_shapes=[
            pltpu.VMEM((count, 4, 128), F32),
            pltpu.VMEM((2, deep + 16, wide, 128), F32),
            pltpu.VMEM((2, deep + 16, wide, 128), F32),
            pltpu.VMEM((2, deep + 16, wide, 128), F32),
            pltpu.VMEM((2, deep + 16, wide, 128), F32),
            pltpu.SMEM((count + 1,), I32),
            pltpu.SemaphoreType.DMA((3,)),
        ],
        compiler_params=pltpu.CompilerParams(vmem_limit_bytes=limit),
        name="bottom",
    )(places, reach, blocks.reshape(count, 4, 128))
    fine_out, coarse_out = pl.pallas_call(
        functools.partial(up_kernel, n_box, n_node),
        out_shape=(like(fine), like(coarse)),
        in_specs=[ANY, ANY, ANY, ANY, SMEM, ANY, ANY, ANY, ANY, ANY, ANY],
        out_specs=(ANY, ANY),
        scratch_shapes=[
            pltpu.VMEM(fine, F32),
            pltpu.VMEM(coarse, F32),
            pltpu.SemaphoreType.DMA((boxes // 2 + 1,)),
            pltpu.VMEM(fine, F32),
            pltpu.VMEM(fine, F32),
            pltpu.VMEM(fine, F32),
            pltpu.SMEM((boxes, 6), I32),
            pltpu.SMEM((1, boxes), I32),
            pltpu.VMEM(coarse, F32),
            pltpu.VMEM(coarse, F32),
            pltpu.VMEM(coarse, F32),
            pltpu.SMEM((1, 6), I32),
            pltpu.VMEM((chips, 4, 128), F32),
            pltpu.SemaphoreType.DMA((10,)),
            pltpu.VMEM((chips, 4, 128), F32),
            pltpu.VMEM((chips, 4, 128), F32),
            pltpu.VMEM((chips, 4, 128), F32),
            pltpu.VMEM((8, 128), F32),
            pltpu.VMEM(coarse, F32),
            pltpu.VMEM(coarse, F32),
            pltpu.VMEM((3, 32, 128), F32),
            pltpu.VMEM((3, 2, 1024), F32),
            pltpu.VMEM((3, 32, 128), F32),
            pltpu.VMEM((3, 2, 1024), F32),
            pltpu.VMEM((8 * n_node, 16, 256), F32),
            pltpu.VMEM((16 * boxes, 256), F32),
            pltpu.VMEM(fine, F32),
            pltpu.VMEM(fine, F32),
            pltpu.VMEM(fine, F32),
            pltpu.VMEM(coarse, F32),
            pltpu.VMEM((3 * boxes, 32, 128), F32),
            pltpu.VMEM((3 * boxes, 2, 1024), F32),
            pltpu.VMEM((3 * boxes, 32, 128), F32),
            pltpu.VMEM((3 * boxes, 2, 1024), F32),
            pltpu.SemaphoreType.DMA((8,)),
            pltpu.SemaphoreType.DMA((8,)),
            pltpu.SemaphoreType.DMA((2, boxes // 2, 4)),
            pltpu.SemaphoreType.DMA((2, boxes // 2, 4)),
            pltpu.SemaphoreType.DMA((2, 1, 4)),
            pltpu.SemaphoreType.DMA((2, 1, 4)),
            pltpu.SemaphoreType.DMA,
            pltpu.SemaphoreType.DMA,
        ],
        compiler_params=pltpu.CompilerParams(
            collective_id=1, has_side_effects=True, vmem_limit_bytes=limit
        ),
        name="up",
    )(
        parts.reshape(grid + (4, 128)),
        fine_u,
        fine_c,
        fine_rhs,
        fine_count,
        fine_nbr,
        fine_cover,
        coarse_u,
        coarse_b,
        coarse_c,
        coarse_nbr,
    )
    return pl.pallas_call(
        hand_on_kernel,
        out_shape=(like(fine), like(coarse)),
        in_specs=[ANY, ANY],
        out_specs=(ANY, ANY),
        scratch_shapes=[
            pltpu.VMEM(fine, F32),
            pltpu.VMEM(coarse, F32),
            pltpu.SemaphoreType.DMA((boxes + 1,)),
            pltpu.SemaphoreType.DMA((boxes + 1,)),
        ],
        compiler_params=pltpu.CompilerParams(vmem_limit_bytes=limit),
        name="hand_on",
    )(fine_out, coarse_out)


def solution(mesh):
    n_box, n_node = mesh.shape["box"], mesh.shape["node"]
    return jax.shard_map(
        functools.partial(shards, n_box, n_node),
        mesh=mesh,
        in_specs=(
            P(("box", "node"), None, None),
            P(("box", "node"), None, None),
            P("box", "node"),
            P(("box", "node"), None),
            P("box", "node"),
            P(("box", "node"), None, None),
            P(("box", "node"), None, None),
            P(("box", "node"), None),
            P(("box", "node")),
            P("box", "node", None),
        ),
        out_specs=(P(("box", "node"), None, None), P(("box", "node"), None, None)),
        check_vma=False,
    )
```

```python
import functools

import jax
import jax.numpy as jnp
from jax import lax
from jax.experimental import pallas as pl
from jax.experimental.pallas import tpu as pltpu
from jax.sharding import PartitionSpec as P

F32, BF16, I32 = jnp.float32, jnp.bfloat16, jnp.int32
MESH = pl.DeviceIdType.MESH
BOT_ITERS = 12
HALO = BOT_ITERS - 1
Y_HALO = 16
AT_ONCE = 4
TILES = 8


def grid_of(n_box):
    return {32: (4, 4, 2), 8: (2, 2, 2)}[n_box]


def lanes_of(shape):
    return lax.broadcasted_iota(I32, shape, len(shape) - 1)


def rows_of(shape):
    return lax.broadcasted_iota(I32, shape, len(shape) - 2)


def thirds(a):
    high = a.astype(BF16)
    rest = a - high.astype(F32)
    middle = rest.astype(BF16)
    low = (rest - middle.astype(F32)).astype(BF16)
    return high, middle, low


def pick_right(a, one_hot):
    high, middle, low = [jnp.dot(t, one_hot, preferred_element_type=F32) for t in thirds(a)]
    return high + (middle + low)


def pick_left(one_hot, a):
    high, middle, low = [jnp.dot(one_hot, t, preferred_element_type=F32) for t in thirds(a)]
    return high + (middle + low)


def one_hot_of(shape, test):
    return jnp.where(test(rows_of(shape), lanes_of(shape)), 1.0, 0.0).astype(BF16)


def roll_lanes(a, shift):
    shift = shift % 128
    return a if shift == 0 else pltpu.roll(a, shift, 1)


def tiles_of(ref, box):
    return [ref[box, :, 128 * t : 128 * (t + 1)] for t in range(TILES)]


def pack_faces(tiles):
    lane = lanes_of((32, 128))
    within, quarter = lane & 31, lane >> 5
    first, last = tiles[0], tiles[-1]
    packed = jnp.where(
        quarter == 0,
        first,
        jnp.where(
            quarter == 1,
            roll_lanes(first, 48),
            jnp.where(quarter == 2, roll_lanes(last, -16), last),
        ),
    )
    for t in range(TILES):
        packed = jnp.where((within >> 1) == t, roll_lanes(tiles[t], 2 * t + 1), packed)
    return packed


def put_faces(tiles, yz_ref, x_ref, slot):
    yz_ref[slot] = pack_faces(tiles)
    for t in range(TILES):
        x_ref[slot, 0:1, 128 * t : 128 * (t + 1)] = tiles[t][0:1, :]
        x_ref[slot, 1:2, 128 * t : 128 * (t + 1)] = tiles[t][31:32, :]


def ghosts_of(yz_ref, x_ref, nbr_ref, box):
    def chosen(ref, face):
        which = nbr_ref[box, face]
        kept = jnp.where(which >= 0, 1.0, 0.0).astype(F32)
        return ref[jnp.maximum(which, 0)], kept

    def tile(face):
        value, kept = chosen(yz_ref, face)
        return value * kept

    x_low, low_kept = chosen(x_ref, 0)
    x_high, high_kept = chosen(x_ref, 1)
    return (
        x_low[1:2] * low_kept,
        x_high[0:1] * high_kept,
        tile(2),
        tile(3),
        tile(4),
        tile(5),
    )


def beside_inside(tiles):
    lane, row = lanes_of((32, 128)), rows_of((32, 128))
    within = lane & 31
    nothing = jnp.zeros((32, 128), F32)
    ups = [nothing] + [roll_lanes(t, 32) for t in tiles]
    downs = [roll_lanes(t, 96) for t in tiles] + [nothing]
    sums = []
    for t in range(TILES):
        along_x = jnp.where(row == 0, 0.0, pltpu.roll(tiles[t], 1, 0)) + jnp.where(
            row == 31, 0.0, pltpu.roll(tiles[t], 31, 0)
        )
        along_y = jnp.where(lane < 32, ups[t], ups[t + 1]) + jnp.where(
            lane >= 96, downs[t + 1], downs[t]
        )
        along_z = jnp.where(within == 0, 0.0, roll_lanes(tiles[t], 1)) + jnp.where(
            within == 31, 0.0, roll_lanes(tiles[t], 127)
        )
        sums.append(along_x + along_y + along_z)
    return sums


def with_ghosts(sums, ghosts):
    x_low, x_high, y_low, y_high, z_low, z_high = ghosts
    lane, row = lanes_of((32, 128)), rows_of((8, 128))
    within = lane & 31
    below = jnp.where(within < 16, roll_lanes(y_low, 48), roll_lanes(y_low, 32))
    above = jnp.where(within < 16, roll_lanes(y_high, 48), roll_lanes(y_high, 96))
    both = jnp.where((lane & 1) == 0, z_low, roll_lanes(z_high, 62))
    edge = (within == 0) | (within == 31)
    full = []
    for t in range(TILES):
        cut = slice(128 * t, 128 * (t + 1))
        value = sums[t] + jnp.where(edge, roll_lanes(both, -32 - 2 * t), 0.0)
        if t == 0:
            value += jnp.where(lane < 32, below, 0.0)
        if t == TILES - 1:
            value += jnp.where(lane >= 96, above, 0.0)
        full.append(
            jnp.concatenate(
                [
                    value[0:8] + jnp.where(row == 0, x_low[:, cut], 0.0),
                    value[8:24],
                    value[24:32] + jnp.where(row == 7, x_high[:, cut], 0.0),
                ],
                axis=0,
            )
        )
    return full


def fan_out(value, step):
    row = rows_of((8, 128))
    for bit in (1, 2, 4):
        value = jnp.where((row & bit) != 0, roll_lanes(value, step * bit), value)
    return value


def swap_eights(value):
    lane = lanes_of((8, 128))
    result = jnp.zeros((8, 128), F32)
    for b in range(8):
        spread = fan_out(jnp.broadcast_to(value[b : b + 1], (8, 128)), -8)
        result = jnp.where((lane >> 3) == b, roll_lanes(spread, 8 * b), result)
    return result


class Copies:
    def __init__(self, send_sems, recv_sems):
        self.send_sems, self.recv_sems, self.made = send_sems, recv_sems, []

    def start(self, source, target, device):
        number = len(self.made)
        copy = pltpu.make_async_remote_copy(
            src_ref=source,
            dst_ref=target,
            send_sem=self.send_sems.at[number],
            recv_sem=self.recv_sems.at[number],
            device_id=device,
            device_id_type=MESH,
        )
        copy.start()
        self.made.append(copy)
        return copy

    def finish(self):
        for copy in self.made:
            copy.wait_send()


def arrived(copies):
    for copy in copies:
        copy.wait_recv()


class Place:
    def __init__(self, n_box, n_node):
        self.n_box, self.n_node = n_box, n_node
        self.ny, self.nz, self.nc = grid_of(n_box)
        self.box, self.node = lax.axis_index("box"), lax.axis_index("node")
        self.line, self.sheet = self.nc * n_node, self.ny * self.nz
        self.chips = self.sheet * n_node
        self.core = self.box & 1
        self.z = (self.box >> 1) & (self.nz - 1)
        self.y = (self.box >> 1) >> (self.nz.bit_length() - 1)

    def along_line(self, step):
        total = self.n_box * self.n_node
        other = (self.box * self.n_node + self.node + step + total) % total
        return (other // self.n_node, other % self.n_node)

    def next_node(self, step):
        return (self.node + step + self.n_node) % self.n_node

    def at_node(self, step):
        return (self.box, self.next_node(step))

    def at_box(self, step):
        return ((self.box + step + self.n_box) % self.n_box, self.node)

    def mate(self):
        return (self.box ^ 1, self.node)

    def at_line(self, step, sign):
        x_bits = self.n_node.bit_length() - 1
        x = (self.node + sign * (step & self.n_node - 1)) & (self.n_node - 1)
        return (self.box ^ (step >> x_bits), x)

    def at_sheet(self, step, sign):
        z_bits = self.nz.bit_length() - 1
        z = (self.z + sign * (step & self.nz - 1)) & (self.nz - 1)
        y = (self.y + sign * (step >> z_bits)) & (self.ny - 1)
        return ((y * self.nz + z) * self.nc + self.core, self.node)

    def before_chip(self, step):
        x_bits = self.n_node.bit_length() - 1
        z_bits = self.nz.bit_length() - 1
        x = (self.node - (step & self.n_node - 1)) & (self.n_node - 1)
        z = (self.z - (step >> x_bits & self.nz - 1)) & (self.nz - 1)
        y = (self.y - (step >> x_bits + z_bits)) & (self.ny - 1)
        return ((y * self.nz + z) * self.nc + self.core, x)

    def peers_node(self):
        for step in range(1, self.n_node):
            yield self.next_node(step), self.at_node(step)

    def greet(self, more, all_chips=False):
        peers = [self.along_line(1), self.along_line(-1)] + more
        barrier = pltpu.get_barrier_semaphore()
        for device in peers:
            pl.semaphore_signal(barrier, inc=1, device_id=device, device_id_type=MESH)

        def chip(step, carry):
            device = self.before_chip(step)
            pl.semaphore_signal(barrier, inc=1, device_id=device, device_id_type=MESH)
            return carry

        if all_chips:
            lax.fori_loop(1, self.chips, chip, 0, unroll=7)
        self.peer_count = len(peers) + (self.chips - 1 if all_chips else 0)

    def greeted(self):
        pl.semaphore_wait(pltpu.get_barrier_semaphore(), self.peer_count)


class Swap:
    def __init__(self, here, yz_ref, x_ref, boxes, step, send_sems, recv_sems):
        self.here, self.refs, self.boxes, self.step = here, (yz_ref, x_ref), boxes, step
        self.send_sems, self.recv_sems = send_sems, recv_sems

    def copies(self, chunk):
        made = []
        for number in range(4):
            ref, later = self.refs[number // 2], 2 * (number % 2)
            at = chunk * self.step
            made.append(
                pltpu.make_async_remote_copy(
                    src_ref=ref.at[pl.ds(self.boxes + at, self.step)],
                    dst_ref=ref.at[pl.ds(later * self.boxes + at, self.step)],
                    send_sem=self.send_sems.at[chunk, number],
                    recv_sem=self.recv_sems.at[chunk, number],
                    device_id=self.here.along_line(1 - later),
                    device_id_type=MESH,
                )
            )
        return made

    def start(self, chunk):
        for copy in self.copies(chunk):
            copy.start()

    def arrived(self):
        for chunk in range(self.boxes // self.step):
            for copy in self.copies(chunk):
                copy.wait_recv()

    def finish(self):
        for chunk in range(self.boxes // self.step):
            for copy in self.copies(chunk):
                copy.wait_send()


def by_chunks(boxes, swap, one):
    step = min(boxes, 2)

    def some(chunk, carry):
        for number in range(step):
            one(chunk * step + number, 0)
        if swap is not None and swap.step == step:
            swap.start(chunk)
        return carry

    lax.fori_loop(0, boxes // step, some, 0)


class Store:
    def __init__(self, source, target, boxes, step, sems):
        self.source, self.target, self.boxes, self.step = source, target, boxes, step
        self.sems = sems

    def copy(self, chunk):
        part = pl.ds(chunk * self.step, self.step)
        return pltpu.make_async_copy(
            self.source.at[part], self.target.at[part], self.sems.at[chunk]
        )

    def start(self, chunk):
        self.copy(chunk).start()

    def finish(self):
        for chunk in range(self.boxes // self.step):
            self.copy(chunk).wait()


class Spread:
    def __init__(self, count, source, target, landed, device, send_sem, recv_sem):
        self.count, self.source, self.target, self.device = count, source, target, device
        self.landed, self.send_sem, self.recv_sem = landed, send_sem, recv_sem

    def copy(self, source, target, device):
        return pltpu.make_async_remote_copy(
            src_ref=source,
            dst_ref=target,
            send_sem=self.send_sem,
            recv_sem=self.recv_sem,
            device_id=device,
            device_id_type=MESH,
        )

    def start(self):
        def one(step, carry):
            self.copy(self.source(step), self.target(step), self.device(step)).start()
            return carry

        lax.fori_loop(1, self.count, one, 0, unroll=7 if self.count > 16 else self.count - 1)

    def whole(self):
        return self.copy(self.landed, self.landed, self.device(1))

    def arrived(self):
        self.whole().wait_recv()

    def finish(self):
        self.whole().wait_send()


def write_to_all(here, ref, send_sems, recv_sems):
    return (
        Spread(
            here.line,
            lambda step: ref.at[0, 0],
            lambda step: ref.at[0, step],
            ref.at[0, pl.ds(1, here.line - 1)],
            lambda step: here.at_line(step, 1),
            send_sems.at[0],
            recv_sems.at[0],
        ),
        Spread(
            here.sheet,
            lambda step: ref.at[0],
            lambda step: ref.at[step],
            ref.at[pl.ds(1, here.sheet - 1)],
            lambda step: here.at_sheet(step, 1),
            send_sems.at[1],
            recv_sems.at[1],
        ),
    )


def write_tiles(ref, box, tiles):
    for t in range(TILES):
        ref[box, :, 128 * t : 128 * (t + 1)] = tiles[t]


def first_sweep(boxes, u_ref, b_ref, d_ref, c_ref, swap, ready=None):
    def one(box, carry):
        if ready is not None:
            ready(box)
        scales, tiles = [], []
        for t in range(TILES):
            cut = slice(128 * t, 128 * (t + 1))
            scales.append(0.8 / (6.0 + d_ref[box, :, cut]))
            tiles.append(scales[t] * b_ref[box, :, cut])
        write_tiles(c_ref, box, scales)
        write_tiles(u_ref, box, tiles)
        put_faces(tiles, *swap.refs, boxes + box)

    by_chunks(boxes, swap, one)


def inside_boxes(boxes, u_ref, b_ref, sum_ref):
    def one(box, carry):
        tiles = tiles_of(u_ref, box)
        sums = beside_inside(tiles)
        sources = tiles_of(b_ref, box)
        write_tiles(sum_ref, box, [sources[t] + sums[t] for t in range(TILES)])

    by_chunks(boxes, None, one)


def sweep_boxes(
    boxes, u_ref, sum_ref, c_ref, came, nbr_ref, out_ref, swap, keep=None, store=None
):
    yz_from, x_from = came.refs

    def one(box, carry):
        tiles = tiles_of(u_ref, box)
        sums = with_ghosts(tiles_of(sum_ref, box), ghosts_of(yz_from, x_from, nbr_ref, box))
        fresh = []
        for t in range(TILES):
            cut = slice(128 * t, 128 * (t + 1))
            fresh.append(0.2 * tiles[t] + c_ref[box, :, cut] * sums[t])
        if keep is not None:
            kept = keep(box)
            fresh = [t * kept for t in fresh]
        write_tiles(out_ref, box, fresh)
        if swap is not None:
            put_faces(fresh, *swap.refs, boxes + box)

    by_chunks(boxes, store if swap is None else swap, one)


def residual_boxes(boxes, u_ref, sum_ref, d_ref, came, nbr_ref, r_ref, keep=None):
    yz_from, x_from = came.refs

    def one(box, carry):
        tiles = tiles_of(u_ref, box)
        sums = with_ghosts(tiles_of(sum_ref, box), ghosts_of(yz_from, x_from, nbr_ref, box))
        rests = []
        for t in range(TILES):
            cut = slice(128 * t, 128 * (t + 1))
            left = sums[t] - (6.0 + d_ref[box, :, cut]) * tiles[t]
            rests.append(left if keep is None else left * keep(box))
        for t in range(TILES):
            r_ref[pl.ds(pl.multiple_of(box * 32, 32), 32), 128 * t : 128 * (t + 1)] = rests[t]

    by_chunks(boxes, None, one)


def down_kernel(
    n_box,
    n_node,
    fine_b_in,
    fine_d_in,
    count_ref,
    nbr_in,
    cover_in,
    source_in,
    coarse_d_in,
    coarse_nbr_in,
    place_ref,
    bottom_d_in,
    fine_u_out,
    fine_c_out,
    coarse_u_out,
    coarse_b_out,
    coarse_c_out,
    reach,
    blocks_out,
    places_out,
    fine_u,
    fine_c,
    coarse_u,
    coarse_b,
    coarse_c,
    fine_nbr,
    cover_ref,
    coarse_nbr,
    fine_b,
    fine_d,
    source_ref,
    coarse_d,
    bottom_d,
    u_first,
    fine_sum,
    coarse_sum,
    yz_fine_0,
    x_fine_0,
    yz_fine_1,
    x_fine_1,
    slab_c,
    rest_ref,
    octants,
    placed,
    lifted,
    found_at,
    cu_first,
    yz_coarse_0,
    x_coarse_0,
    yz_coarse_1,
    x_coarse_1,
    blocks,
    places,
    send_sems,
    recv_sems,
    local_sem,
    fine_sems,
    input_sems,
    output_sems,
    fine_sent,
    fine_came,
    coarse_sent,
    coarse_came,
    spread_sent,
    spread_came,
):
    here = Place(n_box, n_node)
    copies = Copies(send_sems, recv_sems)
    boxes = fine_b.shape[0]

    def fine_input(box, number):
        pair = ((fine_b_in, fine_b), (fine_d_in, fine_d))[number]
        return pltpu.make_async_copy(pair[0].at[box], pair[1].at[box], fine_sems.at[number, box])

    for box in range(boxes):
        fine_input(box, 0).start()
        fine_input(box, 1).start()
    inputs = [
        pltpu.make_async_copy(source, target, input_sems.at[number])
        for number, (source, target) in enumerate(
            (
                (bottom_d_in, bottom_d),
                (source_in, source_ref),
                (coarse_d_in, coarse_d),
                (nbr_in, fine_nbr),
                (cover_in, cover_ref),
                (coarse_nbr_in, coarse_nbr),
            )
        )
    ]
    for copy in inputs:
        copy.start()
    here.greet(
        [here.at_box(step) for step in (1, -1, 2, -2)]
        + [here.at_line(step, 1) for step in range(1, here.line)]
        + [here.at_sheet(step, 1) for step in range(1, here.sheet)]
    )

    def keep(source, target, number):
        copy = pltpu.make_async_copy(source, target, output_sems.at[number])
        copy.start()
        return copy

    def ready(box):
        fine_input(box, 0).wait()
        fine_input(box, 1).wait()

    places[0, 0] = jnp.full((1, 128), place_ref[0], I32)
    fine_swaps = [
        Swap(here, yz, x, boxes, step, fine_sent.at[number], fine_came.at[number])
        for number, (yz, x, step) in enumerate(
            ((yz_fine_0, x_fine_0, boxes), (yz_fine_1, x_fine_1, 2))
        )
    ]
    coarse_swaps = [
        Swap(here, yz, x, 1, 1, coarse_sent.at[number], coarse_came.at[number])
        for number, (yz, x) in enumerate(((yz_coarse_0, x_coarse_0), (yz_coarse_1, x_coarse_1)))
    ]
    place_spreads = write_to_all(here, places, spread_sent.at[0], spread_came.at[0])
    block_spreads = write_to_all(here, blocks, spread_sent.at[1], spread_came.at[1])

    first_sweep(boxes, u_first, fine_b, fine_d, fine_c, fine_swaps[0], ready)
    kept = [keep(fine_c, fine_c_out, 0)]
    rows_x, rows_y = bottom_d.shape[0], bottom_d.shape[1]
    inputs[0].wait()
    part_z = one_hot_of((256, 256), lambda r, l: r == ((l & 127) << 1) + (l >> 7))

    def scale_plane(x, carry):
        slab_c[x] = pick_right(0.8 / (6.0 + bottom_d[x]), part_z)
        return carry

    lax.fori_loop(0, rows_x, scale_plane, 0)
    here.greeted()
    fine_swaps[0].start(0)
    own_x, own_y = pl.ds(HALO, rows_x), pl.ds(Y_HALO, rows_y)
    own_copy = pltpu.make_async_copy(slab_c, reach.at[own_x, own_y], local_sem)
    own_copy.start()
    sides_y = (pl.ds(0, Y_HALO), pl.ds(Y_HALO + rows_y, Y_HALO))
    some = HALO - rows_x
    to_x = (
        (1, 0, rows_x, HALO - rows_x),
        (-1, 0, rows_x, HALO + rows_x),
        (2, rows_x - some, some, 0),
        (-2, 0, some, HALO + 2 * rows_x),
    )
    halo_x = [
        copies.start(
            slab_c.at[pl.ds(first, wide)],
            reach.at[pl.ds(target, wide), own_y],
            here.at_box(step),
        )
        for step, first, wide, target in to_x
    ]
    place_spreads[0].start()

    for copy in inputs[1:]:
        copy.wait()
    for target in range(8 * n_node):
        slot = jnp.int32(-1)
        for box in range(boxes):
            slot = jnp.where(cover_ref[0, box] == target, box, slot)
        found_at[target] = slot

    own_copy.wait()

    inside_boxes(boxes, u_first, fine_b, fine_sum)
    fine_swaps[0].arrived()
    sweep_boxes(
        boxes, u_first, fine_sum, fine_c, fine_swaps[0], fine_nbr, fine_u, fine_swaps[1]
    )
    kept.append(keep(fine_u, fine_u_out, 1))
    place_spreads[0].arrived()
    place_spreads[1].start()
    fold_yz = one_hot_of(
        (1024, 256), lambda r, l: (r >> 6 == l >> 4) & ((r & 31) >> 1 == (l & 15))
    )
    fold_x = one_hot_of((16 * boxes, 32 * boxes), lambda r, l: l >> 1 == r)
    inside_boxes(boxes, fine_u, fine_b, fine_sum)
    fine_swaps[1].arrived()
    live = count_ref[0, 0]
    residual_boxes(
        boxes,
        fine_u,
        fine_sum,
        fine_d,
        fine_swaps[1],
        fine_nbr,
        rest_ref,
        lambda box: jnp.where(box < live, 1.0, 0.0).astype(F32),
    )
    cubes = pick_left(fold_x, pick_right(rest_ref[...], fold_yz)) * 0.5
    for box in range(boxes):
        octants[box] = cubes[16 * box : 16 * (box + 1)]

    def place_one(target, carry):
        slot = found_at[target]
        kept = jnp.where(slot >= 0, 1.0, 0.0).astype(F32)
        placed[target] = octants[jnp.maximum(slot, 0)] * kept
        return carry

    lax.fori_loop(0, 8 * n_node, place_one, 0)
    given = []
    for step, (other, device) in enumerate(here.peers_node()):
        given.append(
            copies.start(
                placed.at[pl.ds(pl.multiple_of(other * 8, 8), 8)], lifted.at[step], device
            )
        )
    spread = one_hot_of(
        (512, 512),
        lambda r, l: (r >> 8 == (l >> 4 & 1)) & ((r >> 4 & 15) == l >> 5) & ((r & 15) == (l & 15)),
    )
    arrived(given)
    halo_y = [
        copies.start(
            slab_c.at[:, pl.ds(rows_y - Y_HALO, Y_HALO)],
            reach.at[own_x, sides_y[0]],
            here.at_node(1),
        ),
        copies.start(
            slab_c.at[:, pl.ds(0, Y_HALO)],
            reach.at[own_x, sides_y[1]],
            here.at_node(-1),
        ),
    ]
    total = placed[pl.ds(pl.multiple_of(here.node * 8, 8), 8)]
    for step in range(n_node - 1):
        total = total + lifted[step]
    pairs = jnp.concatenate(
        [jnp.concatenate([total[2 * k], total[2 * k + 1]], axis=1) for k in range(4)], axis=0
    )
    grown = pick_right(pairs, spread)
    for k in range(4):
        at_x, at_y = 16 * (k // 2), 512 * (k % 2)
        coarse_b[0, at_x : at_x + 16, at_y : at_y + 512] = (
            source_ref[0, at_x : at_x + 16, at_y : at_y + 512] + grown[16 * k : 16 * (k + 1)]
        )

    first_sweep(1, cu_first, coarse_b, coarse_d, coarse_c, coarse_swaps[0])
    kept += [keep(coarse_b, coarse_b_out, 2), keep(coarse_c, coarse_c_out, 3)]
    inside_boxes(1, cu_first, coarse_b, coarse_sum)
    coarse_swaps[0].arrived()
    sweep_boxes(
        1, cu_first, coarse_sum, coarse_c, coarse_swaps[0], coarse_nbr, coarse_u, coarse_swaps[1]
    )
    kept.append(keep(coarse_u, coarse_u_out, 4))
    fold_quarter = one_hot_of(
        (1024, 128), lambda r, l: (r >> 7 == (l >> 3 & 7)) & ((r >> 2 & 7) == ((l & 3) << 1) + (l >> 2 & 1))
    )
    inside_boxes(1, coarse_u, coarse_b, coarse_sum)
    arrived(halo_y)
    for step, first, wide, target in to_x:
        for side in sides_y:
            halo_x.append(
                copies.start(
                    reach.at[pl.ds(HALO + first, wide), side],
                    reach.at[pl.ds(target, wide), side],
                    here.at_box(step),
                )
            )
    coarse_swaps[1].arrived()
    residual_boxes(1, coarse_u, coarse_sum, coarse_d, coarse_swaps[1], coarse_nbr, rest_ref)
    folded = pick_right(rest_ref[0:32], fold_quarter)
    folded = pick_left(one_hot_of((8, 32), lambda r, l: l >> 2 == r), folded) * 0.25
    block = swap_eights(folded)
    late = pltpu.roll(block, 64, 1)
    blocks[0, 0] = jnp.where(lanes_of((4, 128)) < 64, block[0:4], late[4:8])

    block_spreads[0].start()
    place_spreads[1].arrived()
    block_spreads[0].arrived()
    block_spreads[1].start()
    row = jnp.zeros((1, 128), I32)
    lane = lanes_of((1, 128))
    for number in range(n_box * n_node):
        row = jnp.where(lane == number, places[number // here.line, number % here.line], row)
    places_out[...] = row
    block_spreads[1].arrived()
    kept.append(keep(blocks, blocks_out, 5))
    arrived(halo_x)
    copies.finish()
    for copy in kept:
        copy.wait()
    for sent in fine_swaps + coarse_swaps + [*place_spreads, *block_spreads]:
        sent.finish()


def bottom_kernel(
    n_box, n_node, rows_x, rows_y, places, reach, blocks_in, out, blocks, scale, source, first, second, hits, sems
):
    deep, wide, long = reach.shape
    count = n_box * n_node
    per_side = long // 8
    side_bits = per_side.bit_length() - 1
    box, node = lax.axis_index("box"), lax.axis_index("node")
    at_x, at_y = box * rows_x - HALO, node * rows_y - Y_HALO
    fills = [
        pltpu.make_async_copy(
            reach.at[:, :, 128 * half : 128 * (half + 1)],
            scale.at[half, pl.ds(8, deep)],
            sems.at[half],
        )
        for half in range(2)
    ]
    fills.append(pltpu.make_async_copy(blocks_in, blocks, sems.at[2]))
    for copy in fills:
        copy.start()
    zeros = jnp.zeros((wide, 128), F32)

    def clear(x, carry):
        for half in range(2):
            source[half, x] = zeros
            first[half, x] = zeros
        return carry

    lax.fori_loop(8, 8 + deep, clear, 0, unroll=2)
    out[...] = jnp.zeros(out.shape, F32)

    def where_is(number):
        place = places[0, number]
        return (
            (place >> 2 * side_bits << 3) - at_x,
            ((place >> side_bits & per_side - 1) << 3) - at_y,
            place & per_side - 1,
        )

    def look(number, found):
        x, y, _ = where_is(number)
        hits[found] = number
        hit = (x > -8) & (x < deep) & (y >= 0) & (y < wide)
        return found + hit.astype(I32)

    found = lax.fori_loop(0, count, look, jnp.int32(0), unroll=8)

    for copy in fills:
        copy.wait()

    def empty(x, carry):
        for half in range(2):
            scale[half, x] = zeros
        return carry

    lax.fori_loop(8, 8 + jnp.maximum(-at_x, 0), empty, 0)
    lax.fori_loop(8 + jnp.minimum(rows_x * n_box - at_x, deep), 8 + deep, empty, 0)

    def empty_rows(start):
        def one(x, carry):
            for half in range(2):
                scale[half, x, start : start + Y_HALO] = jnp.zeros((Y_HALO, 128), F32)
            return carry

        lax.fori_loop(8, 8 + deep, one, 0)

    pl.when(node == 0)(lambda: empty_rows(0))
    pl.when(node == n_node - 1)(lambda: empty_rows(Y_HALO + rows_y))

    lane, row = lanes_of((8, 128)), rows_of((8, 128))

    def put(at, carry):
        number = hits[at]
        x, y, z = where_is(number)
        block = blocks[number]
        kept = (lane >> 2) == z
        rows = pl.ds(pl.multiple_of(y, 8), 8)
        spots = [(half, x + ix + 8, rows) for half in range(2) for ix in range(8)]
        before = [source[spot] for spot in spots]
        first_before = [first[spot] for spot in spots]
        scales = [scale[spot] for spot in spots]
        whole = jnp.concatenate([block, pltpu.roll(block, 64, 1)], axis=0)
        fresh = []
        for half in range(2):
            for ix in range(8):
                shift = (z << 2) + 128 - 4 * half - 8 * ix & 127
                fresh.append(jnp.where(kept, pltpu.roll(whole, shift, 1), 0.0))
        for number, spot in enumerate(spots):
            source[spot] = before[number] + fresh[number]
            first[spot] = first_before[number] + fresh[number] * scales[number]
        return carry

    lax.fori_loop(0, found, put, 0)

    refs = (first, second)
    eight = (8, 128)
    lane = lanes_of(eight)
    for sweep_no in range(HALO):
        left = HALO - 1 - sweep_no
        margin = (left + 3) // 4 * 4
        low = Y_HALO - margin
        here, there = refs[sweep_no % 2], refs[(sweep_no + 1) % 2]

        def planes(group, carry):
            fresh = []
            for number in range(AT_ONCE):
                x = 8 + HALO - left + AT_ONCE * group + number
                for at in range(low, low + rows_y + 2 * margin, 8):
                    cut = slice(at, at + 8)
                    mids = [here[half, x, cut, :] for half in range(2)]
                    turned = (
                        jnp.where(lane == 0, 0.0, pltpu.roll(mids[1], 1, 1)),
                        jnp.where(lane == 127, 0.0, pltpu.roll(mids[0], 127, 1)),
                    )
                    for half in range(2):
                        around = here[half, x - 1, cut, :] + here[half, x + 1, cut, :]
                        around += here[half, x, at - 1 : at + 7, :]
                        around += here[half, x, at + 1 : at + 9, :]
                        around += mids[1 - half] + turned[half]
                        value = 0.2 * mids[half] + scale[half, x, cut, :] * (
                            source[half, x, cut, :] + around
                        )
                        fresh.append((half, x, cut, value))
            for half, x, cut, value in fresh:
                there[half, x, cut, :] = value
            return carry

        lax.fori_loop(0, (rows_x + 2 * left + AT_ONCE - 1) // AT_ONCE, planes, 0)
    solved = refs[HALO % 2]

    def take(at, carry):
        number = hits[at]
        x, y, z = where_is(number)

        @pl.when((x == HALO) & (y >= Y_HALO) & (y < Y_HALO + rows_y))
        def _():
            rows = pl.ds(pl.multiple_of(y, 8), 8)
            back = 128 - (z << 2)
            gathered = jnp.zeros(eight, F32)
            for ix in range(8):
                for half in range(2):
                    turned = pltpu.roll(
                        solved[half, 8 + HALO + ix, rows, :], back + 4 * half + 8 * ix & 127, 1
                    )
                    gathered = jnp.where((lane >> 2) == 2 * ix + half, turned, gathered)
            late = pltpu.roll(gathered, 64, 1)
            out[number] = jnp.where(lanes_of((4, 128)) < 64, gathered[0:4], late[4:8])

        return carry

    lax.fori_loop(0, found, take, 0)


def up_kernel(
    n_box,
    n_node,
    parts_in,
    fine_u_in,
    fine_c_in,
    fine_b_in,
    count_ref,
    nbr_in,
    cover_in,
    coarse_u_in,
    coarse_b_in,
    coarse_c_in,
    coarse_nbr_in,
    fine_to,
    coarse_to,
    fine_out,
    coarse_out,
    output_sems,
    fine_u,
    fine_c,
    fine_b,
    fine_nbr,
    cover_ref,
    coarse_u,
    coarse_b,
    coarse_c,
    coarse_nbr,
    own_parts,
    input_sems,
    from_core,
    sum_core,
    from_chips,
    own_block,
    cu_first,
    cu_second,
    yz_coarse_0,
    x_coarse_0,
    yz_coarse_1,
    x_coarse_1,
    octants,
    picked,
    u_first,
    u_second,
    fine_sum,
    coarse_sum,
    yz_fine_0,
    x_fine_0,
    yz_fine_1,
    x_fine_1,
    send_sems,
    recv_sems,
    fine_sent,
    fine_came,
    coarse_sent,
    coarse_came,
    spread_sent,
    spread_came,
):
    here = Place(n_box, n_node)
    copies = Copies(send_sems, recv_sems)
    boxes = fine_u.shape[0]
    inputs = [
        pltpu.make_async_copy(source, target, input_sems.at[number])
        for number, (source, target) in enumerate(
            (
                (parts_in.at[:, pl.ds(0, n_node)], own_parts),
                (coarse_u_in, coarse_u),
                (coarse_b_in, coarse_b),
                (coarse_c_in, coarse_c),
                (coarse_nbr_in, coarse_nbr),
                (nbr_in, fine_nbr),
                (cover_in, cover_ref),
                (fine_u_in, fine_u),
                (fine_c_in, fine_c),
                (fine_b_in, fine_b),
            )
        )
    ]
    for copy in inputs:
        copy.start()
    fine_swaps = [
        Swap(here, yz, x, boxes, 2, fine_sent.at[number], fine_came.at[number])
        for number, (yz, x) in enumerate(((yz_fine_0, x_fine_0), (yz_fine_1, x_fine_1)))
    ]
    coarse_swaps = [
        Swap(here, yz, x, 1, 1, coarse_sent.at[number], coarse_came.at[number])
        for number, (yz, x) in enumerate(((yz_coarse_0, x_coarse_0), (yz_coarse_1, x_coarse_1)))
    ]
    here.greet([here.mate()], True)
    here.greeted()

    from_mate = copies.start(parts_in.at[:, pl.ds(n_node, n_node)], from_core, here.mate())
    for copy in inputs:
        copy.wait()
    arrived([from_mate])
    sum_core[...] = own_parts[...] + from_core[...]
    x_bits = n_node.bit_length() - 1
    spread = Spread(
        here.chips,
        lambda step: sum_core.at[step >> x_bits, step & n_node - 1],
        lambda step: from_chips.at[step],
        from_chips.at[pl.ds(1, here.chips - 1)],
        here.before_chip,
        spread_sent,
        spread_came,
    )
    from_chips[0] = sum_core[0, 0]
    spread.start()
    grow_quarter = one_hot_of(
        (128, 1024), lambda r, l: r == (l >> 7 << 3) + (l >> 3 & 3) + (l >> 2 & 1) * 4
    )
    spread.arrived()
    block = jnp.sum(from_chips[...], axis=0)
    own_block[0:4] = block
    own_block[4:8] = pltpu.roll(block, 64, 1)
    grown = pick_right(swap_eights(own_block[...]), grow_quarter)
    grown = pick_left(one_hot_of((32, 8), lambda r, l: r >> 2 == l), grown)
    cu_first[0] = coarse_u[0] + grown
    put_faces(tiles_of(cu_first, 0), yz_coarse_0, x_coarse_0, 1)
    coarse_swaps[0].start(0)
    inside_boxes(1, cu_first, coarse_b, coarse_sum)
    coarse_swaps[0].arrived()
    sweep_boxes(
        1, cu_first, coarse_sum, coarse_c, coarse_swaps[0], coarse_nbr, cu_second, coarse_swaps[1]
    )
    split = one_hot_of(
        (512, 512),
        lambda r, l: (l >> 8 == (r >> 4 & 1)) & ((l >> 4 & 15) == r >> 5) & ((l & 15) == (r & 15)),
    )
    inside_boxes(1, cu_second, coarse_b, coarse_sum)
    coarse_swaps[1].arrived()
    sweep_boxes(
        1, cu_second, coarse_sum, coarse_c, coarse_swaps[1], coarse_nbr, coarse_out, None
    )
    coarse_store = Store(coarse_out, coarse_to, 1, 1, output_sems.at[pl.ds(boxes // 2, 1)])
    coarse_store.start(0)

    quarters = jnp.concatenate(
        [
            coarse_out[0, 16 * (k // 2) : 16 * (k // 2) + 16, 512 * (k % 2) : 512 * (k % 2) + 512]
            for k in range(4)
        ],
        axis=0,
    )
    cubes = pick_right(quarters, split)
    base = pl.multiple_of(here.node * 8, 8)
    for k in range(8):
        octants[base + k] = cubes[16 * (k // 2) : 16 * (k // 2) + 16, 256 * (k % 2) : 256 * (k % 2) + 256]
    own = octants.at[pl.ds(base, 8)]
    waits = [copies.start(own, own, device) for _, device in here.peers_node()]
    grow_yz = one_hot_of(
        (256, 1024), lambda r, l: (l >> 6 == r >> 4) & ((l >> 1 & 15) == (r & 15))
    )
    grow_x = one_hot_of((32 * boxes, 16 * boxes), lambda r, l: r >> 1 == l)
    arrived(waits)
    for box in range(boxes):
        picked[16 * box : 16 * (box + 1)] = octants[cover_ref[0, box]]
    tall = pick_right(pick_left(grow_x, picked[...]), grow_yz)
    for box in range(boxes):
        u_first[box] = fine_u[box] + tall[32 * box : 32 * (box + 1)]

    def faces_of(box, carry):
        put_faces(tiles_of(u_first, box), yz_fine_0, x_fine_0, boxes + box)

    by_chunks(boxes, fine_swaps[0], faces_of)
    inside_boxes(boxes, u_first, fine_b, fine_sum)
    fine_swaps[0].arrived()
    sweep_boxes(
        boxes, u_first, fine_sum, fine_c, fine_swaps[0], fine_nbr, u_second, fine_swaps[1]
    )
    inside_boxes(boxes, u_second, fine_b, fine_sum)
    fine_swaps[1].arrived()
    live = count_ref[0, 0]
    fine_store = Store(fine_out, fine_to, boxes, 2, output_sems)
    sweep_boxes(
        boxes,
        u_second,
        fine_sum,
        fine_c,
        fine_swaps[1],
        fine_nbr,
        fine_out,
        None,
        lambda box: jnp.where(box < live, 1.0, 0.0).astype(F32),
        fine_store,
    )
    copies.finish()
    for sent in fine_swaps + coarse_swaps + [spread, fine_store, coarse_store]:
        sent.finish()


def hand_on_kernel(fine_from, coarse_from, fine_to, coarse_to, fine_held, coarse_held, came, sent):
    boxes = fine_from.shape[0]
    paths = [
        (fine_from.at[box], fine_held.at[box], fine_to.at[box], came.at[box], sent.at[box])
        for box in range(boxes)
    ]
    paths.append((coarse_from, coarse_held, coarse_to, came.at[boxes], sent.at[boxes]))
    ins = [pltpu.make_async_copy(a, b, sem) for a, b, _, sem, _ in paths]
    outs = [pltpu.make_async_copy(b, c, sem) for _, b, c, _, sem in paths]
    for copy in ins:
        copy.start()
    for coming, going in zip(ins, outs):
        coming.wait()
        going.start()
    for copy in outs:
        copy.wait()


VMEM, SMEM, ANY = (
    pl.BlockSpec(memory_space=pltpu.VMEM),
    pl.BlockSpec(memory_space=pltpu.SMEM),
    pl.BlockSpec(memory_space=pl.ANY),
)


def shards(
    n_box,
    n_node,
    fine_rhs,
    fine_diag,
    fine_count,
    fine_nbr,
    fine_cover,
    coarse_source,
    coarse_diag,
    coarse_nbr,
    coarse_place,
    bottom_diag,
):
    boxes = fine_rhs.shape[0]
    ny, nz, nc = grid_of(n_box)
    rows_x, rows_y, long = bottom_diag.shape
    deep, wide = rows_x + 2 * HALO, rows_y + 2 * Y_HALO
    count = n_box * n_node

    def like(shape, kind=F32):
        return jax.ShapeDtypeStruct(shape, kind)

    fine, coarse = (boxes, 32, 1024), (1, 32, 1024)
    line = nc * n_node
    grid = (ny * nz, line)
    limit = 62 * 1024 * 1024
    fine_u, fine_c, coarse_u, coarse_b, coarse_c, reach, blocks, places = pl.pallas_call(
        functools.partial(down_kernel, n_box, n_node),
        out_shape=(
            like(fine),
            like(fine),
            like(coarse),
            like(coarse),
            like(coarse),
            like((deep, wide, long)),
            like(grid + (4, 128)),
            like((1, 128), I32),
        ),
        in_specs=[ANY, ANY, SMEM, ANY, ANY, ANY, ANY, ANY, SMEM, ANY],
        out_specs=(ANY, ANY, ANY, ANY, ANY, ANY, ANY, VMEM),
        scratch_shapes=[
            pltpu.VMEM(fine, F32),
            pltpu.VMEM(fine, F32),
            pltpu.VMEM(coarse, F32),
            pltpu.VMEM(coarse, F32),
            pltpu.VMEM(coarse, F32),
            pltpu.SMEM((boxes, 6), I32),
            pltpu.SMEM((1, boxes), I32),
            pltpu.SMEM((1, 6), I32),
            pltpu.VMEM(fine, F32),
            pltpu.VMEM(fine, F32),
            pltpu.VMEM(coarse, F32),
            pltpu.VMEM(coarse, F32),
            pltpu.VMEM((rows_x, rows_y, long), F32),
            pltpu.VMEM(fine, F32),
            pltpu.VMEM(fine, F32),
            pltpu.VMEM(coarse, F32),
            pltpu.VMEM((3 * boxes, 32, 128), F32),
            pltpu.VMEM((3 * boxes, 2, 1024), F32),
            pltpu.VMEM((3 * boxes, 32, 128), F32),
            pltpu.VMEM((3 * boxes, 2, 1024), F32),
            pltpu.VMEM((rows_x, rows_y, long), F32),
            pltpu.VMEM((32 * boxes, 1024), F32),
            pltpu.VMEM((boxes, 16, 256), F32),
            pltpu.VMEM((8 * n_node, 16, 256), F32),
            pltpu.VMEM((n_node - 1, 8, 16, 256), F32),
            pltpu.SMEM((8 * n_node,), I32),
            pltpu.VMEM(coarse, F32),
            pltpu.VMEM((3, 32, 128), F32),
            pltpu.VMEM((3, 2, 1024), F32),
            pltpu.VMEM((3, 32, 128), F32),
            pltpu.VMEM((3, 2, 1024), F32),
            pltpu.VMEM(grid + (4, 128), F32),
            pltpu.VMEM(grid + (1, 128), I32),
            pltpu.SemaphoreType.DMA((64,)),
            pltpu.SemaphoreType.DMA((64,)),
            pltpu.SemaphoreType.DMA,
            pltpu.SemaphoreType.DMA((2, boxes)),
            pltpu.SemaphoreType.DMA((6,)),
            pltpu.SemaphoreType.DMA((6,)),
            pltpu.SemaphoreType.DMA((2, boxes // 2, 4)),
            pltpu.SemaphoreType.DMA((2, boxes // 2, 4)),
            pltpu.SemaphoreType.DMA((2, 1, 4)),
            pltpu.SemaphoreType.DMA((2, 1, 4)),
            pltpu.SemaphoreType.DMA((2, 2)),
            pltpu.SemaphoreType.DMA((2, 2)),
        ],
        compiler_params=pltpu.CompilerParams(
            collective_id=0, has_side_effects=True, vmem_limit_bytes=limit
        ),
        name="down",
    )(
        fine_rhs,
        fine_diag,
        fine_count,
        fine_nbr,
        fine_cover,
        coarse_source,
        coarse_diag,
        coarse_nbr,
        coarse_place,
        bottom_diag,
    )
    parts = pl.pallas_call(
        functools.partial(bottom_kernel, n_box, n_node, rows_x, rows_y),
        out_shape=like((count, 4, 128)),
        in_specs=[SMEM, ANY, ANY],
        out_specs=VMEM,
        scratch_shapes=[
            pltpu.VMEM((count, 4, 128), F32),
            pltpu.VMEM((2, deep + 16, wide, 128), F32),
            pltpu.VMEM((2, deep + 16, wide, 128), F32),
            pltpu.VMEM((2, deep + 16, wide, 128), F32),
            pltpu.VMEM((2, deep + 16, wide, 128), F32),
            pltpu.SMEM((count + 1,), I32),
            pltpu.SemaphoreType.DMA((3,)),
        ],
        compiler_params=pltpu.CompilerParams(vmem_limit_bytes=limit),
        name="bottom",
    )(places, reach, blocks.reshape(count, 4, 128))
    fine_out, coarse_out = pl.pallas_call(
        functools.partial(up_kernel, n_box, n_node),
        out_shape=(like(fine), like(coarse)),
        in_specs=[ANY, ANY, ANY, ANY, SMEM, ANY, ANY, ANY, ANY, ANY, ANY],
        out_specs=(ANY, ANY),
        scratch_shapes=[
            pltpu.VMEM(fine, F32),
            pltpu.VMEM(coarse, F32),
            pltpu.SemaphoreType.DMA((boxes // 2 + 1,)),
            pltpu.VMEM(fine, F32),
            pltpu.VMEM(fine, F32),
            pltpu.VMEM(fine, F32),
            pltpu.SMEM((boxes, 6), I32),
            pltpu.SMEM((1, boxes), I32),
            pltpu.VMEM(coarse, F32),
            pltpu.VMEM(coarse, F32),
            pltpu.VMEM(coarse, F32),
            pltpu.SMEM((1, 6), I32),
            pltpu.VMEM((ny * nz, n_node, 4, 128), F32),
            pltpu.SemaphoreType.DMA((10,)),
            pltpu.VMEM((ny * nz, n_node, 4, 128), F32),
            pltpu.VMEM((ny * nz, n_node, 4, 128), F32),
            pltpu.VMEM((ny * nz * n_node, 4, 128), F32),
            pltpu.VMEM((8, 128), F32),
            pltpu.VMEM(coarse, F32),
            pltpu.VMEM(coarse, F32),
            pltpu.VMEM((3, 32, 128), F32),
            pltpu.VMEM((3, 2, 1024), F32),
            pltpu.VMEM((3, 32, 128), F32),
            pltpu.VMEM((3, 2, 1024), F32),
            pltpu.VMEM((8 * n_node, 16, 256), F32),
            pltpu.VMEM((16 * boxes, 256), F32),
            pltpu.VMEM(fine, F32),
            pltpu.VMEM(fine, F32),
            pltpu.VMEM(fine, F32),
            pltpu.VMEM(coarse, F32),
            pltpu.VMEM((3 * boxes, 32, 128), F32),
            pltpu.VMEM((3 * boxes, 2, 1024), F32),
            pltpu.VMEM((3 * boxes, 32, 128), F32),
            pltpu.VMEM((3 * boxes, 2, 1024), F32),
            pltpu.SemaphoreType.DMA((8,)),
            pltpu.SemaphoreType.DMA((8,)),
            pltpu.SemaphoreType.DMA((2, boxes // 2, 4)),
            pltpu.SemaphoreType.DMA((2, boxes // 2, 4)),
            pltpu.SemaphoreType.DMA((2, 1, 4)),
            pltpu.SemaphoreType.DMA((2, 1, 4)),
            pltpu.SemaphoreType.DMA,
            pltpu.SemaphoreType.DMA,
        ],
        compiler_params=pltpu.CompilerParams(
            collective_id=1, has_side_effects=True, vmem_limit_bytes=limit
        ),
        name="up",
    )(
        parts.reshape(grid + (4, 128)),
        fine_u,
        fine_c,
        fine_rhs,
        fine_count,
        fine_nbr,
        fine_cover,
        coarse_u,
        coarse_b,
        coarse_c,
        coarse_nbr,
    )
    return pl.pallas_call(
        hand_on_kernel,
        out_shape=(like(fine), like(coarse)),
        in_specs=[ANY, ANY],
        out_specs=(ANY, ANY),
        scratch_shapes=[
            pltpu.VMEM(fine, F32),
            pltpu.VMEM(coarse, F32),
            pltpu.SemaphoreType.DMA((boxes + 1,)),
            pltpu.SemaphoreType.DMA((boxes + 1,)),
        ],
        compiler_params=pltpu.CompilerParams(vmem_limit_bytes=limit),
        name="hand_on",
    )(fine_out, coarse_out)


def solution(mesh):
    n_box, n_node = mesh.shape["box"], mesh.shape["node"]
    return jax.shard_map(
        functools.partial(shards, n_box, n_node),
        mesh=mesh,
        in_specs=(
            P(("box", "node"), None, None),
            P(("box", "node"), None, None),
            P("box", "node"),
            P(("box", "node"), None),
            P("box", "node"),
            P(("box", "node"), None, None),
            P(("box", "node"), None, None),
            P(("box", "node"), None),
            P(("box", "node")),
            P("box", "node", None),
        ),
        out_specs=(P(("box", "node"), None, None), P(("box", "node"), None, None)),
        check_vma=False,
    )
```

```python
import functools

import jax
import jax.numpy as jnp
from jax import lax
from jax.experimental import pallas as pl
from jax.experimental.pallas import tpu as pltpu
from jax.sharding import PartitionSpec as P

F32, BF16, I32 = jnp.float32, jnp.bfloat16, jnp.int32
MESH = pl.DeviceIdType.MESH
BOT_ITERS = 12
HALO = BOT_ITERS - 1
Y_HALO = 16
AT_ONCE = 6
TILES = 8


def grid_of(n_box):
    return {32: (4, 4, 2), 8: (2, 2, 2)}[n_box]


def lanes_of(shape):
    return lax.broadcasted_iota(I32, shape, len(shape) - 1)


def rows_of(shape):
    return lax.broadcasted_iota(I32, shape, len(shape) - 2)


def thirds(a):
    high = a.astype(BF16)
    rest = a - high.astype(F32)
    middle = rest.astype(BF16)
    low = (rest - middle.astype(F32)).astype(BF16)
    return high, middle, low


def pick_right(a, one_hot):
    high, middle, low = [jnp.dot(t, one_hot, preferred_element_type=F32) for t in thirds(a)]
    return high + (middle + low)


def pick_left(one_hot, a):
    high, middle, low = [jnp.dot(one_hot, t, preferred_element_type=F32) for t in thirds(a)]
    return high + (middle + low)


def one_hot_of(shape, test):
    return jnp.where(test(rows_of(shape), lanes_of(shape)), 1.0, 0.0).astype(BF16)


def roll_lanes(a, shift):
    shift = shift % 128
    return a if shift == 0 else pltpu.roll(a, shift, 1)


def tiles_of(ref, box):
    return [ref[box, :, 128 * t : 128 * (t + 1)] for t in range(TILES)]


def pack_faces(tiles):
    lane = lanes_of((32, 128))
    within, quarter = lane & 31, lane >> 5
    first, last = tiles[0], tiles[-1]
    packed = jnp.where(
        quarter == 0,
        first,
        jnp.where(
            quarter == 1,
            roll_lanes(first, 48),
            jnp.where(quarter == 2, roll_lanes(last, -16), last),
        ),
    )
    for t in range(TILES):
        packed = jnp.where((within >> 1) == t, roll_lanes(tiles[t], 2 * t + 1), packed)
    return packed


def put_faces(tiles, yz_ref, x_ref, slot):
    yz_ref[slot] = pack_faces(tiles)
    for t in range(TILES):
        x_ref[slot, 0:1, 128 * t : 128 * (t + 1)] = tiles[t][0:1, :]
        x_ref[slot, 1:2, 128 * t : 128 * (t + 1)] = tiles[t][31:32, :]


def ghosts_of(yz_ref, x_ref, nbr_ref, box):
    def chosen(ref, face):
        which = nbr_ref[box, face]
        kept = jnp.where(which >= 0, 1.0, 0.0).astype(F32)
        return ref[jnp.maximum(which, 0)], kept

    def tile(face):
        value, kept = chosen(yz_ref, face)
        return value * kept

    x_low, low_kept = chosen(x_ref, 0)
    x_high, high_kept = chosen(x_ref, 1)
    return (
        x_low[1:2] * low_kept,
        x_high[0:1] * high_kept,
        tile(2),
        tile(3),
        tile(4),
        tile(5),
    )


def beside_inside(tiles):
    lane, row = lanes_of((32, 128)), rows_of((32, 128))
    within = lane & 31
    nothing = jnp.zeros((32, 128), F32)
    ups = [nothing] + [roll_lanes(t, 32) for t in tiles]
    downs = [roll_lanes(t, 96) for t in tiles] + [nothing]
    sums = []
    for t in range(TILES):
        along_x = jnp.where(row == 0, 0.0, pltpu.roll(tiles[t], 1, 0)) + jnp.where(
            row == 31, 0.0, pltpu.roll(tiles[t], 31, 0)
        )
        along_y = jnp.where(lane < 32, ups[t], ups[t + 1]) + jnp.where(
            lane >= 96, downs[t + 1], downs[t]
        )
        along_z = jnp.where(within == 0, 0.0, roll_lanes(tiles[t], 1)) + jnp.where(
            within == 31, 0.0, roll_lanes(tiles[t], 127)
        )
        sums.append(along_x + along_y + along_z)
    return sums


def with_ghosts(sums, ghosts):
    x_low, x_high, y_low, y_high, z_low, z_high = ghosts
    lane, row = lanes_of((32, 128)), rows_of((8, 128))
    within = lane & 31
    below = jnp.where(within < 16, roll_lanes(y_low, 48), roll_lanes(y_low, 32))
    above = jnp.where(within < 16, roll_lanes(y_high, 48), roll_lanes(y_high, 96))
    both = jnp.where((lane & 1) == 0, z_low, roll_lanes(z_high, 62))
    edge = (within == 0) | (within == 31)
    full = []
    for t in range(TILES):
        cut = slice(128 * t, 128 * (t + 1))
        value = sums[t] + jnp.where(edge, roll_lanes(both, -32 - 2 * t), 0.0)
        if t == 0:
            value += jnp.where(lane < 32, below, 0.0)
        if t == TILES - 1:
            value += jnp.where(lane >= 96, above, 0.0)
        full.append(
            jnp.concatenate(
                [
                    value[0:8] + jnp.where(row == 0, x_low[:, cut], 0.0),
                    value[8:24],
                    value[24:32] + jnp.where(row == 7, x_high[:, cut], 0.0),
                ],
                axis=0,
            )
        )
    return full


def fan_out(value, step):
    row = rows_of((8, 128))
    for bit in (1, 2, 4):
        value = jnp.where((row & bit) != 0, roll_lanes(value, step * bit), value)
    return value


def swap_eights(value):
    lane = lanes_of((8, 128))
    result = jnp.zeros((8, 128), F32)
    for b in range(8):
        spread = fan_out(jnp.broadcast_to(value[b : b + 1], (8, 128)), -8)
        result = jnp.where((lane >> 3) == b, roll_lanes(spread, 8 * b), result)
    return result


class Copies:
    def __init__(self, send_sems, recv_sems):
        self.send_sems, self.recv_sems, self.made = send_sems, recv_sems, []

    def start(self, source, target, device):
        number = len(self.made)
        copy = pltpu.make_async_remote_copy(
            src_ref=source,
            dst_ref=target,
            send_sem=self.send_sems.at[number],
            recv_sem=self.recv_sems.at[number],
            device_id=device,
            device_id_type=MESH,
        )
        copy.start()
        self.made.append(copy)
        return copy

    def finish(self):
        for copy in self.made:
            copy.wait_send()


def arrived(copies):
    for copy in copies:
        copy.wait_recv()


class Place:
    def __init__(self, n_box, n_node):
        self.n_box, self.n_node = n_box, n_node
        self.ny, self.nz, self.nc = grid_of(n_box)
        self.box, self.node = lax.axis_index("box"), lax.axis_index("node")
        self.line, self.sheet = self.nc * n_node, self.ny * self.nz
        self.chips = self.sheet * n_node
        self.core = self.box & 1
        self.z = (self.box >> 1) & (self.nz - 1)
        self.y = (self.box >> 1) >> (self.nz.bit_length() - 1)

    def along_line(self, step):
        total = self.n_box * self.n_node
        other = (self.box * self.n_node + self.node + step + total) % total
        return (other // self.n_node, other % self.n_node)

    def next_node(self, step):
        return (self.node + step + self.n_node) % self.n_node

    def at_node(self, step):
        return (self.box, self.next_node(step))

    def at_box(self, step):
        return ((self.box + step + self.n_box) % self.n_box, self.node)

    def mate(self):
        return (self.box ^ 1, self.node)

    def at_line(self, step, sign):
        x_bits = self.n_node.bit_length() - 1
        x = (self.node + sign * (step & self.n_node - 1)) & (self.n_node - 1)
        return (self.box ^ (step >> x_bits), x)

    def at_sheet(self, step, sign):
        z_bits = self.nz.bit_length() - 1
        z = (self.z + sign * (step & self.nz - 1)) & (self.nz - 1)
        y = (self.y + sign * (step >> z_bits)) & (self.ny - 1)
        return ((y * self.nz + z) * self.nc + self.core, self.node)

    def before_chip(self, step):
        x_bits = self.n_node.bit_length() - 1
        z_bits = self.nz.bit_length() - 1
        x = (self.node - (step & self.n_node - 1)) & (self.n_node - 1)
        z = (self.z - (step >> x_bits & self.nz - 1)) & (self.nz - 1)
        y = (self.y - (step >> x_bits + z_bits)) & (self.ny - 1)
        return ((y * self.nz + z) * self.nc + self.core, x)

    def peers_node(self):
        for step in range(1, self.n_node):
            yield self.next_node(step), self.at_node(step)

    def greet(self, more, all_chips=False):
        peers = [self.along_line(1), self.along_line(-1)] + more
        barrier = pltpu.get_barrier_semaphore()
        for device in peers:
            pl.semaphore_signal(barrier, inc=1, device_id=device, device_id_type=MESH)

        def chip(step, carry):
            device = self.before_chip(step)
            pl.semaphore_signal(barrier, inc=1, device_id=device, device_id_type=MESH)
            return carry

        if all_chips:
            lax.fori_loop(1, self.chips, chip, 0, unroll=7)
        self.peer_count = len(peers) + (self.chips - 1 if all_chips else 0)

    def greeted(self):
        pl.semaphore_wait(pltpu.get_barrier_semaphore(), self.peer_count)


class Swap:
    def __init__(self, here, yz_ref, x_ref, boxes, step, send_sems, recv_sems):
        self.here, self.refs, self.boxes, self.step = here, (yz_ref, x_ref), boxes, step
        self.send_sems, self.recv_sems = send_sems, recv_sems

    def copies(self, chunk):
        made = []
        for number in range(4):
            ref, later = self.refs[number // 2], 2 * (number % 2)
            at = chunk * self.step
            made.append(
                pltpu.make_async_remote_copy(
                    src_ref=ref.at[pl.ds(self.boxes + at, self.step)],
                    dst_ref=ref.at[pl.ds(later * self.boxes + at, self.step)],
                    send_sem=self.send_sems.at[chunk, number],
                    recv_sem=self.recv_sems.at[chunk, number],
                    device_id=self.here.along_line(1 - later),
                    device_id_type=MESH,
                )
            )
        return made

    def start(self, chunk):
        for copy in self.copies(chunk):
            copy.start()

    def arrived(self):
        for chunk in range(self.boxes // self.step):
            for copy in self.copies(chunk):
                copy.wait_recv()

    def finish(self):
        for chunk in range(self.boxes // self.step):
            for copy in self.copies(chunk):
                copy.wait_send()


def by_chunks(boxes, swap, one):
    step = min(boxes, 2)

    def some(chunk, carry):
        for number in range(step):
            one(chunk * step + number, 0)
        if swap is not None and swap.step == step:
            swap.start(chunk)
        return carry

    lax.fori_loop(0, boxes // step, some, 0)


class Store:
    def __init__(self, source, target, boxes, step, sems):
        self.source, self.target, self.boxes, self.step = source, target, boxes, step
        self.sems = sems

    def copy(self, chunk):
        part = pl.ds(chunk * self.step, self.step)
        return pltpu.make_async_copy(
            self.source.at[part], self.target.at[part], self.sems.at[chunk]
        )

    def start(self, chunk):
        self.copy(chunk).start()

    def finish(self):
        for chunk in range(self.boxes // self.step):
            self.copy(chunk).wait()


class Spread:
    def __init__(self, count, source, target, landed, device, send_sem, recv_sem):
        self.count, self.source, self.target, self.device = count, source, target, device
        self.landed, self.send_sem, self.recv_sem = landed, send_sem, recv_sem

    def copy(self, source, target, device):
        return pltpu.make_async_remote_copy(
            src_ref=source,
            dst_ref=target,
            send_sem=self.send_sem,
            recv_sem=self.recv_sem,
            device_id=device,
            device_id_type=MESH,
        )

    def start(self):
        def one(step, carry):
            self.copy(self.source(step), self.target(step), self.device(step)).start()
            return carry

        lax.fori_loop(1, self.count, one, 0, unroll=7 if self.count > 16 else self.count - 1)

    def whole(self):
        return self.copy(self.landed, self.landed, self.device(1))

    def arrived(self):
        self.whole().wait_recv()

    def finish(self):
        self.whole().wait_send()


def write_to_all(here, ref, send_sems, recv_sems):
    return (
        Spread(
            here.line,
            lambda step: ref.at[0, 0],
            lambda step: ref.at[0, step],
            ref.at[0, pl.ds(1, here.line - 1)],
            lambda step: here.at_line(step, 1),
            send_sems.at[0],
            recv_sems.at[0],
        ),
        Spread(
            here.sheet,
            lambda step: ref.at[0],
            lambda step: ref.at[step],
            ref.at[pl.ds(1, here.sheet - 1)],
            lambda step: here.at_sheet(step, 1),
            send_sems.at[1],
            recv_sems.at[1],
        ),
    )


def write_tiles(ref, box, tiles):
    for t in range(TILES):
        ref[box, :, 128 * t : 128 * (t + 1)] = tiles[t]


def first_sweep(boxes, u_ref, b_ref, d_ref, c_ref, swap, ready=None):
    def one(box, carry):
        if ready is not None:
            ready(box)
        scales, tiles = [], []
        for t in range(TILES):
            cut = slice(128 * t, 128 * (t + 1))
            scales.append(0.8 / (6.0 + d_ref[box, :, cut]))
            tiles.append(scales[t] * b_ref[box, :, cut])
        write_tiles(c_ref, box, scales)
        write_tiles(u_ref, box, tiles)
        put_faces(tiles, *swap.refs, boxes + box)

    by_chunks(boxes, swap, one)


def inside_boxes(boxes, u_ref, b_ref, sum_ref):
    def one(box, carry):
        tiles = tiles_of(u_ref, box)
        sums = beside_inside(tiles)
        sources = tiles_of(b_ref, box)
        write_tiles(sum_ref, box, [sources[t] + sums[t] for t in range(TILES)])

    by_chunks(boxes, None, one)


def sweep_boxes(
    boxes, u_ref, sum_ref, c_ref, came, nbr_ref, out_ref, swap, keep=None, store=None
):
    yz_from, x_from = came.refs

    def one(box, carry):
        tiles = tiles_of(u_ref, box)
        sums = with_ghosts(tiles_of(sum_ref, box), ghosts_of(yz_from, x_from, nbr_ref, box))
        fresh = []
        for t in range(TILES):
            cut = slice(128 * t, 128 * (t + 1))
            fresh.append(0.2 * tiles[t] + c_ref[box, :, cut] * sums[t])
        if keep is not None:
            kept = keep(box)
            fresh = [t * kept for t in fresh]
        write_tiles(out_ref, box, fresh)
        if swap is not None:
            put_faces(fresh, *swap.refs, boxes + box)

    by_chunks(boxes, store if swap is None else swap, one)


def residual_boxes(boxes, u_ref, sum_ref, d_ref, came, nbr_ref, r_ref, keep=None):
    yz_from, x_from = came.refs

    def one(box, carry):
        tiles = tiles_of(u_ref, box)
        sums = with_ghosts(tiles_of(sum_ref, box), ghosts_of(yz_from, x_from, nbr_ref, box))
        rests = []
        for t in range(TILES):
            cut = slice(128 * t, 128 * (t + 1))
            left = sums[t] - (6.0 + d_ref[box, :, cut]) * tiles[t]
            rests.append(left if keep is None else left * keep(box))
        for t in range(TILES):
            r_ref[pl.ds(pl.multiple_of(box * 32, 32), 32), 128 * t : 128 * (t + 1)] = rests[t]

    by_chunks(boxes, None, one)


def down_kernel(
    n_box,
    n_node,
    fine_b_in,
    fine_d_in,
    count_ref,
    nbr_in,
    cover_in,
    source_in,
    coarse_d_in,
    coarse_nbr_in,
    place_ref,
    bottom_d_in,
    fine_u_out,
    fine_c_out,
    coarse_u_out,
    coarse_b_out,
    coarse_c_out,
    reach,
    blocks_out,
    places_out,
    fine_u,
    fine_c,
    coarse_u,
    coarse_b,
    coarse_c,
    fine_nbr,
    cover_ref,
    coarse_nbr,
    fine_b,
    fine_d,
    source_ref,
    coarse_d,
    bottom_d,
    u_first,
    fine_sum,
    coarse_sum,
    yz_fine_0,
    x_fine_0,
    yz_fine_1,
    x_fine_1,
    slab_c,
    rest_ref,
    octants,
    placed,
    lifted,
    found_at,
    cu_first,
    yz_coarse_0,
    x_coarse_0,
    yz_coarse_1,
    x_coarse_1,
    blocks,
    places,
    send_sems,
    recv_sems,
    local_sem,
    fine_sems,
    input_sems,
    output_sems,
    fine_sent,
    fine_came,
    coarse_sent,
    coarse_came,
    spread_sent,
    spread_came,
):
    here = Place(n_box, n_node)
    copies = Copies(send_sems, recv_sems)
    boxes = fine_b.shape[0]

    def fine_input(box, number):
        pair = ((fine_b_in, fine_b), (fine_d_in, fine_d))[number]
        return pltpu.make_async_copy(pair[0].at[box], pair[1].at[box], fine_sems.at[number, box])

    for box in range(boxes):
        fine_input(box, 0).start()
        fine_input(box, 1).start()
    inputs = [
        pltpu.make_async_copy(source, target, input_sems.at[number])
        for number, (source, target) in enumerate(
            (
                (bottom_d_in, bottom_d),
                (source_in, source_ref),
                (coarse_d_in, coarse_d),
                (nbr_in, fine_nbr),
                (cover_in, cover_ref),
                (coarse_nbr_in, coarse_nbr),
            )
        )
    ]
    for copy in inputs:
        copy.start()
    here.greet(
        [here.at_box(step) for step in (1, -1, 2, -2)]
        + [here.at_line(step, 1) for step in range(1, here.line)]
        + [here.at_sheet(step, 1) for step in range(1, here.sheet)]
    )

    def keep(source, target, number):
        copy = pltpu.make_async_copy(source, target, output_sems.at[number])
        copy.start()
        return copy

    def ready(box):
        fine_input(box, 0).wait()
        fine_input(box, 1).wait()

    places[0, 0] = jnp.full((1, 128), place_ref[0], I32)
    fine_swaps = [
        Swap(here, yz, x, boxes, step, fine_sent.at[number], fine_came.at[number])
        for number, (yz, x, step) in enumerate(
            ((yz_fine_0, x_fine_0, boxes), (yz_fine_1, x_fine_1, 2))
        )
    ]
    coarse_swaps = [
        Swap(here, yz, x, 1, 1, coarse_sent.at[number], coarse_came.at[number])
        for number, (yz, x) in enumerate(((yz_coarse_0, x_coarse_0), (yz_coarse_1, x_coarse_1)))
    ]
    place_spreads = write_to_all(here, places, spread_sent.at[0], spread_came.at[0])
    block_spreads = write_to_all(here, blocks, spread_sent.at[1], spread_came.at[1])

    first_sweep(boxes, u_first, fine_b, fine_d, fine_c, fine_swaps[0], ready)
    here.greeted()
    fine_swaps[0].start(0)
    kept = [keep(fine_c, fine_c_out, 0)]
    rows_x, rows_y = bottom_d.shape[0], bottom_d.shape[1]
    inputs[0].wait()
    part_z = one_hot_of((256, 256), lambda r, l: r == ((l & 127) << 1) + (l >> 7))

    def scale_plane(x, carry):
        slab_c[x] = pick_right(0.8 / (6.0 + bottom_d[x]), part_z)
        return carry

    lax.fori_loop(0, rows_x, scale_plane, 0)
    own_x, own_y = pl.ds(HALO, rows_x), pl.ds(Y_HALO, rows_y)
    own_copy = pltpu.make_async_copy(slab_c, reach.at[own_x, own_y], local_sem)
    own_copy.start()
    sides_y = (pl.ds(0, Y_HALO), pl.ds(Y_HALO + rows_y, Y_HALO))
    some = HALO - rows_x
    to_x = (
        (1, 0, rows_x, HALO - rows_x),
        (-1, 0, rows_x, HALO + rows_x),
        (2, rows_x - some, some, 0),
        (-2, 0, some, HALO + 2 * rows_x),
    )
    halo_x = [
        copies.start(
            slab_c.at[pl.ds(first, wide)],
            reach.at[pl.ds(target, wide), own_y],
            here.at_box(step),
        )
        for step, first, wide, target in to_x
    ]
    place_spreads[0].start()

    for copy in inputs[1:]:
        copy.wait()
    for target in range(8 * n_node):
        slot = jnp.int32(-1)
        for box in range(boxes):
            slot = jnp.where(cover_ref[0, box] == target, box, slot)
        found_at[target] = slot

    own_copy.wait()

    inside_boxes(boxes, u_first, fine_b, fine_sum)
    fine_swaps[0].arrived()
    sweep_boxes(
        boxes, u_first, fine_sum, fine_c, fine_swaps[0], fine_nbr, fine_u, fine_swaps[1]
    )
    kept.append(keep(fine_u, fine_u_out, 1))
    place_spreads[0].arrived()
    place_spreads[1].start()
    fold_yz = one_hot_of(
        (1024, 256), lambda r, l: (r >> 6 == l >> 4) & ((r & 31) >> 1 == (l & 15))
    )
    fold_x = one_hot_of((16 * boxes, 32 * boxes), lambda r, l: l >> 1 == r)
    inside_boxes(boxes, fine_u, fine_b, fine_sum)
    fine_swaps[1].arrived()
    live = count_ref[0, 0]
    residual_boxes(
        boxes,
        fine_u,
        fine_sum,
        fine_d,
        fine_swaps[1],
        fine_nbr,
        rest_ref,
        lambda box: jnp.where(box < live, 1.0, 0.0).astype(F32),
    )
    cubes = pick_left(fold_x, pick_right(rest_ref[...], fold_yz)) * 0.5
    for box in range(boxes):
        octants[box] = cubes[16 * box : 16 * (box + 1)]

    def place_one(target, carry):
        slot = found_at[target]
        kept = jnp.where(slot >= 0, 1.0, 0.0).astype(F32)
        placed[target] = octants[jnp.maximum(slot, 0)] * kept
        return carry

    lax.fori_loop(0, 8 * n_node, place_one, 0)
    given = []
    for step, (other, device) in enumerate(here.peers_node()):
        given.append(
            copies.start(
                placed.at[pl.ds(pl.multiple_of(other * 8, 8), 8)], lifted.at[step], device
            )
        )
    spread = one_hot_of(
        (512, 512),
        lambda r, l: (r >> 8 == (l >> 4 & 1)) & ((r >> 4 & 15) == l >> 5) & ((r & 15) == (l & 15)),
    )
    arrived(given)
    halo_y = [
        copies.start(
            slab_c.at[:, pl.ds(rows_y - Y_HALO, Y_HALO)],
            reach.at[own_x, sides_y[0]],
            here.at_node(1),
        ),
        copies.start(
            slab_c.at[:, pl.ds(0, Y_HALO)],
            reach.at[own_x, sides_y[1]],
            here.at_node(-1),
        ),
    ]
    total = placed[pl.ds(pl.multiple_of(here.node * 8, 8), 8)]
    for step in range(n_node - 1):
        total = total + lifted[step]
    pairs = jnp.concatenate(
        [jnp.concatenate([total[2 * k], total[2 * k + 1]], axis=1) for k in range(4)], axis=0
    )
    grown = pick_right(pairs, spread)
    for k in range(4):
        at_x, at_y = 16 * (k // 2), 512 * (k % 2)
        coarse_b[0, at_x : at_x + 16, at_y : at_y + 512] = (
            source_ref[0, at_x : at_x + 16, at_y : at_y + 512] + grown[16 * k : 16 * (k + 1)]
        )

    first_sweep(1, cu_first, coarse_b, coarse_d, coarse_c, coarse_swaps[0])
    kept += [keep(coarse_b, coarse_b_out, 2), keep(coarse_c, coarse_c_out, 3)]
    inside_boxes(1, cu_first, coarse_b, coarse_sum)
    coarse_swaps[0].arrived()
    sweep_boxes(
        1, cu_first, coarse_sum, coarse_c, coarse_swaps[0], coarse_nbr, coarse_u, coarse_swaps[1]
    )
    kept.append(keep(coarse_u, coarse_u_out, 4))
    fold_quarter = one_hot_of(
        (1024, 128), lambda r, l: (r >> 7 == (l >> 3 & 7)) & ((r >> 2 & 7) == ((l & 3) << 1) + (l >> 2 & 1))
    )
    inside_boxes(1, coarse_u, coarse_b, coarse_sum)
    arrived(halo_y)
    for step, first, wide, target in to_x:
        for side in sides_y:
            halo_x.append(
                copies.start(
                    reach.at[pl.ds(HALO + first, wide), side],
                    reach.at[pl.ds(target, wide), side],
                    here.at_box(step),
                )
            )
    coarse_swaps[1].arrived()
    residual_boxes(1, coarse_u, coarse_sum, coarse_d, coarse_swaps[1], coarse_nbr, rest_ref)
    folded = pick_right(rest_ref[0:32], fold_quarter)
    folded = pick_left(one_hot_of((8, 32), lambda r, l: l >> 2 == r), folded) * 0.25
    block = swap_eights(folded)
    late = pltpu.roll(block, 64, 1)
    blocks[0, 0] = jnp.where(lanes_of((4, 128)) < 64, block[0:4], late[4:8])

    block_spreads[0].start()
    place_spreads[1].arrived()
    block_spreads[0].arrived()
    block_spreads[1].start()
    row = jnp.zeros((1, 128), I32)
    lane = lanes_of((1, 128))
    for number in range(n_box * n_node):
        row = jnp.where(lane == number, places[number // here.line, number % here.line], row)
    places_out[...] = row
    block_spreads[1].arrived()
    kept.append(keep(blocks, blocks_out, 5))
    arrived(halo_x)
    copies.finish()
    for copy in kept:
        copy.wait()
    for sent in fine_swaps + coarse_swaps + [*place_spreads, *block_spreads]:
        sent.finish()


def bottom_kernel(
    n_box, n_node, rows_x, rows_y, places, reach, blocks_in, out, blocks, scale, source, first, second, hits, sems
):
    deep, wide, long = reach.shape
    count = n_box * n_node
    per_side = long // 8
    side_bits = per_side.bit_length() - 1
    box, node = lax.axis_index("box"), lax.axis_index("node")
    at_x, at_y = box * rows_x - HALO, node * rows_y - Y_HALO
    fills = [
        pltpu.make_async_copy(
            reach.at[:, :, 128 * half : 128 * (half + 1)],
            scale.at[half, pl.ds(8, deep)],
            sems.at[half],
        )
        for half in range(2)
    ]
    fills.append(pltpu.make_async_copy(blocks_in, blocks, sems.at[2]))
    for copy in fills:
        copy.start()
    zeros = jnp.zeros((wide, 128), F32)

    def clear(x, carry):
        for half in range(2):
            source[half, x] = zeros
            first[half, x] = zeros
        return carry

    lax.fori_loop(8, 8 + deep, clear, 0, unroll=2)
    out[...] = jnp.zeros(out.shape, F32)

    def where_is(number):
        place = places[0, number]
        return (
            (place >> 2 * side_bits << 3) - at_x,
            ((place >> side_bits & per_side - 1) << 3) - at_y,
            place & per_side - 1,
        )

    def look(number, found):
        x, y, _ = where_is(number)
        hits[found] = number
        hit = (x > -8) & (x < deep) & (y >= 0) & (y < wide)
        return found + hit.astype(I32)

    found = lax.fori_loop(0, count, look, jnp.int32(0), unroll=8)

    for copy in fills:
        copy.wait()

    def empty(x, carry):
        for half in range(2):
            scale[half, x] = zeros
        return carry

    lax.fori_loop(8, 8 + jnp.maximum(-at_x, 0), empty, 0)
    lax.fori_loop(8 + jnp.minimum(rows_x * n_box - at_x, deep), 8 + deep, empty, 0)

    def empty_rows(start):
        def one(x, carry):
            for half in range(2):
                scale[half, x, start : start + Y_HALO] = jnp.zeros((Y_HALO, 128), F32)
            return carry

        lax.fori_loop(8, 8 + deep, one, 0)

    pl.when(node == 0)(lambda: empty_rows(0))
    pl.when(node == n_node - 1)(lambda: empty_rows(Y_HALO + rows_y))

    lane, row = lanes_of((8, 128)), rows_of((8, 128))

    def put(at, carry):
        number = hits[at]
        x, y, z = where_is(number)
        block = blocks[number]
        kept = (lane >> 2) == z
        rows = pl.ds(pl.multiple_of(y, 8), 8)
        spots = [(half, x + ix + 8, rows) for half in range(2) for ix in range(8)]
        before = [source[spot] for spot in spots]
        first_before = [first[spot] for spot in spots]
        scales = [scale[spot] for spot in spots]
        whole = jnp.concatenate([block, pltpu.roll(block, 64, 1)], axis=0)
        fresh = []
        for half in range(2):
            for ix in range(8):
                shift = (z << 2) + 128 - 4 * half - 8 * ix & 127
                fresh.append(jnp.where(kept, pltpu.roll(whole, shift, 1), 0.0))
        for number, spot in enumerate(spots):
            source[spot] = before[number] + fresh[number]
            first[spot] = first_before[number] + fresh[number] * scales[number]
        return carry

    lax.fori_loop(0, found, put, 0)

    refs = (first, second)
    eight = (8, 128)
    lane = lanes_of(eight)
    for sweep_no in range(HALO):
        left = HALO - 1 - sweep_no
        margin = (left + 3) // 4 * 4
        low = Y_HALO - margin
        here, there = refs[sweep_no % 2], refs[(sweep_no + 1) % 2]

        def planes(group, carry):
            fresh = []
            for number in range(AT_ONCE):
                x = 8 + HALO - left + AT_ONCE * group + number
                for at in range(low, low + rows_y + 2 * margin, 8):
                    cut = slice(at, at + 8)
                    mids = [here[half, x, cut, :] for half in range(2)]
                    turned = (
                        jnp.where(lane == 0, 0.0, pltpu.roll(mids[1], 1, 1)),
                        jnp.where(lane == 127, 0.0, pltpu.roll(mids[0], 127, 1)),
                    )
                    for half in range(2):
                        around = here[half, x - 1, cut, :] + here[half, x + 1, cut, :]
                        around += here[half, x, at - 1 : at + 7, :]
                        around += here[half, x, at + 1 : at + 9, :]
                        around += mids[1 - half] + turned[half]
                        value = 0.2 * mids[half] + scale[half, x, cut, :] * (
                            source[half, x, cut, :] + around
                        )
                        fresh.append((half, x, cut, value))
            for half, x, cut, value in fresh:
                there[half, x, cut, :] = value
            return carry

        lax.fori_loop(0, (rows_x + 2 * left + AT_ONCE - 1) // AT_ONCE, planes, 0)
    solved = refs[HALO % 2]

    def take(at, carry):
        number = hits[at]
        x, y, z = where_is(number)

        @pl.when((x == HALO) & (y >= Y_HALO) & (y < Y_HALO + rows_y))
        def _():
            rows = pl.ds(pl.multiple_of(y, 8), 8)
            back = 128 - (z << 2)
            gathered = jnp.zeros(eight, F32)
            for ix in range(8):
                for half in range(2):
                    turned = pltpu.roll(
                        solved[half, 8 + HALO + ix, rows, :], back + 4 * half + 8 * ix & 127, 1
                    )
                    gathered = jnp.where((lane >> 2) == 2 * ix + half, turned, gathered)
            late = pltpu.roll(gathered, 64, 1)
            out[number] = jnp.where(lanes_of((4, 128)) < 64, gathered[0:4], late[4:8])

        return carry

    lax.fori_loop(0, found, take, 0)


def up_kernel(
    n_box,
    n_node,
    parts_in,
    fine_u_in,
    fine_c_in,
    fine_b_in,
    count_ref,
    nbr_in,
    cover_in,
    coarse_u_in,
    coarse_b_in,
    coarse_c_in,
    coarse_nbr_in,
    fine_to,
    coarse_to,
    fine_out,
    coarse_out,
    output_sems,
    fine_u,
    fine_c,
    fine_b,
    fine_nbr,
    cover_ref,
    coarse_u,
    coarse_b,
    coarse_c,
    coarse_nbr,
    own_parts,
    input_sems,
    from_core,
    sum_core,
    from_chips,
    own_block,
    cu_first,
    cu_second,
    yz_coarse_0,
    x_coarse_0,
    yz_coarse_1,
    x_coarse_1,
    octants,
    picked,
    u_first,
    u_second,
    fine_sum,
    coarse_sum,
    yz_fine_0,
    x_fine_0,
    yz_fine_1,
    x_fine_1,
    send_sems,
    recv_sems,
    fine_sent,
    fine_came,
    coarse_sent,
    coarse_came,
    spread_sent,
    spread_came,
):
    here = Place(n_box, n_node)
    copies = Copies(send_sems, recv_sems)
    boxes = fine_u.shape[0]
    inputs = [
        pltpu.make_async_copy(source, target, input_sems.at[number])
        for number, (source, target) in enumerate(
            (
                (parts_in.at[:, pl.ds(0, n_node)], own_parts),
                (coarse_u_in, coarse_u),
                (coarse_b_in, coarse_b),
                (coarse_c_in, coarse_c),
                (coarse_nbr_in, coarse_nbr),
                (nbr_in, fine_nbr),
                (cover_in, cover_ref),
                (fine_u_in, fine_u),
                (fine_c_in, fine_c),
                (fine_b_in, fine_b),
            )
        )
    ]
    for copy in inputs:
        copy.start()
    fine_swaps = [
        Swap(here, yz, x, boxes, 2, fine_sent.at[number], fine_came.at[number])
        for number, (yz, x) in enumerate(((yz_fine_0, x_fine_0), (yz_fine_1, x_fine_1)))
    ]
    coarse_swaps = [
        Swap(here, yz, x, 1, 1, coarse_sent.at[number], coarse_came.at[number])
        for number, (yz, x) in enumerate(((yz_coarse_0, x_coarse_0), (yz_coarse_1, x_coarse_1)))
    ]
    here.greet([here.mate()], True)
    here.greeted()

    from_mate = copies.start(parts_in.at[:, pl.ds(n_node, n_node)], from_core, here.mate())
    for copy in inputs:
        copy.wait()
    arrived([from_mate])
    sum_core[...] = own_parts[...] + from_core[...]
    x_bits = n_node.bit_length() - 1
    spread = Spread(
        here.chips,
        lambda step: sum_core.at[step >> x_bits, step & n_node - 1],
        lambda step: from_chips.at[step],
        from_chips.at[pl.ds(1, here.chips - 1)],
        here.before_chip,
        spread_sent,
        spread_came,
    )
    from_chips[0] = sum_core[0, 0]
    spread.start()
    grow_quarter = one_hot_of(
        (128, 1024), lambda r, l: r == (l >> 7 << 3) + (l >> 3 & 3) + (l >> 2 & 1) * 4
    )
    spread.arrived()
    block = jnp.sum(from_chips[...], axis=0)
    own_block[0:4] = block
    own_block[4:8] = pltpu.roll(block, 64, 1)
    grown = pick_right(swap_eights(own_block[...]), grow_quarter)
    grown = pick_left(one_hot_of((32, 8), lambda r, l: r >> 2 == l), grown)
    cu_first[0] = coarse_u[0] + grown
    put_faces(tiles_of(cu_first, 0), yz_coarse_0, x_coarse_0, 1)
    coarse_swaps[0].start(0)
    inside_boxes(1, cu_first, coarse_b, coarse_sum)
    coarse_swaps[0].arrived()
    sweep_boxes(
        1, cu_first, coarse_sum, coarse_c, coarse_swaps[0], coarse_nbr, cu_second, coarse_swaps[1]
    )
    split = one_hot_of(
        (512, 512),
        lambda r, l: (l >> 8 == (r >> 4 & 1)) & ((l >> 4 & 15) == r >> 5) & ((l & 15) == (r & 15)),
    )
    inside_boxes(1, cu_second, coarse_b, coarse_sum)
    coarse_swaps[1].arrived()
    sweep_boxes(
        1, cu_second, coarse_sum, coarse_c, coarse_swaps[1], coarse_nbr, coarse_out, None
    )
    coarse_store = Store(coarse_out, coarse_to, 1, 1, output_sems.at[pl.ds(boxes // 2, 1)])
    coarse_store.start(0)

    quarters = jnp.concatenate(
        [
            coarse_out[0, 16 * (k // 2) : 16 * (k // 2) + 16, 512 * (k % 2) : 512 * (k % 2) + 512]
            for k in range(4)
        ],
        axis=0,
    )
    cubes = pick_right(quarters, split)
    base = pl.multiple_of(here.node * 8, 8)
    for k in range(8):
        octants[base + k] = cubes[16 * (k // 2) : 16 * (k // 2) + 16, 256 * (k % 2) : 256 * (k % 2) + 256]
    own = octants.at[pl.ds(base, 8)]
    waits = [copies.start(own, own, device) for _, device in here.peers_node()]
    grow_yz = one_hot_of(
        (256, 1024), lambda r, l: (l >> 6 == r >> 4) & ((l >> 1 & 15) == (r & 15))
    )
    grow_x = one_hot_of((32 * boxes, 16 * boxes), lambda r, l: r >> 1 == l)
    arrived(waits)
    for box in range(boxes):
        picked[16 * box : 16 * (box + 1)] = octants[cover_ref[0, box]]
    tall = pick_right(pick_left(grow_x, picked[...]), grow_yz)
    for box in range(boxes):
        u_first[box] = fine_u[box] + tall[32 * box : 32 * (box + 1)]

    def faces_of(box, carry):
        put_faces(tiles_of(u_first, box), yz_fine_0, x_fine_0, boxes + box)

    by_chunks(boxes, fine_swaps[0], faces_of)
    inside_boxes(boxes, u_first, fine_b, fine_sum)
    fine_swaps[0].arrived()
    sweep_boxes(
        boxes, u_first, fine_sum, fine_c, fine_swaps[0], fine_nbr, u_second, fine_swaps[1]
    )
    inside_boxes(boxes, u_second, fine_b, fine_sum)
    fine_swaps[1].arrived()
    live = count_ref[0, 0]
    fine_store = Store(fine_out, fine_to, boxes, 2, output_sems)
    sweep_boxes(
        boxes,
        u_second,
        fine_sum,
        fine_c,
        fine_swaps[1],
        fine_nbr,
        fine_out,
        None,
        lambda box: jnp.where(box < live, 1.0, 0.0).astype(F32),
        fine_store,
    )
    copies.finish()
    for sent in fine_swaps + coarse_swaps + [spread, fine_store, coarse_store]:
        sent.finish()


def hand_on_kernel(fine_from, coarse_from, fine_to, coarse_to, fine_held, coarse_held, came, sent):
    boxes = fine_from.shape[0]
    paths = [
        (fine_from.at[box], fine_held.at[box], fine_to.at[box], came.at[box], sent.at[box])
        for box in range(boxes)
    ]
    paths.append((coarse_from, coarse_held, coarse_to, came.at[boxes], sent.at[boxes]))
    ins = [pltpu.make_async_copy(a, b, sem) for a, b, _, sem, _ in paths]
    outs = [pltpu.make_async_copy(b, c, sem) for _, b, c, _, sem in paths]
    for copy in ins:
        copy.start()
    for coming, going in zip(ins, outs):
        coming.wait()
        going.start()
    for copy in outs:
        copy.wait()


VMEM, SMEM, ANY = (
    pl.BlockSpec(memory_space=pltpu.VMEM),
    pl.BlockSpec(memory_space=pltpu.SMEM),
    pl.BlockSpec(memory_space=pl.ANY),
)


def shards(
    n_box,
    n_node,
    fine_rhs,
    fine_diag,
    fine_count,
    fine_nbr,
    fine_cover,
    coarse_source,
    coarse_diag,
    coarse_nbr,
    coarse_place,
    bottom_diag,
):
    boxes = fine_rhs.shape[0]
    ny, nz, nc = grid_of(n_box)
    rows_x, rows_y, long = bottom_diag.shape
    deep, wide = rows_x + 2 * HALO, rows_y + 2 * Y_HALO
    count = n_box * n_node

    def like(shape, kind=F32):
        return jax.ShapeDtypeStruct(shape, kind)

    fine, coarse = (boxes, 32, 1024), (1, 32, 1024)
    line = nc * n_node
    grid = (ny * nz, line)
    limit = 62 * 1024 * 1024
    fine_u, fine_c, coarse_u, coarse_b, coarse_c, reach, blocks, places = pl.pallas_call(
        functools.partial(down_kernel, n_box, n_node),
        out_shape=(
            like(fine),
            like(fine),
            like(coarse),
            like(coarse),
            like(coarse),
            like((deep, wide, long)),
            like(grid + (4, 128)),
            like((1, 128), I32),
        ),
        in_specs=[ANY, ANY, SMEM, ANY, ANY, ANY, ANY, ANY, SMEM, ANY],
        out_specs=(ANY, ANY, ANY, ANY, ANY, ANY, ANY, VMEM),
        scratch_shapes=[
            pltpu.VMEM(fine, F32),
            pltpu.VMEM(fine, F32),
            pltpu.VMEM(coarse, F32),
            pltpu.VMEM(coarse, F32),
            pltpu.VMEM(coarse, F32),
            pltpu.SMEM((boxes, 6), I32),
            pltpu.SMEM((1, boxes), I32),
            pltpu.SMEM((1, 6), I32),
            pltpu.VMEM(fine, F32),
            pltpu.VMEM(fine, F32),
            pltpu.VMEM(coarse, F32),
            pltpu.VMEM(coarse, F32),
            pltpu.VMEM((rows_x, rows_y, long), F32),
            pltpu.VMEM(fine, F32),
            pltpu.VMEM(fine, F32),
            pltpu.VMEM(coarse, F32),
            pltpu.VMEM((3 * boxes, 32, 128), F32),
            pltpu.VMEM((3 * boxes, 2, 1024), F32),
            pltpu.VMEM((3 * boxes, 32, 128), F32),
            pltpu.VMEM((3 * boxes, 2, 1024), F32),
            pltpu.VMEM((rows_x, rows_y, long), F32),
            pltpu.VMEM((32 * boxes, 1024), F32),
            pltpu.VMEM((boxes, 16, 256), F32),
            pltpu.VMEM((8 * n_node, 16, 256), F32),
            pltpu.VMEM((n_node - 1, 8, 16, 256), F32),
            pltpu.SMEM((8 * n_node,), I32),
            pltpu.VMEM(coarse, F32),
            pltpu.VMEM((3, 32, 128), F32),
            pltpu.VMEM((3, 2, 1024), F32),
            pltpu.VMEM((3, 32, 128), F32),
            pltpu.VMEM((3, 2, 1024), F32),
            pltpu.VMEM(grid + (4, 128), F32),
            pltpu.VMEM(grid + (1, 128), I32),
            pltpu.SemaphoreType.DMA((64,)),
            pltpu.SemaphoreType.DMA((64,)),
            pltpu.SemaphoreType.DMA,
            pltpu.SemaphoreType.DMA((2, boxes)),
            pltpu.SemaphoreType.DMA((6,)),
            pltpu.SemaphoreType.DMA((6,)),
            pltpu.SemaphoreType.DMA((2, boxes // 2, 4)),
            pltpu.SemaphoreType.DMA((2, boxes // 2, 4)),
            pltpu.SemaphoreType.DMA((2, 1, 4)),
            pltpu.SemaphoreType.DMA((2, 1, 4)),
            pltpu.SemaphoreType.DMA((2, 2)),
            pltpu.SemaphoreType.DMA((2, 2)),
        ],
        compiler_params=pltpu.CompilerParams(
            collective_id=0, has_side_effects=True, vmem_limit_bytes=limit
        ),
        name="down",
    )(
        fine_rhs,
        fine_diag,
        fine_count,
        fine_nbr,
        fine_cover,
        coarse_source,
        coarse_diag,
        coarse_nbr,
        coarse_place,
        bottom_diag,
    )
    parts = pl.pallas_call(
        functools.partial(bottom_kernel, n_box, n_node, rows_x, rows_y),
        out_shape=like((count, 4, 128)),
        in_specs=[SMEM, ANY, ANY],
        out_specs=VMEM,
        scratch_shapes=[
            pltpu.VMEM((count, 4, 128), F32),
            pltpu.VMEM((2, deep + 16, wide, 128), F32),
            pltpu.VMEM((2, deep + 16, wide, 128), F32),
            pltpu.VMEM((2, deep + 16, wide, 128), F32),
            pltpu.VMEM((2, deep + 16, wide, 128), F32),
            pltpu.SMEM((count + 1,), I32),
            pltpu.SemaphoreType.DMA((3,)),
        ],
        compiler_params=pltpu.CompilerParams(vmem_limit_bytes=limit),
        name="bottom",
    )(places, reach, blocks.reshape(count, 4, 128))
    fine_out, coarse_out = pl.pallas_call(
        functools.partial(up_kernel, n_box, n_node),
        out_shape=(like(fine), like(coarse)),
        in_specs=[ANY, ANY, ANY, ANY, SMEM, ANY, ANY, ANY, ANY, ANY, ANY],
        out_specs=(ANY, ANY),
        scratch_shapes=[
            pltpu.VMEM(fine, F32),
            pltpu.VMEM(coarse, F32),
            pltpu.SemaphoreType.DMA((boxes // 2 + 1,)),
            pltpu.VMEM(fine, F32),
            pltpu.VMEM(fine, F32),
            pltpu.VMEM(fine, F32),
            pltpu.SMEM((boxes, 6), I32),
            pltpu.SMEM((1, boxes), I32),
            pltpu.VMEM(coarse, F32),
            pltpu.VMEM(coarse, F32),
            pltpu.VMEM(coarse, F32),
            pltpu.SMEM((1, 6), I32),
            pltpu.VMEM((ny * nz, n_node, 4, 128), F32),
            pltpu.SemaphoreType.DMA((10,)),
            pltpu.VMEM((ny * nz, n_node, 4, 128), F32),
            pltpu.VMEM((ny * nz, n_node, 4, 128), F32),
            pltpu.VMEM((ny * nz * n_node, 4, 128), F32),
            pltpu.VMEM((8, 128), F32),
            pltpu.VMEM(coarse, F32),
            pltpu.VMEM(coarse, F32),
            pltpu.VMEM((3, 32, 128), F32),
            pltpu.VMEM((3, 2, 1024), F32),
            pltpu.VMEM((3, 32, 128), F32),
            pltpu.VMEM((3, 2, 1024), F32),
            pltpu.VMEM((8 * n_node, 16, 256), F32),
            pltpu.VMEM((16 * boxes, 256), F32),
            pltpu.VMEM(fine, F32),
            pltpu.VMEM(fine, F32),
            pltpu.VMEM(fine, F32),
            pltpu.VMEM(coarse, F32),
            pltpu.VMEM((3 * boxes, 32, 128), F32),
            pltpu.VMEM((3 * boxes, 2, 1024), F32),
            pltpu.VMEM((3 * boxes, 32, 128), F32),
            pltpu.VMEM((3 * boxes, 2, 1024), F32),
            pltpu.SemaphoreType.DMA((8,)),
            pltpu.SemaphoreType.DMA((8,)),
            pltpu.SemaphoreType.DMA((2, boxes // 2, 4)),
            pltpu.SemaphoreType.DMA((2, boxes // 2, 4)),
            pltpu.SemaphoreType.DMA((2, 1, 4)),
            pltpu.SemaphoreType.DMA((2, 1, 4)),
            pltpu.SemaphoreType.DMA,
            pltpu.SemaphoreType.DMA,
        ],
        compiler_params=pltpu.CompilerParams(
            collective_id=1, has_side_effects=True, vmem_limit_bytes=limit
        ),
        name="up",
    )(
        parts.reshape(grid + (4, 128)),
        fine_u,
        fine_c,
        fine_rhs,
        fine_count,
        fine_nbr,
        fine_cover,
        coarse_u,
        coarse_b,
        coarse_c,
        coarse_nbr,
    )
    return pl.pallas_call(
        hand_on_kernel,
        out_shape=(like(fine), like(coarse)),
        in_specs=[ANY, ANY],
        out_specs=(ANY, ANY),
        scratch_shapes=[
            pltpu.VMEM(fine, F32),
            pltpu.VMEM(coarse, F32),
            pltpu.SemaphoreType.DMA((boxes + 1,)),
            pltpu.SemaphoreType.DMA((boxes + 1,)),
        ],
        compiler_params=pltpu.CompilerParams(vmem_limit_bytes=limit),
        name="hand_on",
    )(fine_out, coarse_out)


def solution(mesh):
    n_box, n_node = mesh.shape["box"], mesh.shape["node"]
    return jax.shard_map(
        functools.partial(shards, n_box, n_node),
        mesh=mesh,
        in_specs=(
            P(("box", "node"), None, None),
            P(("box", "node"), None, None),
            P("box", "node"),
            P(("box", "node"), None),
            P("box", "node"),
            P(("box", "node"), None, None),
            P(("box", "node"), None, None),
            P(("box", "node"), None),
            P(("box", "node")),
            P("box", "node", None),
        ),
        out_specs=(P(("box", "node"), None, None), P(("box", "node"), None, None)),
        check_vma=False,
    )
```
